32 devices in a mesh: batch: 2 (over y), gx: 4 (over z), gy: 4 (over x, core).
Axes of the slice: x: 2, y: 2, z: 4, core: 2. Of those that a mesh axis runs over, the one named last changes fastest.
Arguments:
- tokens: bfloat16 [64, 2, 18432], P(None, None, ('batch', 'gy')), may hold values from -6 to 6
- w_query: bfloat16 [18432, 12288], P(('batch', 'gy'), 'gx'), may hold values from -0.046875 to 0.046875
- w_keyval: bfloat16 [18432, 512], P(('batch', 'gy'), 'gx'), may hold values from -0.09375 to 0.09375
- w_out: bfloat16 [12288, 18432], P('gx', ('batch', 'gy')), may hold values from -0.19921875 to 0.19921875
- cache_keys: bfloat16 [64, 2048, 256], P(('batch', 'gx', 'gy')), may hold values from -140 to 140
- cache_values: bfloat16 [64, 2048, 256], P(('batch', 'gx', 'gy')), may hold values from -6 to 6
- lengths: int32 [64], P(('batch', 'gx', 'gy')), may hold values from 512 to 2048, as said below
Outputs:
- mixed: bfloat16 [64, 2, 18432], P('gx', None, ('batch', 'gy'))
The draws below stay inside these ranges and needn't reach their ends.
Inputs may be any that keep to these rules, and one draw needn't show every extreme that they name: `lengths`: every draw has a sequence with 2048 valid positions and one with 512.
All inputs are finite; a program needn't handle non-finite values.
Results may differ from the reference program's by a relative error of at most 0.02.
Values may be sent and summed in bfloat16 or wider, within the bound.
No kernel may reach another device: no remote copies, remote signals or barrier semaphores. Data moves between devices by JAX's collectives and lax.ppermute only.
A program may use at most 128 MiB of HBM per device.

```python
import jax
import jax.numpy as jnp
from jax import lax

D = 18432
HQ = 48
HD = 256
S = 2048
STEPS = 2
B = 64
N_BATCH = 2
N_GY = 4


def draw_cache_keys(key, part):
    key = jax.random.fold_in(key, 11)
    first_key = jax.random.fold_in(key, 0)
    base = 2.0 * jax.random.normal(first_key, (B, S, HD), jnp.float32)
    return jnp.clip(base, -12.0, 12.0).astype(jnp.bfloat16)


def draw_lengths(key, part):
    key = jax.random.fold_in(key, 23)
    first_key, second_key = jax.random.split(key, 2)
    values = jax.random.randint(first_key, (B,), S // 4, S + 1)
    order = jax.random.permutation(second_key, B)
    values = values.at[order[0]].set(S).at[order[1]].set(S // 4)
    return values.astype(jnp.int32)


def spiked(entries, key, source, target, shards_of, factor):
    owner, partner = [(jnp.arange(entries.shape[axis_at]) // (entries.shape[axis_at] // shards_of)).reshape([-1 if axis == axis_at else 1 for axis in range(entries.ndim)]) for axis_at in (source, target)]
    chosen = jax.random.permutation(key, shards_of)[partner]
    strong = (owner == chosen) | (owner == (partner + shards_of // 2) % shards_of)
    return jnp.where(strong, factor * entries, entries)


def level_of(key, shape, cuts, low, high):
    factor_of, own = 1.0, jax.random.fold_in(key, 6)
    for position, blocks in cuts:
        draws = jnp.exp(jax.random.uniform(jax.random.fold_in(own, position), (blocks,), jnp.float32, low / len(cuts), high / len(cuts)))
        factor_of = factor_of * jnp.repeat(draws, shape[position] // blocks).reshape([-1 if axis == position else 1 for axis in range(len(shape))])
    return factor_of


def normal_values(key, dims, scale, limit, cuts=(), kind=jnp.bfloat16):
    gain = level_of(key, dims, cuts, -0.22, 0.18) if cuts else 1.0
    drawn = jax.random.normal(key, dims, jnp.float32) * scale * gain
    return jnp.minimum(jnp.maximum(drawn, -limit), limit).astype(kind)


def noise_with(key, shape, spread, limit, cuts, heavy, kind=jnp.bfloat16):
    values = spread * jax.random.normal(key, shape, jnp.float32)
    if cuts:
        values = values * level_of(key, shape, cuts, -0.22, 0.18)
    return jnp.clip(spiked(values, jax.random.fold_in(key, 3), *heavy), -limit, limit).astype(kind)


def setup_inputs(seed: int = 0) -> dict:
    seeds = jax.random.split(jax.random.key(seed), 8)
    tokens = noise_with(seeds[0], (B, STEPS, D), 1.0, 6.0, ((2, 8),), (2, 0, 8, 2.0))
    w_query = normal_values(seeds[1], (D, HQ * HD), D ** -0.5, 0.046875, ((0, 8), (1, 4)))
    w_keyval = normal_values(seeds[2], (D, 2 * HD), (D // 4) ** -0.5, 0.09375, ((0, 8), (1, 4)))
    w_out = normal_values(seeds[3], (HQ * HD, D), 0.03, 0.19921875, ((0, 4), (1, 8)))
    cache_keys = draw_cache_keys(jax.random.fold_in(seeds[7], 71), 0)
    cache_values = normal_values(seeds[5], (B, S, HD), 1.0, 6.0, ((0, 32),))
    lengths = draw_lengths(jax.random.fold_in(seeds[7], 71), 0)
    return dict(tokens=tokens, w_query=w_query, w_keyval=w_keyval, w_out=w_out, cache_keys=cache_keys, cache_values=cache_values, lengths=lengths)


def rotate(values, positions):
    half_width = values.shape[-1] // 2
    freqs = 10000.0 ** (-(jnp.arange(half_width, dtype=jnp.float32) * 2.0 / values.shape[-1]))
    angles = positions[..., None] * freqs
    cosine = jnp.cos(angles)
    sine = jnp.sin(angles)
    first_half = values[..., :half_width]
    second_half = values[..., half_width:]
    return jnp.concatenate([first_half * cosine - second_half * sine, second_half * cosine + first_half * sine], axis=-1)


def attend(queries, keys_cache, values_cache, new_keys, new_values, length_now):
    scaling = 1.0 / (queries.shape[-1] ** 0.5)
    cached = jnp.einsum('thd,sd->ths', queries.astype(jnp.float32), keys_cache.astype(jnp.float32)) * scaling
    valid = jnp.arange(keys_cache.shape[0], dtype=jnp.int32) < length_now
    cached = jnp.where(valid[None, None, :], cached, -1e30)
    fresh = jnp.einsum('thd,ud->thu', queries.astype(jnp.float32), new_keys.astype(jnp.float32)) * scaling
    steps_here = queries.shape[0]
    causal = jnp.arange(steps_here)[None, :] <= jnp.arange(steps_here)[:, None]
    fresh = jnp.where(causal[:, None, :], fresh, -1e30)
    highest = jnp.maximum(cached.max(-1, keepdims=True), fresh.max(-1, keepdims=True))
    exp_cached = jnp.exp(cached - highest)
    exp_fresh = jnp.exp(fresh - highest)
    denom = exp_cached.sum(-1, keepdims=True) + exp_fresh.sum(-1, keepdims=True)
    probs_cached = (exp_cached / denom).astype(jnp.bfloat16)
    probs_fresh = (exp_fresh / denom).astype(jnp.bfloat16)
    result = jnp.einsum('ths,sd->thd', probs_cached.astype(jnp.float32), values_cache.astype(jnp.float32))
    result = result + jnp.einsum('thu,ud->thd', probs_fresh.astype(jnp.float32), new_values.astype(jnp.float32))
    return result.reshape(steps_here, -1).astype(jnp.bfloat16)


def reference(tokens, w_query, w_keyval, w_out, cache_keys, cache_values, lengths):
    joined = jnp.concatenate([w_query, w_keyval], axis=1)
    flat = tokens.reshape(B * STEPS, D)
    block_total = N_BATCH * N_GY
    block_width = D // block_total

    def accumulate(carry, index):
        rows_in = lax.dynamic_slice_in_dim(flat, index * block_width, block_width, 1)
        weights_in = lax.dynamic_slice_in_dim(joined, index * block_width, block_width, 0)
        return carry + jnp.dot(rows_in, weights_in, preferred_element_type=jnp.float32), None

    summed, unused = lax.scan(accumulate, jnp.zeros((B * STEPS, joined.shape[1]), jnp.float32),
                              jnp.arange(block_total, dtype=jnp.int32))
    projected = summed.astype(jnp.bfloat16)
    queries = projected[:, :HQ * HD].reshape(B, STEPS, HQ, HD)
    new_keys = projected[:, HQ * HD:HQ * HD + HD].reshape(B, STEPS, HD)
    new_values = projected[:, HQ * HD + HD:].reshape(B, STEPS, HD)
    positions = (lengths[:, None] + jnp.arange(STEPS, dtype=jnp.int32)[None, :]).astype(jnp.float32)
    rot_queries = rotate(queries.astype(jnp.float32), positions[:, :, None]).astype(jnp.bfloat16)
    rot_keys = rotate(new_keys.astype(jnp.float32), positions).astype(jnp.bfloat16)
    attended = lax.map(lambda items: attend(*items),
                       (rot_queries, cache_keys, cache_values, rot_keys, new_values, lengths))
    mixed = jnp.dot(attended.reshape(B * STEPS, HQ * HD), w_out, preferred_element_type=jnp.float32)
    return mixed.astype(jnp.bfloat16).reshape(B, STEPS, D)
```

```python
import jax
import jax.numpy as jnp
from jax import lax
from jax.sharding import PartitionSpec as P

PLANE = ("batch", "gy")


def rotate(values, positions):
    half_width = values.shape[-1] // 2
    freqs = 10000.0 ** (-(jnp.arange(half_width, dtype=jnp.float32) * 2.0 / values.shape[-1]))
    angles = positions[..., None] * freqs
    cosine = jnp.cos(angles)
    sine = jnp.sin(angles)
    first_half = values[..., :half_width]
    second_half = values[..., half_width:]
    return jnp.concatenate(
        [first_half * cosine - second_half * sine, second_half * cosine + first_half * sine],
        axis=-1,
    )


def attend(queries, keys_cache, values_cache, new_keys, new_values, length_now):
    scaling = 1.0 / queries.shape[-1] ** 0.5
    cached = (
        jnp.einsum("thd,sd->ths", queries, keys_cache, preferred_element_type=jnp.float32) * scaling
    )
    valid = jnp.arange(keys_cache.shape[0], dtype=jnp.int32) < length_now
    cached = jnp.where(valid[None, None, :], cached, -1e30)
    fresh = (
        jnp.einsum("thd,ud->thu", queries, new_keys, preferred_element_type=jnp.float32) * scaling
    )
    steps_here = queries.shape[0]
    causal = jnp.arange(steps_here)[None, :] <= jnp.arange(steps_here)[:, None]
    fresh = jnp.where(causal[:, None, :], fresh, -1e30)
    highest = jnp.maximum(cached.max(-1, keepdims=True), fresh.max(-1, keepdims=True))
    exp_cached = jnp.exp(cached - highest)
    exp_fresh = jnp.exp(fresh - highest)
    denom = exp_cached.sum(-1, keepdims=True) + exp_fresh.sum(-1, keepdims=True)
    probs_cached = (exp_cached / denom).astype(jnp.bfloat16)
    probs_fresh = (exp_fresh / denom).astype(jnp.bfloat16)
    result = jnp.einsum(
        "ths,sd->thd", probs_cached, values_cache, preferred_element_type=jnp.float32
    )
    result = result + jnp.einsum(
        "thu,ud->thd", probs_fresh, new_values, preferred_element_type=jnp.float32
    )
    return result.astype(jnp.bfloat16)


def local(tokens, w_query, w_keyval, w_out, cache_keys, cache_values, lengths):
    batch_count = lax.axis_size("batch")
    gx_count = lax.axis_size("gx")
    gy_count = lax.axis_size("gy")
    plane_count = batch_count * gy_count
    owned = cache_keys.shape[0]
    head_width = cache_keys.shape[2]
    sequences, steps, width = tokens.shape
    query_cols = w_query.shape[1]
    pair_cols = w_keyval.shape[1]
    heads_here = query_cols // head_width
    rows_here = gx_count * owned * steps

    arranged = tokens.reshape(batch_count, gx_count, gy_count, owned * steps, width)
    arranged = arranged.transpose(0, 2, 1, 3, 4).reshape(sequences * steps, width)
    joined = jnp.concatenate([w_query, w_keyval], axis=1)
    partial = jnp.dot(arranged, joined, preferred_element_type=jnp.float32).astype(jnp.bfloat16)
    partial = partial.reshape(plane_count, rows_here, query_cols + pair_cols)
    terms = lax.all_to_all(partial, PLANE, split_axis=0, concat_axis=0, tiled=True)
    summed = terms.astype(jnp.float32).sum(0).astype(jnp.bfloat16)
    summed = summed.reshape(gx_count, owned * steps, query_cols + pair_cols)
    mine = lax.all_to_all(summed, "gx", split_axis=0, concat_axis=0, tiled=True)

    queries = mine[..., :query_cols].reshape(gx_count, owned, steps, heads_here, head_width)
    queries = queries.transpose(1, 2, 0, 3, 4).reshape(owned, steps, gx_count * heads_here, head_width)
    key_value = mine[..., query_cols:].transpose(1, 0, 2).reshape(owned, steps, gx_count * pair_cols)
    new_keys = key_value[..., :head_width]
    new_values = key_value[..., head_width:]
    positions = (lengths[:, None] + jnp.arange(steps, dtype=jnp.int32)[None, :]).astype(jnp.float32)
    rot_queries = rotate(queries.astype(jnp.float32), positions[:, :, None]).astype(jnp.bfloat16)
    rot_keys = rotate(new_keys.astype(jnp.float32), positions).astype(jnp.bfloat16)
    attended = jax.vmap(attend)(
        rot_queries, cache_keys, cache_values, rot_keys, new_values, lengths
    )

    by_group = attended.reshape(owned * steps, gx_count, query_cols).transpose(1, 0, 2)
    grouped = lax.all_to_all(by_group, "gx", split_axis=0, concat_axis=0, tiled=True)
    grouped = grouped.reshape(rows_here, query_cols)
    everyone = lax.all_gather(grouped, PLANE, axis=0, tiled=True)
    outs = jnp.dot(everyone, w_out, preferred_element_type=jnp.float32).astype(jnp.bfloat16)
    out_cols = w_out.shape[1]
    outs = outs.reshape(batch_count, gy_count, gx_count, owned * steps, out_cols)
    outs = outs.transpose(0, 2, 1, 3, 4).reshape(gx_count, sequences * steps // gx_count, out_cols)
    pieces = lax.all_to_all(outs, "gx", split_axis=0, concat_axis=0, tiled=True)
    mixed = pieces.astype(jnp.float32).sum(0).astype(jnp.bfloat16)
    return mixed.reshape(sequences // gx_count, steps, out_cols)


def solution(mesh):
    placed = (
        P(None, None, ("batch", "gy")),
        P(("batch", "gy"), "gx"),
        P(("batch", "gy"), "gx"),
        P("gx", ("batch", "gy")),
        P(("batch", "gx", "gy"), None, None),
        P(("batch", "gx", "gy"), None, None),
        P(("batch", "gx", "gy")),
    )
    return jax.shard_map(
        local, mesh=mesh, in_specs=placed, out_specs=P("gx", None, ("batch", "gy")), check_vma=False
    )
```

```python
import jax
import jax.numpy as jnp
import numpy as np
from jax import lax
from jax.sharding import PartitionSpec as P

PLANE = ("batch", "gy")


def turned(blocks, shift, axis):
    count = blocks.shape[axis]
    if count == 1:
        return blocks
    doubled = jnp.concatenate([blocks, blocks], axis=axis)
    return lax.dynamic_slice_in_dim(doubled, shift, count, axis)


def moved(value, axes, sizes, offset):
    pairs = []
    for place in np.ndindex(*sizes):
        target = tuple((p + o) % n for p, o, n in zip(place, offset, sizes))
        pairs.append((int(np.ravel_multi_index(place, sizes)), int(np.ravel_multi_index(target, sizes))))
    return lax.ppermute(value, axes, pairs)


def pair_swap(value, plane_sizes):
    pairs = []
    for place in np.ndindex(*plane_sizes):
        target = (place[0], place[1] ^ 1)
        pairs.append((int(np.ravel_multi_index(place, plane_sizes)), int(np.ravel_multi_index(target, plane_sizes))))
    return lax.ppermute(value, ("batch", "gy"), pairs)


def rotate(values, positions):
    half_width = values.shape[-1] // 2
    freqs = 10000.0 ** (-(jnp.arange(half_width, dtype=jnp.float32) * 2.0 / values.shape[-1]))
    angles = positions[..., None] * freqs
    cosine = jnp.cos(angles)
    sine = jnp.sin(angles)
    first_half = values[..., :half_width]
    second_half = values[..., half_width:]
    return jnp.concatenate(
        [first_half * cosine - second_half * sine, second_half * cosine + first_half * sine],
        axis=-1,
    )


def attend(queries, keys_cache, values_cache, new_keys, new_values, length_now):
    scaling = 1.0 / queries.shape[-1] ** 0.5
    cached = (
        jnp.einsum("thd,sd->ths", queries, keys_cache, preferred_element_type=jnp.float32) * scaling
    )
    valid = jnp.arange(keys_cache.shape[0], dtype=jnp.int32) < length_now
    cached = jnp.where(valid[None, None, :], cached, -1e30)
    fresh = (
        jnp.einsum("thd,ud->thu", queries, new_keys, preferred_element_type=jnp.float32) * scaling
    )
    steps_here = queries.shape[0]
    causal = jnp.arange(steps_here)[None, :] <= jnp.arange(steps_here)[:, None]
    fresh = jnp.where(causal[:, None, :], fresh, -1e30)
    highest = jnp.maximum(cached.max(-1, keepdims=True), fresh.max(-1, keepdims=True))
    exp_cached = jnp.exp(cached - highest)
    exp_fresh = jnp.exp(fresh - highest)
    denom = exp_cached.sum(-1, keepdims=True) + exp_fresh.sum(-1, keepdims=True)
    probs_cached = (exp_cached / denom).astype(jnp.bfloat16)
    probs_fresh = (exp_fresh / denom).astype(jnp.bfloat16)
    result = jnp.einsum(
        "ths,sd->thd", probs_cached, values_cache, preferred_element_type=jnp.float32
    )
    result = result + jnp.einsum(
        "thu,ud->thd", probs_fresh, new_values, preferred_element_type=jnp.float32
    )
    return result.astype(jnp.bfloat16)


def local(tokens, w_query, w_keyval, w_out, cache_keys, cache_values, lengths):
    batch_count = lax.axis_size("batch")
    gx_count = lax.axis_size("gx")
    gy_count = lax.axis_size("gy")
    high_count = gy_count // 2
    plane_sizes = (batch_count, gy_count)
    here_batch = lax.axis_index("batch")
    here_gx = lax.axis_index("gx")
    here_high = lax.axis_index("gy") // 2
    here_low = lax.axis_index("gy") % 2
    owned = cache_keys.shape[0]
    head_width = cache_keys.shape[2]
    sequences, steps, width = tokens.shape
    query_cols = w_query.shape[1]
    pair_cols = w_keyval.shape[1]
    all_cols = query_cols + pair_cols
    heads_here = query_cols // head_width
    rows = owned * steps
    rows_here = gx_count * rows
    far = [(db, dh) for db in range(batch_count) for dh in range(high_count) if (db, dh) != (0, 0)]

    arranged = tokens.reshape(batch_count, gx_count, high_count, 2, rows, width)
    arranged = arranged.transpose(3, 0, 2, 1, 4, 5).reshape(sequences * steps, width)
    joined = jnp.concatenate([w_query, w_keyval], axis=1)
    partial = jnp.dot(arranged, joined, preferred_element_type=jnp.float32).astype(jnp.bfloat16)
    partial = partial.reshape(2, sequences * steps // 2, all_cols)
    kept = lax.dynamic_index_in_dim(partial, here_low, 0, keepdims=False)
    given = lax.dynamic_index_in_dim(partial, 1 - here_low, 0, keepdims=False)
    swapped = pair_swap(given, plane_sizes)
    half = (kept.astype(jnp.float32) + swapped.astype(jnp.float32)).astype(jnp.bfloat16)
    half = half.reshape(batch_count, high_count, rows_here, all_cols)

    def half_block(db, dh):
        block = lax.dynamic_index_in_dim(half, (here_batch + db) % batch_count, 0, keepdims=False)
        return lax.dynamic_index_in_dim(block, (here_high + dh) % high_count, 0, keepdims=False)

    total = half_block(0, 0).astype(jnp.float32)
    for db, dh in far:
        total = total + moved(half_block(db, dh), PLANE, plane_sizes, (db, 2 * dh)).astype(jnp.float32)
    summed = total.astype(jnp.bfloat16).reshape(gx_count, rows, all_cols)

    blocks = [lax.dynamic_index_in_dim(summed, here_gx, 0, keepdims=False)]
    for k in range(1, gx_count):
        block = lax.dynamic_index_in_dim(summed, (here_gx + k) % gx_count, 0, keepdims=False)
        blocks.append(moved(block, "gx", (gx_count,), (k,)))
    mine = jnp.stack(blocks)

    queries = mine[..., :query_cols].reshape(gx_count, owned, steps, heads_here, head_width)
    queries = queries.transpose(1, 2, 0, 3, 4).reshape(owned, steps, gx_count * heads_here, head_width)
    key_value = turned(mine[::-1, :, query_cols:], gx_count - 1 - here_gx, 0)
    key_value = key_value.transpose(1, 0, 2).reshape(owned, steps, gx_count * pair_cols)
    new_keys = key_value[..., :head_width]
    new_values = key_value[..., head_width:]
    positions = (lengths[:, None] + jnp.arange(steps, dtype=jnp.int32)[None, :]).astype(jnp.float32)
    rot_queries = rotate(queries.astype(jnp.float32), positions[:, :, None]).astype(jnp.bfloat16)
    rot_keys = rotate(new_keys.astype(jnp.float32), positions).astype(jnp.bfloat16)
    attended = jax.vmap(attend)(
        rot_queries, cache_keys, cache_values, rot_keys, new_values, lengths
    )

    by_group = attended.reshape(rows, gx_count, query_cols)
    blocks = [by_group[:, 0]]
    for k in range(1, gx_count):
        blocks.append(moved(by_group[:, k], "gx", (gx_count,), (-k,)))
    grouped = turned(jnp.stack(blocks), (gx_count - here_gx) % gx_count, 0).reshape(rows_here, query_cols)

    quarter = [[None] * high_count for _ in range(batch_count)]
    quarter[0][0] = grouped
    for db, dh in far:
        quarter[db][dh] = moved(grouped, PLANE, plane_sizes, (-db, -2 * dh))
    gathered = jnp.stack([jnp.stack(line) for line in quarter])
    gathered = turned(gathered, (batch_count - here_batch) % batch_count, 0)
    gathered = turned(gathered, (high_count - here_high) % high_count, 1)
    other = pair_swap(gathered, plane_sizes)
    first = jnp.where(here_low == 0, gathered, other)
    second = jnp.where(here_low == 0, other, gathered)
    everyone = jnp.stack([first, second], axis=2)
    everyone = everyone.reshape(batch_count, gy_count, gx_count, rows, query_cols)
    everyone = everyone.transpose(0, 2, 1, 3, 4).reshape(sequences * steps, query_cols)
    outs = jnp.dot(everyone, w_out, preferred_element_type=jnp.float32).astype(jnp.bfloat16)
    out_cols = w_out.shape[1]
    outs = outs.reshape(gx_count, sequences * steps // gx_count, out_cols)
    mixed = lax.dynamic_index_in_dim(outs, here_gx, 0, keepdims=False).astype(jnp.float32)
    for k in range(1, gx_count):
        block = lax.dynamic_index_in_dim(outs, (here_gx + k) % gx_count, 0, keepdims=False)
        mixed = mixed + moved(block, "gx", (gx_count,), (k,)).astype(jnp.float32)
    return mixed.astype(jnp.bfloat16).reshape(sequences // gx_count, steps, out_cols)


def solution(mesh):
    placed = (
        P(None, None, ("batch", "gy")),
        P(("batch", "gy"), "gx"),
        P(("batch", "gy"), "gx"),
        P("gx", ("batch", "gy")),
        P(("batch", "gx", "gy"), None, None),
        P(("batch", "gx", "gy"), None, None),
        P(("batch", "gx", "gy")),
    )
    return jax.shard_map(
        local, mesh=mesh, in_specs=placed, out_specs=P("gx", None, ("batch", "gy")), check_vma=False
    )
```

```python
import functools

import jax
import jax.numpy as jnp
import numpy as np
from jax import lax
from jax.experimental import pallas as pl
from jax.experimental.pallas import tpu as pltpu
from jax.sharding import Mesh
from jax.sharding import PartitionSpec as P

PLANE = ("batch", "gh", "gl")


def swapped_with(value, axes, sizes, differs):
    pairs = []
    for place in np.ndindex(*sizes):
        target = tuple(p ^ d for p, d in zip(place, differs))
        pairs.append((int(np.ravel_multi_index(place, sizes)), int(np.ravel_multi_index(target, sizes))))
    return lax.ppermute(value, axes, pairs)


def unxored(blocks, here):
    count = len(blocks)
    bit = 1
    while bit < count:
        turn = (here & bit) != 0
        blocks = [jnp.where(turn, blocks[k ^ bit], blocks[k]) for k in range(count)]
        bit *= 2
    return blocks


def project_kernel(
    dims, chunks, low_ref, tokens_hbm, query_hbm, pair_hbm, kept_ref, given_ref, tokens_ref, rows_ref, query_ref, pair_ref, sems
):
    batch_count, gx_count, high_count, owned = dims
    query_cols = query_ref.shape[1]
    copies = [
        pltpu.make_async_copy(tokens_hbm, tokens_ref, sems.at[0]),
        pltpu.make_async_copy(pair_hbm, pair_ref, sems.at[1]),
    ]
    for place, (start, size) in enumerate(chunks):
        window = pl.ds(start, size)
        copies.append(
            pltpu.make_async_copy(query_hbm.at[:, window], query_ref.at[:, window], sems.at[place + 2])
        )
    for copy in copies:
        copy.start()
    steps, width = tokens_ref.shape[1:]
    block = gx_count * owned * steps
    half = rows_ref.shape[0] // 2
    copies[0].wait()
    for relative in range(2):
        low = low_ref[0] if relative == 0 else 1 - low_ref[0]
        for b in range(batch_count):
            for h in range(high_count):
                parts = []
                for g in range(gx_count):
                    first = (((b * gx_count + g) * high_count + h) * 2 + low) * owned
                    parts.append(tokens_ref[pl.ds(first, owned)])
                joined = jnp.concatenate(parts, axis=0).reshape(block, width)
                at = ((relative * batch_count + b) * high_count + h) * block
                rows_ref[pl.ds(at, block)] = joined

    def emit(weights, start):
        product = jnp.dot(rows_ref[...], weights, preferred_element_type=jnp.float32)
        product = product.astype(jnp.bfloat16)
        window = pl.ds(start, product.shape[1])
        kept_ref[:, window] = product[:half]
        given_ref[:, window] = product[half:]

    copies[1].wait()
    emit(pair_ref[...], query_cols)
    for copy, (start, size) in zip(copies[2:], chunks):
        copy.wait()
        emit(query_ref[:, pl.ds(start, size)], start)


def project(tokens, w_query, w_keyval, low, dims):
    sequences, steps, width = tokens.shape
    query_cols, pair_cols = w_query.shape[1], w_keyval.shape[1]
    rows = sequences * steps
    chunks, start = [], 0
    while start < query_cols:
        size = min(512 if query_cols - start > 512 else 256, query_cols - start)
        chunks.append((start, size))
        start += size
    vmem = pl.BlockSpec(memory_space=pltpu.VMEM)
    hbm = pl.BlockSpec(memory_space=pltpu.HBM)
    shape = jax.ShapeDtypeStruct((rows // 2, query_cols + pair_cols), jnp.bfloat16)
    return pl.pallas_call(
        functools.partial(project_kernel, dims, chunks),
        out_shape=(shape, shape),
        in_specs=[pl.BlockSpec(memory_space=pltpu.SMEM), hbm, hbm, hbm],
        out_specs=(vmem, vmem),
        scratch_shapes=[
            pltpu.VMEM(tokens.shape, jnp.bfloat16),
            pltpu.VMEM((rows, width), jnp.bfloat16),
            pltpu.VMEM((width, query_cols), jnp.bfloat16),
            pltpu.VMEM((width, pair_cols), jnp.bfloat16),
            pltpu.SemaphoreType.DMA((2 + len(chunks),)),
        ],
        compiler_params=pltpu.CompilerParams(vmem_limit_bytes=58 * 1024 * 1024),
        cost_estimate=pl.CostEstimate(
            flops=2 * rows * width * (query_cols + pair_cols),
            bytes_accessed=2 * width * (query_cols + pair_cols),
            transcendentals=0,
        ),
        name="project",
    )(low, tokens, w_query, w_keyval)


def attend_kernel(dims, place_ref, lengths_ref, cos_ref, sin_ref, keys_ref, values_ref, *refs):
    gx_count, owned, steps, heads, width = dims
    blocks, outs, (rows_ref, result_ref) = refs[:gx_count], refs[gx_count:-2], refs[-2:]
    query_cols = heads * width
    half = width // 2
    scaling = 1.0 / width**0.5
    slots = keys_ref.shape[1]
    count = gx_count * heads * steps
    cosine, sine = cos_ref[...], sin_ref[...]

    def turn(first, second):
        return first * cosine - second * sine, second * cosine + first * sine

    key_value = [ref[:, pl.ds(query_cols, ref.shape[1] - query_cols)].astype(jnp.float32) for ref in blocks]
    key_value = jnp.concatenate(unxored(key_value, place_ref[0]), axis=1)
    new_values = key_value[:, width:]
    new_keys = turn(key_value[:, :half], key_value[:, half:width])
    new_keys = jnp.concatenate(new_keys, axis=1).astype(jnp.bfloat16).astype(jnp.float32)
    for k in range(gx_count):
        for h in range(heads):
            first = blocks[k][:, pl.ds(h * width, half)].astype(jnp.float32)
            second = blocks[k][:, pl.ds(h * width + half, half)].astype(jnp.float32)
            for part, value in enumerate(turn(first, second)):
                for s in range(owned):
                    window = pl.ds((k * heads + h) * steps, steps)
                    rows_ref[s, window, pl.ds(part * half, half)] = value[s * steps : (s + 1) * steps]
    step_of = lax.broadcasted_iota(jnp.int32, (count, 1), 0) % steps
    slot_of = lax.broadcasted_iota(jnp.int32, (1, slots), 1)
    for s in range(owned):
        queries = rows_ref[s].astype(jnp.bfloat16)
        cached = lax.dot_general(
            queries, keys_ref[s], (((1,), (1,)), ((), ())), preferred_element_type=jnp.float32
        )
        cached = jnp.where(slot_of < lengths_ref[s], cached * scaling, -1e30)
        highest = cached.max(-1, keepdims=True)
        wide = queries.astype(jnp.float32)
        fresh = []
        for u in range(steps):
            row = s * steps + u
            score = (wide * new_keys[row : row + 1]).sum(-1, keepdims=True) * scaling
            fresh.append(jnp.where(step_of >= u, score, -1e30))
            highest = jnp.maximum(highest, fresh[-1])
        exp_cached = jnp.exp(cached - highest)
        denom = exp_cached.sum(-1, keepdims=True)
        total = jnp.dot(
            exp_cached.astype(jnp.bfloat16), values_ref[s], preferred_element_type=jnp.float32
        )
        for u in range(steps):
            row = s * steps + u
            exp_fresh = jnp.exp(fresh[u] - highest)
            denom = denom + exp_fresh
            total = total + exp_fresh * new_values[row : row + 1]
        result_ref[s] = total / denom
    for k in range(gx_count):
        for h in range(heads):
            window = pl.ds((k * heads + h) * steps, steps)
            value = jnp.concatenate([result_ref[s, window] for s in range(owned)], axis=0)
            outs[k][:, pl.ds(h * width, width)] = value.astype(jnp.bfloat16)


def attend(blocks, cache_keys, cache_values, lengths, place, query_cols):
    gx_count = len(blocks)
    owned, slots, width = cache_keys.shape
    rows = blocks[0].shape[0]
    steps = rows // owned
    heads = query_cols // width
    count = gx_count * heads * steps
    freqs = 10000.0 ** (-(jnp.arange(width // 2, dtype=jnp.float32) * 2.0 / width))
    positions = (lengths[:, None] + jnp.arange(steps, dtype=jnp.int32)[None, :]).astype(jnp.float32)
    angles = positions.reshape(rows, 1) * freqs
    vmem = pl.BlockSpec(memory_space=pltpu.VMEM)
    smem = pl.BlockSpec(memory_space=pltpu.SMEM)
    return pl.pallas_call(
        functools.partial(attend_kernel, (gx_count, owned, steps, heads, width)),
        out_shape=[jax.ShapeDtypeStruct((rows, query_cols), jnp.bfloat16)] * gx_count,
        in_specs=[smem, smem] + [vmem] * (4 + gx_count),
        out_specs=[vmem] * gx_count,
        scratch_shapes=[
            pltpu.VMEM((owned, count, width), jnp.float32),
            pltpu.VMEM((owned, count, width), jnp.float32),
        ],
        compiler_params=pltpu.CompilerParams(vmem_limit_bytes=24 * 1024 * 1024),
        cost_estimate=pl.CostEstimate(
            flops=200 * owned * count * slots * width,
            bytes_accessed=4 * owned * slots * width,
            transcendentals=owned * count * slots,
        ),
        name="attend",
    )(place, lengths, jnp.cos(angles), jnp.sin(angles), cache_keys, cache_values, *blocks)


def mix_kernel(dims, chunk, where_ref, weight_ref, *refs):
    batch_count, gx_count, high_count, block = dims
    count = 2 * batch_count * high_count
    blocks, own_ref, sends, (rows_ref, sum_ref) = refs[:count], refs[count], refs[count + 1 : -2], refs[-2:]
    shards = gx_count // batch_count
    group = block // shards
    for relative in range(2):
        for db in range(batch_count):
            for dh in range(high_count):
                b, h = where_ref[1] ^ db, where_ref[2] ^ dh
                at = ((relative * batch_count + b) * high_count + h) * block
                source = blocks[(relative * batch_count + db) * high_count + dh]
                rows_ref[pl.ds(pl.multiple_of(at, block), block)] = source[...]
    lhs = rows_ref[...]
    out_cols = weight_ref.shape[1]
    for start in range(0, out_cols, chunk):
        size = min(chunk, out_cols - start)
        window = pl.ds(start, size)
        sum_ref[:, pl.ds(0, size)] = jnp.dot(
            lhs, weight_ref[:, window], preferred_element_type=jnp.float32
        )
        for k in range(gx_count):
            shard = where_ref[0] ^ k
            b, hi = shard // shards, shard % shards
            parts = []
            for relative in range(2):
                for h in range(high_count):
                    at = ((relative * batch_count + b) * high_count + h) * block + hi * group
                    at = pl.multiple_of(at, group)
                    parts.append(sum_ref[pl.ds(at, group), pl.ds(0, size)])
            piece = jnp.concatenate(parts, axis=0)
            target = own_ref if k == 0 else sends[k - 1]
            target[:, window] = piece.astype(target.dtype)


def mix(blocks, w_out, where, dims):
    batch_count, gx_count, high_count, block = dims
    depth, out_cols = w_out.shape
    rows = len(blocks) * block
    chunk = min(768, out_cols)
    vmem = pl.BlockSpec(memory_space=pltpu.VMEM)
    shapes = [jax.ShapeDtypeStruct((rows // gx_count, out_cols), jnp.float32)]
    shapes += [jax.ShapeDtypeStruct((rows // gx_count, out_cols), jnp.bfloat16)] * (gx_count - 1)
    return pl.pallas_call(
        functools.partial(mix_kernel, dims, chunk),
        out_shape=shapes,
        in_specs=[pl.BlockSpec(memory_space=pltpu.SMEM)] + [vmem] * (1 + len(blocks)),
        out_specs=[vmem] * gx_count,
        scratch_shapes=[pltpu.VMEM((rows, depth), jnp.bfloat16), pltpu.VMEM((rows, chunk), jnp.float32)],
        compiler_params=pltpu.CompilerParams(vmem_limit_bytes=36 * 1024 * 1024),
        cost_estimate=pl.CostEstimate(
            flops=2 * rows * depth * out_cols, bytes_accessed=2 * depth * out_cols, transcendentals=0
        ),
        name="mix",
    )(where, w_out, *blocks)


def finish_kernel(dims, low_ref, own_ref, *refs):
    received, out_ref = refs[:-1], refs[-1]
    batch_count, high_count, owned = dims
    steps, out_cols = out_ref.shape[1:]
    size = batch_count * owned * steps
    for relative in range(2):
        low = low_ref[0] if relative == 0 else 1 - low_ref[0]
        for h in range(high_count):
            window = pl.ds((relative * high_count + h) * size, size)
            total = own_ref[window]
            for other in received:
                total = total + other[window].astype(jnp.float32)
            total = total.reshape(batch_count, owned, steps, out_cols).astype(jnp.bfloat16)
            for g in range(batch_count):
                first = ((g * high_count + h) * 2 + low) * owned
                out_ref[pl.ds(first, owned)] = total[g]


def finish(own, received, low, dims, steps):
    rows, out_cols = own.shape
    vmem = pl.BlockSpec(memory_space=pltpu.VMEM)
    return pl.pallas_call(
        functools.partial(finish_kernel, dims),
        out_shape=jax.ShapeDtypeStruct((rows // steps, steps, out_cols), jnp.bfloat16),
        in_specs=[pl.BlockSpec(memory_space=pltpu.SMEM)] + [vmem] * (1 + len(received)),
        out_specs=vmem,
        compiler_params=pltpu.CompilerParams(vmem_limit_bytes=16 * 1024 * 1024),
        name="finish",
    )(low, own, *received)


def local(tokens, w_query, w_keyval, w_out, cache_keys, cache_values, lengths):
    batch_count = lax.axis_size("batch")
    gx_count = lax.axis_size("gx")
    high_count = lax.axis_size("gh")
    sizes = (batch_count, high_count, 2)
    here_batch = lax.axis_index("batch")
    here_gx = lax.axis_index("gx")
    here_high = lax.axis_index("gh")
    here_low = lax.axis_index("gl")
    low = here_low.astype(jnp.int32).reshape(1)
    owned = cache_keys.shape[0]
    sequences, steps, width = tokens.shape
    query_cols = w_query.shape[1]
    pair_cols = w_keyval.shape[1]
    all_cols = query_cols + pair_cols
    rows = owned * steps
    rows_here = gx_count * rows

    kept, given = project(tokens, w_query, w_keyval, low, (batch_count, gx_count, high_count, owned))
    taken = swapped_with(given, PLANE, sizes, (0, 0, 1))
    half = (kept.astype(jnp.float32) + taken.astype(jnp.float32)).astype(jnp.bfloat16)
    half = half.reshape(batch_count, high_count, rows_here, all_cols)
    far = [(db, dh) for db in range(batch_count) for dh in range(high_count)]

    def half_block(db, dh):
        block = lax.dynamic_index_in_dim(half, here_batch ^ db, 0, keepdims=False)
        return lax.dynamic_index_in_dim(block, here_high ^ dh, 0, keepdims=False)

    total = half_block(0, 0).astype(jnp.float32)
    for db, dh in far[1:]:
        total = total + swapped_with(half_block(db, dh), PLANE, sizes, (db, dh, 0)).astype(jnp.float32)
    summed = total.astype(jnp.bfloat16).reshape(gx_count, rows, all_cols)

    blocks = [lax.dynamic_index_in_dim(summed, here_gx, 0, keepdims=False)]
    for k in range(1, gx_count):
        block = lax.dynamic_index_in_dim(summed, here_gx ^ k, 0, keepdims=False)
        blocks.append(swapped_with(block, "gx", (gx_count,), (k,)))
    place = here_gx.astype(jnp.int32).reshape(1)
    blocks = attend(blocks, cache_keys, cache_values, lengths, place, query_cols)
    blocks = [blocks[0]] + [
        swapped_with(blocks[k], "gx", (gx_count,), (k,)) for k in range(1, gx_count)
    ]
    grouped = jnp.stack(unxored(blocks, here_gx)).reshape(rows_here, query_cols)

    ours = [grouped] + [swapped_with(grouped, PLANE, sizes, (db, dh, 0)) for db, dh in far[1:]]
    theirs = [swapped_with(block, PLANE, sizes, (0, 0, 1)) for block in ours]
    where = jnp.stack([here_gx, here_batch, here_high]).astype(jnp.int32)
    own, *sends = mix(ours + theirs, w_out, where, (batch_count, gx_count, high_count, rows_here))
    received = [swapped_with(sends[k - 1], "gx", (gx_count,), (k,)) for k in range(1, gx_count)]
    return finish(own, received, low, (batch_count, high_count, owned), steps)


def solution(mesh):
    batch_count, gx_count, gy_count = mesh.devices.shape
    split = Mesh(
        mesh.devices.reshape(batch_count, gx_count, gy_count // 2, 2), ("batch", "gx", "gh", "gl")
    )
    plane = ("batch", "gh", "gl")
    placed = (
        P(None, None, plane),
        P(plane, "gx"),
        P(plane, "gx"),
        P("gx", plane),
        P(("batch", "gx", "gh", "gl"), None, None),
        P(("batch", "gx", "gh", "gl"), None, None),
        P(("batch", "gx", "gh", "gl")),
    )
    return jax.shard_map(
        local, mesh=split, in_specs=placed, out_specs=P("gx", None, plane), check_vma=False
    )
```

```python
import functools

import jax
import jax.numpy as jnp
import numpy as np
from jax import lax
from jax.experimental import pallas as pl
from jax.experimental.pallas import tpu as pltpu
from jax.sharding import Mesh
from jax.sharding import PartitionSpec as P

PLANE = ("batch", "gh", "gl")


def swapped_with(value, axes, sizes, differs):
    pairs = []
    for place in np.ndindex(*sizes):
        target = tuple(p ^ d for p, d in zip(place, differs))
        pairs.append((int(np.ravel_multi_index(place, sizes)), int(np.ravel_multi_index(target, sizes))))
    return lax.ppermute(value, axes, pairs)


def unxored(blocks, here):
    count = len(blocks)
    bit = 1
    while bit < count:
        turn = (here & bit) != 0
        blocks = [jnp.where(turn, blocks[k ^ bit], blocks[k]) for k in range(count)]
        bit *= 2
    return blocks


def project_kernel(
    dims, chunks, low_ref, tokens_hbm, query_hbm, pair_hbm, kept_ref, given_ref, tokens_ref, rows_ref, query_ref, pair_ref, sems
):
    batch_count, gx_count, high_count, owned = dims
    query_cols = query_ref.shape[1]
    copies = [
        pltpu.make_async_copy(tokens_hbm, tokens_ref, sems.at[0]),
        pltpu.make_async_copy(pair_hbm, pair_ref, sems.at[1]),
    ]
    for place, (start, size) in enumerate(chunks):
        window = pl.ds(start, size)
        copies.append(
            pltpu.make_async_copy(query_hbm.at[:, window], query_ref.at[:, window], sems.at[place + 2])
        )
    for copy in copies:
        copy.start()
    steps, width = tokens_ref.shape[1:]
    block = gx_count * owned * steps
    half = rows_ref.shape[0] // 2
    copies[0].wait()
    for relative in range(2):
        low = low_ref[0] if relative == 0 else 1 - low_ref[0]
        for b in range(batch_count):
            for h in range(high_count):
                parts = []
                for g in range(gx_count):
                    first = (((b * gx_count + g) * high_count + h) * 2 + low) * owned
                    parts.append(tokens_ref[pl.ds(first, owned)])
                joined = jnp.concatenate(parts, axis=0).reshape(block, width)
                at = ((relative * batch_count + b) * high_count + h) * block
                rows_ref[pl.ds(at, block)] = joined

    def emit(weights, start):
        product = jnp.dot(rows_ref[...], weights, preferred_element_type=jnp.float32)
        product = product.astype(jnp.bfloat16)
        window = pl.ds(start, product.shape[1])
        kept_ref[:, window] = product[:half]
        given_ref[:, window] = product[half:]

    copies[1].wait()
    emit(pair_ref[...], query_cols)
    for copy, (start, size) in zip(copies[2:], chunks):
        copy.wait()
        emit(query_ref[:, pl.ds(start, size)], start)


def project(tokens, w_query, w_keyval, low, dims):
    sequences, steps, width = tokens.shape
    query_cols, pair_cols = w_query.shape[1], w_keyval.shape[1]
    rows = sequences * steps
    chunks, start = [], 0
    while start < query_cols:
        size = min(512 if query_cols - start > 512 else 256, query_cols - start)
        chunks.append((start, size))
        start += size
    vmem = pl.BlockSpec(memory_space=pltpu.VMEM)
    hbm = pl.BlockSpec(memory_space=pltpu.HBM)
    shape = jax.ShapeDtypeStruct((rows // 2, query_cols + pair_cols), jnp.bfloat16)
    return pl.pallas_call(
        functools.partial(project_kernel, dims, chunks),
        out_shape=(shape, shape),
        in_specs=[pl.BlockSpec(memory_space=pltpu.SMEM), hbm, hbm, hbm],
        out_specs=(vmem, vmem),
        scratch_shapes=[
            pltpu.VMEM(tokens.shape, jnp.bfloat16),
            pltpu.VMEM((rows, width), jnp.bfloat16),
            pltpu.VMEM((width, query_cols), jnp.bfloat16),
            pltpu.VMEM((width, pair_cols), jnp.bfloat16),
            pltpu.SemaphoreType.DMA((2 + len(chunks),)),
        ],
        compiler_params=pltpu.CompilerParams(vmem_limit_bytes=62 * 1024 * 1024),
        cost_estimate=pl.CostEstimate(
            flops=2 * rows * width * (query_cols + pair_cols),
            bytes_accessed=2 * width * (query_cols + pair_cols),
            transcendentals=0,
        ),
        name="project",
    )(low, tokens, w_query, w_keyval)


def near_kernel(after_ref, source_ref, target_ref, token_ref, sem):
    copy = pltpu.make_async_copy(source_ref, target_ref, sem)
    copy.start()
    copy.wait()
    token_ref[...] = jnp.zeros_like(token_ref)


def near(after, array):
    anywhere = pl.BlockSpec(memory_space=pl.ANY)
    return pl.pallas_call(
        near_kernel,
        out_shape=(
            jax.ShapeDtypeStruct(array.shape, array.dtype),
            jax.ShapeDtypeStruct((8, 128), jnp.float32),
        ),
        in_specs=[anywhere, anywhere],
        out_specs=(anywhere, pl.BlockSpec(memory_space=pltpu.VMEM)),
        scratch_shapes=[pltpu.SemaphoreType.DMA],
        compiler_params=pltpu.CompilerParams(vmem_limit_bytes=36 * 1024 * 1024),
        cost_estimate=pl.CostEstimate(
            flops=0, bytes_accessed=2 * array.size * array.dtype.itemsize, transcendentals=0
        ),
        name="near",
    )(after, array)


def staged_kernel(source_ref, target_ref):
    target_ref[...] = source_ref[...]


def staged(array):
    vmem = pl.BlockSpec(memory_space=pltpu.VMEM)
    return pl.pallas_call(
        staged_kernel,
        out_shape=jax.ShapeDtypeStruct(array.shape, array.dtype),
        in_specs=[vmem],
        out_specs=vmem,
        compiler_params=pltpu.CompilerParams(vmem_limit_bytes=8 * 1024 * 1024),
        name="staged",
    )(array)


def combine_kernel(dims, place_ref, kept_ref, taken_ref, own_ref, *sends):
    batch_count, high_count, block = dims
    for db in range(batch_count):
        for dh in range(high_count):
            at = ((place_ref[1] ^ db) * high_count + (place_ref[2] ^ dh)) * block
            window = pl.ds(pl.multiple_of(at, block), block)
            total = kept_ref[window].astype(jnp.float32) + taken_ref[window].astype(jnp.float32)
            target = sends[db * high_count + dh - 1] if db or dh else own_ref
            target[...] = total.astype(target.dtype)


def combine(kept, taken, place, dims):
    batch_count, high_count, block = dims
    cols = kept.shape[1]
    vmem = pl.BlockSpec(memory_space=pltpu.VMEM)
    count = batch_count * high_count
    return pl.pallas_call(
        functools.partial(combine_kernel, dims),
        out_shape=[jax.ShapeDtypeStruct((block, cols), jnp.float32)]
        + [jax.ShapeDtypeStruct((block, cols), jnp.bfloat16)] * (count - 1),
        in_specs=[pl.BlockSpec(memory_space=pltpu.SMEM), vmem, vmem],
        out_specs=[vmem] * count,
        compiler_params=pltpu.CompilerParams(vmem_limit_bytes=8 * 1024 * 1024),
        name="combine",
    )(place, kept, taken)


def collect_kernel(count, place_ref, own_ref, after_ref, *refs):
    received, outs, total_ref = refs[: -count - 1], refs[-count - 1 : -1], refs[-1]
    total = own_ref[...]
    for other in received:
        total = total + other[...].astype(jnp.float32)
    rows = outs[0].shape[0]
    for g in range(count):
        total_ref[g] = total[g * rows : (g + 1) * rows]
    for k in range(count):
        outs[k][...] = total_ref[place_ref[0] ^ k].astype(jnp.bfloat16)


def collect(own, received, place, after, gx_count):
    block, cols = own.shape
    rows = block // gx_count
    vmem = pl.BlockSpec(memory_space=pltpu.VMEM)
    return pl.pallas_call(
        functools.partial(collect_kernel, gx_count),
        out_shape=[jax.ShapeDtypeStruct((rows, cols), jnp.bfloat16)] * gx_count,
        in_specs=[pl.BlockSpec(memory_space=pltpu.SMEM), vmem, pl.BlockSpec(memory_space=pl.ANY)]
        + [vmem] * len(received),
        out_specs=[vmem] * gx_count,
        scratch_shapes=[pltpu.VMEM((gx_count, rows, cols), jnp.float32)],
        compiler_params=pltpu.CompilerParams(vmem_limit_bytes=8 * 1024 * 1024),
        name="collect",
    )(place, own, after, *received)


def attend_kernel(dims, place_ref, lengths_ref, cos_ref, sin_ref, keys_ref, values_ref, *refs):
    gx_count, owned, steps, heads, width = dims
    blocks, outs, (rows_ref, result_ref) = refs[:gx_count], refs[gx_count:-2], refs[-2:]
    query_cols = heads * width
    half = width // 2
    scaling = 1.0 / width**0.5
    slots = keys_ref.shape[1]
    count = gx_count * heads * steps
    cosine, sine = cos_ref[...], sin_ref[...]

    def turn(first, second):
        return first * cosine - second * sine, second * cosine + first * sine

    key_value = [ref[:, pl.ds(query_cols, ref.shape[1] - query_cols)].astype(jnp.float32) for ref in blocks]
    key_value = jnp.concatenate(unxored(key_value, place_ref[0]), axis=1)
    new_values = key_value[:, width:]
    new_keys = turn(key_value[:, :half], key_value[:, half:width])
    new_keys = jnp.concatenate(new_keys, axis=1).astype(jnp.bfloat16).astype(jnp.float32)
    for k in range(gx_count):
        for h in range(heads):
            first = blocks[k][:, pl.ds(h * width, half)].astype(jnp.float32)
            second = blocks[k][:, pl.ds(h * width + half, half)].astype(jnp.float32)
            for part, value in enumerate(turn(first, second)):
                for s in range(owned):
                    window = pl.ds((k * heads + h) * steps, steps)
                    rows_ref[s, window, pl.ds(part * half, half)] = value[s * steps : (s + 1) * steps]
    step_of = lax.broadcasted_iota(jnp.int32, (count, 1), 0) % steps
    slot_of = lax.broadcasted_iota(jnp.int32, (1, slots), 1)
    for s in range(owned):
        queries = rows_ref[s].astype(jnp.bfloat16)
        cached = lax.dot_general(
            queries, keys_ref[s], (((1,), (1,)), ((), ())), preferred_element_type=jnp.float32
        )
        cached = jnp.where(slot_of < lengths_ref[s], cached * scaling, -1e30)
        highest = cached.max(-1, keepdims=True)
        wide = queries.astype(jnp.float32)
        fresh = []
        for u in range(steps):
            row = s * steps + u
            score = (wide * new_keys[row : row + 1]).sum(-1, keepdims=True) * scaling
            fresh.append(jnp.where(step_of >= u, score, -1e30))
            highest = jnp.maximum(highest, fresh[-1])
        exp_cached = jnp.exp(cached - highest)
        denom = exp_cached.sum(-1, keepdims=True)
        total = jnp.dot(
            exp_cached.astype(jnp.bfloat16), values_ref[s], preferred_element_type=jnp.float32
        )
        for u in range(steps):
            row = s * steps + u
            exp_fresh = jnp.exp(fresh[u] - highest)
            denom = denom + exp_fresh
            total = total + exp_fresh * new_values[row : row + 1]
        result_ref[s] = total / denom
    for k in range(gx_count):
        for h in range(heads):
            window = pl.ds((k * heads + h) * steps, steps)
            value = jnp.concatenate([result_ref[s, window] for s in range(owned)], axis=0)
            outs[k][:, pl.ds(h * width, width)] = value.astype(jnp.bfloat16)


def attend(blocks, cache_keys, cache_values, lengths, place, query_cols):
    gx_count = len(blocks)
    owned, slots, width = cache_keys.shape
    rows = blocks[0].shape[0]
    steps = rows // owned
    heads = query_cols // width
    count = gx_count * heads * steps
    freqs = 10000.0 ** (-(jnp.arange(width // 2, dtype=jnp.float32) * 2.0 / width))
    positions = (lengths[:, None] + jnp.arange(steps, dtype=jnp.int32)[None, :]).astype(jnp.float32)
    angles = positions.reshape(rows, 1) * freqs
    vmem = pl.BlockSpec(memory_space=pltpu.VMEM)
    smem = pl.BlockSpec(memory_space=pltpu.SMEM)
    return pl.pallas_call(
        functools.partial(attend_kernel, (gx_count, owned, steps, heads, width)),
        out_shape=[jax.ShapeDtypeStruct((rows, query_cols), jnp.bfloat16)] * gx_count,
        in_specs=[smem, smem] + [vmem] * (4 + gx_count),
        out_specs=[vmem] * gx_count,
        scratch_shapes=[
            pltpu.VMEM((owned, count, width), jnp.float32),
            pltpu.VMEM((owned, count, width), jnp.float32),
        ],
        compiler_params=pltpu.CompilerParams(vmem_limit_bytes=12 * 1024 * 1024),
        cost_estimate=pl.CostEstimate(
            flops=4 * owned * count * slots * width,
            bytes_accessed=4 * owned * slots * width,
            transcendentals=owned * count * slots,
        ),
        name="attend",
    )(place, lengths, jnp.cos(angles), jnp.sin(angles), cache_keys, cache_values, *blocks)


def mix_kernel(dims, chunk, where_ref, weight_ref, *refs):
    batch_count, gx_count, high_count, block = dims
    count = 2 * batch_count * high_count
    blocks, own_ref, sends, (rows_ref, sum_ref) = refs[:count], refs[count], refs[count + 1 : -2], refs[-2:]
    shards = gx_count // batch_count
    group = block // shards
    for relative in range(2):
        for db in range(batch_count):
            for dh in range(high_count):
                b, h = where_ref[1] ^ db, where_ref[2] ^ dh
                at = ((relative * batch_count + b) * high_count + h) * block
                source = blocks[(relative * batch_count + db) * high_count + dh]
                rows_ref[pl.ds(pl.multiple_of(at, block), block)] = source[...]
    lhs = rows_ref[...]
    out_cols = weight_ref.shape[1]
    for start in range(0, out_cols, chunk):
        size = min(chunk, out_cols - start)
        window = pl.ds(start, size)
        sum_ref[:, pl.ds(0, size)] = jnp.dot(
            lhs, weight_ref[:, window], preferred_element_type=jnp.float32
        )
        for k in range(gx_count):
            shard = where_ref[0] ^ k
            b, hi = shard // shards, shard % shards
            parts = []
            for relative in range(2):
                for h in range(high_count):
                    at = ((relative * batch_count + b) * high_count + h) * block + hi * group
                    at = pl.multiple_of(at, group)
                    parts.append(sum_ref[pl.ds(at, group), pl.ds(0, size)])
            piece = jnp.concatenate(parts, axis=0)
            target = own_ref if k == 0 else sends[k - 1]
            target[:, window] = piece.astype(target.dtype)


def mix(blocks, w_out, where, dims):
    batch_count, gx_count, high_count, block = dims
    depth, out_cols = w_out.shape
    rows = len(blocks) * block
    chunk = min(768, out_cols)
    vmem = pl.BlockSpec(memory_space=pltpu.VMEM)
    shapes = [jax.ShapeDtypeStruct((rows // gx_count, out_cols), jnp.float32)]
    shapes += [jax.ShapeDtypeStruct((rows // gx_count, out_cols), jnp.bfloat16)] * (gx_count - 1)
    return pl.pallas_call(
        functools.partial(mix_kernel, dims, chunk),
        out_shape=shapes,
        in_specs=[pl.BlockSpec(memory_space=pltpu.SMEM)] + [vmem] * (1 + len(blocks)),
        out_specs=[vmem] * gx_count,
        scratch_shapes=[pltpu.VMEM((rows, depth), jnp.bfloat16), pltpu.VMEM((rows, chunk), jnp.float32)],
        compiler_params=pltpu.CompilerParams(vmem_limit_bytes=20 * 1024 * 1024),
        cost_estimate=pl.CostEstimate(
            flops=2 * rows * depth * out_cols, bytes_accessed=2 * depth * out_cols, transcendentals=0
        ),
        name="mix",
    )(where, w_out, *blocks)


def finish_kernel(dims, low_ref, own_ref, *refs):
    received, out_ref = refs[:-1], refs[-1]
    batch_count, high_count, owned = dims
    steps, out_cols = out_ref.shape[1:]
    size = batch_count * owned * steps
    for relative in range(2):
        low = low_ref[0] if relative == 0 else 1 - low_ref[0]
        for h in range(high_count):
            window = pl.ds((relative * high_count + h) * size, size)
            total = own_ref[window]
            for other in received:
                total = total + other[window].astype(jnp.float32)
            total = total.reshape(batch_count, owned, steps, out_cols).astype(jnp.bfloat16)
            for g in range(batch_count):
                first = ((g * high_count + h) * 2 + low) * owned
                out_ref[pl.ds(first, owned)] = total[g]


def finish(own, received, low, dims, steps):
    rows, out_cols = own.shape
    vmem = pl.BlockSpec(memory_space=pltpu.VMEM)
    return pl.pallas_call(
        functools.partial(finish_kernel, dims),
        out_shape=jax.ShapeDtypeStruct((rows // steps, steps, out_cols), jnp.bfloat16),
        in_specs=[pl.BlockSpec(memory_space=pltpu.SMEM)] + [vmem] * (1 + len(received)),
        out_specs=vmem,
        compiler_params=pltpu.CompilerParams(vmem_limit_bytes=16 * 1024 * 1024),
        name="finish",
    )(low, own, *received)


def local(tokens, w_query, w_keyval, w_out, cache_keys, cache_values, lengths):
    batch_count = lax.axis_size("batch")
    gx_count = lax.axis_size("gx")
    high_count = lax.axis_size("gh")
    sizes = (batch_count, high_count, 2)
    here_batch = lax.axis_index("batch")
    here_gx = lax.axis_index("gx")
    here_high = lax.axis_index("gh")
    here_low = lax.axis_index("gl")
    low = here_low.astype(jnp.int32).reshape(1)
    owned = cache_keys.shape[0]
    sequences, steps, width = tokens.shape
    query_cols = w_query.shape[1]
    rows = owned * steps
    rows_here = gx_count * rows

    kept, given = project(tokens, w_query, w_keyval, low, (batch_count, gx_count, high_count, owned))
    taken = swapped_with(given, PLANE, sizes, (0, 0, 1))
    place = jnp.stack([here_gx, here_batch, here_high]).astype(jnp.int32)
    far = [(db, dh) for db in range(batch_count) for dh in range(high_count)][1:]
    own, *sends = combine(staged(kept), taken, place, (batch_count, high_count, rows_here))
    received = [
        swapped_with(block, PLANE, sizes, (db, dh, 0)) for block, (db, dh) in zip(sends, far)
    ]
    w_out, token = near(own, w_out)
    blocks = collect(own, received, place, token, gx_count)
    swaps = {k: swapped_with(blocks[k], "gx", (gx_count,), (k,)) for k in reversed(range(1, gx_count))}
    blocks = [blocks[0]] + [swaps[k] for k in range(1, gx_count)]
    blocks = attend(blocks, cache_keys, cache_values, lengths, place, query_cols)
    blocks = [blocks[0]] + [
        swapped_with(blocks[k], "gx", (gx_count,), (k,)) for k in range(1, gx_count)
    ]
    grouped = jnp.stack(unxored(blocks, here_gx)).reshape(rows_here, query_cols)

    ours = [grouped] + [swapped_with(grouped, PLANE, sizes, (db, dh, 0)) for db, dh in far]
    theirs = [swapped_with(block, PLANE, sizes, (0, 0, 1)) for block in ours]
    own, *sends = mix(ours + theirs, w_out, place, (batch_count, gx_count, high_count, rows_here))
    order = [*range(2, gx_count), 1]
    received = [swapped_with(sends[k - 1], "gx", (gx_count,), (k,)) for k in order]
    return finish(own, received, low, (batch_count, high_count, owned), steps)


def solution(mesh):
    batch_count, gx_count, gy_count = mesh.devices.shape
    split = Mesh(
        mesh.devices.reshape(batch_count, gx_count, gy_count // 2, 2), ("batch", "gx", "gh", "gl")
    )
    plane = ("batch", "gh", "gl")
    placed = (
        P(None, None, plane),
        P(plane, "gx"),
        P(plane, "gx"),
        P("gx", plane),
        P(("batch", "gx", "gh", "gl"), None, None),
        P(("batch", "gx", "gh", "gl"), None, None),
        P(("batch", "gx", "gh", "gl")),
    )
    return jax.shard_map(
        local, mesh=split, in_specs=placed, out_specs=P("gx", None, plane), check_vma=False
    )
```

```python
import functools

import jax
import jax.numpy as jnp
import numpy as np
from jax import lax
from jax.experimental import pallas as pl
from jax.experimental.pallas import tpu as pltpu
from jax.sharding import Mesh
from jax.sharding import PartitionSpec as P

PLANE = ("batch", "gh", "gl")


def swapped_with(value, axes, sizes, differs):
    pairs = []
    for place in np.ndindex(*sizes):
        target = tuple(p ^ d for p, d in zip(place, differs))
        pairs.append((int(np.ravel_multi_index(place, sizes)), int(np.ravel_multi_index(target, sizes))))
    return lax.ppermute(value, axes, pairs)


def unxored(blocks, here):
    count = len(blocks)
    bit = 1
    while bit < count:
        turn = (here & bit) != 0
        blocks = [jnp.where(turn, blocks[k ^ bit], blocks[k]) for k in range(count)]
        bit *= 2
    return blocks


def project_kernel(
    dims, chunks, place_ref, tokens_hbm, query_hbm, pair_hbm, kept_ref, given_ref, tokens_ref, rows_ref, query_ref, pair_ref, sems
):
    batch_count, gx_count, high_count, owned = dims
    query_cols = query_ref.shape[1]
    copies = [
        pltpu.make_async_copy(tokens_hbm, tokens_ref, sems.at[0]),
        pltpu.make_async_copy(pair_hbm, pair_ref, sems.at[1]),
    ]
    for place, (start, size) in enumerate(chunks):
        window = pl.ds(start, size)
        copies.append(
            pltpu.make_async_copy(query_hbm.at[:, window], query_ref.at[:, window], sems.at[place + 2])
        )
    for copy in copies:
        copy.start()
    steps, width = tokens_ref.shape[1:]
    block = gx_count * owned * steps
    half = rows_ref.shape[0] // 2
    copies[0].wait()
    for relative in range(2):
        low = place_ref[3] if relative == 0 else 1 - place_ref[3]
        for b in range(batch_count):
            for h in range(high_count):
                parts = []
                for g in range(gx_count):
                    first = (((b * gx_count + g) * high_count + h) * 2 + low) * owned
                    parts.append(tokens_ref[pl.ds(first, owned)])
                joined = jnp.concatenate(parts, axis=0).reshape(block, width)
                at = ((relative * batch_count + b) * high_count + h) * block
                rows_ref[pl.ds(at, block)] = joined

    def emit(weights, start):
        product = jnp.dot(rows_ref[...], weights, preferred_element_type=jnp.float32)
        product = product.astype(jnp.bfloat16)
        window = pl.ds(start, product.shape[1])
        kept_ref[:, window] = product[:half]
        given_ref[:, window] = product[half:]

    copies[1].wait()
    emit(pair_ref[...], query_cols)
    for copy, (start, size) in zip(copies[2:], chunks):
        copy.wait()
        emit(query_ref[:, pl.ds(start, size)], start)


def project(tokens, w_query, w_keyval, place, dims):
    sequences, steps, width = tokens.shape
    query_cols, pair_cols = w_query.shape[1], w_keyval.shape[1]
    rows = sequences * steps
    chunks, start = [], 0
    while start < query_cols:
        size = min(512 if query_cols - start > 512 else 256, query_cols - start)
        chunks.append((start, size))
        start += size
    vmem = pl.BlockSpec(memory_space=pltpu.VMEM)
    hbm = pl.BlockSpec(memory_space=pltpu.HBM)
    shape = jax.ShapeDtypeStruct((rows // 2, query_cols + pair_cols), jnp.bfloat16)
    return pl.pallas_call(
        functools.partial(project_kernel, dims, chunks),
        out_shape=(shape, shape),
        in_specs=[pl.BlockSpec(memory_space=pltpu.SMEM), hbm, hbm, hbm],
        out_specs=(vmem, vmem),
        scratch_shapes=[
            pltpu.VMEM(tokens.shape, jnp.bfloat16),
            pltpu.VMEM((rows, width), jnp.bfloat16),
            pltpu.VMEM((width, query_cols), jnp.bfloat16),
            pltpu.VMEM((width, pair_cols), jnp.bfloat16),
            pltpu.SemaphoreType.DMA((2 + len(chunks),)),
        ],
        compiler_params=pltpu.CompilerParams(vmem_limit_bytes=62 * 1024 * 1024),
        cost_estimate=pl.CostEstimate(
            flops=2 * rows * width * (query_cols + pair_cols),
            bytes_accessed=2 * width * (query_cols + pair_cols),
            transcendentals=0,
        ),
        name="project",
    )(place, tokens, w_query, w_keyval)


def near_kernel(after_ref, source_ref, target_ref, token_ref, sem):
    copy = pltpu.make_async_copy(source_ref, target_ref, sem)
    copy.start()
    copy.wait()
    token_ref[...] = jnp.zeros_like(token_ref)


def near(after, array):
    anywhere = pl.BlockSpec(memory_space=pl.ANY)
    return pl.pallas_call(
        near_kernel,
        out_shape=(
            jax.ShapeDtypeStruct(array.shape, array.dtype),
            jax.ShapeDtypeStruct((8, 128), jnp.float32),
        ),
        in_specs=[anywhere, anywhere],
        out_specs=(anywhere, pl.BlockSpec(memory_space=pltpu.VMEM)),
        scratch_shapes=[pltpu.SemaphoreType.DMA],
        compiler_params=pltpu.CompilerParams(vmem_limit_bytes=36 * 1024 * 1024),
        cost_estimate=pl.CostEstimate(
            flops=0, bytes_accessed=2 * array.size * array.dtype.itemsize, transcendentals=0
        ),
        name="near",
    )(after, array)


def staged_kernel(source_ref, target_ref):
    target_ref[...] = source_ref[...]


def staged(array):
    vmem = pl.BlockSpec(memory_space=pltpu.VMEM)
    return pl.pallas_call(
        staged_kernel,
        out_shape=jax.ShapeDtypeStruct(array.shape, array.dtype),
        in_specs=[vmem],
        out_specs=vmem,
        compiler_params=pltpu.CompilerParams(vmem_limit_bytes=8 * 1024 * 1024),
        name="staged",
    )(array)


def combine_kernel(dims, place_ref, kept_ref, taken_ref, own_ref, *sends):
    batch_count, high_count, block = dims
    for db in range(batch_count):
        for dh in range(high_count):
            at = ((place_ref[1] ^ db) * high_count + (place_ref[2] ^ dh)) * block
            window = pl.ds(pl.multiple_of(at, block), block)
            total = kept_ref[window].astype(jnp.float32) + taken_ref[window].astype(jnp.float32)
            target = sends[db * high_count + dh - 1] if db or dh else own_ref
            target[...] = total.astype(target.dtype)


def combine(kept, taken, place, dims):
    batch_count, high_count, block = dims
    cols = kept.shape[1]
    vmem = pl.BlockSpec(memory_space=pltpu.VMEM)
    count = batch_count * high_count
    return pl.pallas_call(
        functools.partial(combine_kernel, dims),
        out_shape=[jax.ShapeDtypeStruct((block, cols), jnp.float32)]
        + [jax.ShapeDtypeStruct((block, cols), jnp.bfloat16)] * (count - 1),
        in_specs=[pl.BlockSpec(memory_space=pltpu.SMEM), vmem, vmem],
        out_specs=[vmem] * count,
        compiler_params=pltpu.CompilerParams(vmem_limit_bytes=8 * 1024 * 1024),
        name="combine",
    )(place, kept, taken)


def collect_kernel(count, place_ref, own_ref, after_ref, *refs):
    received, outs, total_ref = refs[: -count - 1], refs[-count - 1 : -1], refs[-1]
    total = own_ref[...]
    for other in received:
        total = total + other[...].astype(jnp.float32)
    rows = outs[0].shape[0]
    for g in range(count):
        total_ref[g] = total[g * rows : (g + 1) * rows]
    for k in range(count):
        outs[k][...] = total_ref[place_ref[0] ^ k].astype(jnp.bfloat16)


def collect(own, received, place, after, gx_count):
    block, cols = own.shape
    rows = block // gx_count
    vmem = pl.BlockSpec(memory_space=pltpu.VMEM)
    return pl.pallas_call(
        functools.partial(collect_kernel, gx_count),
        out_shape=[jax.ShapeDtypeStruct((rows, cols), jnp.bfloat16)] * gx_count,
        in_specs=[pl.BlockSpec(memory_space=pltpu.SMEM), vmem, pl.BlockSpec(memory_space=pl.ANY)]
        + [vmem] * len(received),
        out_specs=[vmem] * gx_count,
        scratch_shapes=[pltpu.VMEM((gx_count, rows, cols), jnp.float32)],
        compiler_params=pltpu.CompilerParams(vmem_limit_bytes=8 * 1024 * 1024),
        name="collect",
    )(place, own, after, *received)


def attend_kernel(dims, place_ref, lengths_ref, cos_ref, sin_ref, keys_ref, values_ref, *refs):
    gx_count, owned, steps, heads, width = dims
    blocks, outs = (refs[0], *refs[gx_count - 1 : 0 : -1]), refs[gx_count:-2]
    rows_ref, result_ref = refs[-2:]
    query_cols = heads * width
    half = width // 2
    scaling = 1.0 / width**0.5
    slots = keys_ref.shape[1]
    count = gx_count * heads * steps
    cosine = jnp.concatenate([cos_ref[s] for s in range(owned)], axis=0)
    sine = jnp.concatenate([sin_ref[s] for s in range(owned)], axis=0)

    def turn(first, second):
        return first * cosine - second * sine, second * cosine + first * sine

    key_value = [ref[:, pl.ds(query_cols, ref.shape[1] - query_cols)].astype(jnp.float32) for ref in blocks]
    key_value = jnp.concatenate(unxored(key_value, place_ref[0]), axis=1)
    new_values = key_value[:, width:]
    new_keys = turn(key_value[:, :half], key_value[:, half:width])
    new_keys = jnp.concatenate(new_keys, axis=1).astype(jnp.bfloat16).astype(jnp.float32)
    for k in range(gx_count):
        for h in range(heads):
            first = blocks[k][:, pl.ds(h * width, half)].astype(jnp.float32)
            second = blocks[k][:, pl.ds(h * width + half, half)].astype(jnp.float32)
            for part, value in enumerate(turn(first, second)):
                for s in range(owned):
                    window = pl.ds((k * heads + h) * steps, steps)
                    rows_ref[s, window, pl.ds(part * half, half)] = value[s * steps : (s + 1) * steps]
    step_of = lax.broadcasted_iota(jnp.int32, (count, 1), 0) % steps
    slot_of = lax.broadcasted_iota(jnp.int32, (1, slots), 1)
    for s in range(owned):
        queries = rows_ref[s].astype(jnp.bfloat16)
        cached = lax.dot_general(
            queries, keys_ref[s], (((1,), (1,)), ((), ())), preferred_element_type=jnp.float32
        )
        cached = jnp.where(slot_of < lengths_ref[s], cached * scaling, -1e30)
        highest = cached.max(-1, keepdims=True)
        wide = queries.astype(jnp.float32)
        fresh = []
        for u in range(steps):
            row = s * steps + u
            score = (wide * new_keys[row : row + 1]).sum(-1, keepdims=True) * scaling
            fresh.append(jnp.where(step_of >= u, score, -1e30))
            highest = jnp.maximum(highest, fresh[-1])
        exp_cached = jnp.exp(cached - highest)
        denom = exp_cached.sum(-1, keepdims=True)
        total = jnp.dot(
            exp_cached.astype(jnp.bfloat16), values_ref[s], preferred_element_type=jnp.float32
        )
        for u in range(steps):
            row = s * steps + u
            exp_fresh = jnp.exp(fresh[u] - highest)
            denom = denom + exp_fresh
            total = total + exp_fresh * new_values[row : row + 1]
        result_ref[s] = total / denom
    for k in range(gx_count):
        for h in range(heads):
            window = pl.ds((k * heads + h) * steps, steps)
            value = jnp.concatenate([result_ref[s, window] for s in range(owned)], axis=0)
            outs[k][:, pl.ds(h * width, width)] = value.astype(jnp.bfloat16)


def attend(blocks, cache_keys, cache_values, lengths, place, query_cols):
    gx_count = len(blocks)
    owned, slots, width = cache_keys.shape
    rows = blocks[0].shape[0]
    steps = rows // owned
    heads = query_cols // width
    count = gx_count * heads * steps
    freqs = 10000.0 ** (-(jnp.arange(width // 2, dtype=jnp.float32) * 2.0 / width))
    positions = lengths[:, None, None] + jnp.arange(steps, dtype=jnp.int32)[None, :, None]
    angles = positions.astype(jnp.float32) * freqs
    vmem = pl.BlockSpec(memory_space=pltpu.VMEM)
    smem = pl.BlockSpec(memory_space=pltpu.SMEM)
    return pl.pallas_call(
        functools.partial(attend_kernel, (gx_count, owned, steps, heads, width)),
        out_shape=[jax.ShapeDtypeStruct((rows, query_cols), jnp.bfloat16)] * gx_count,
        in_specs=[smem, smem] + [vmem] * (4 + gx_count),
        out_specs=[vmem] * gx_count,
        scratch_shapes=[
            pltpu.VMEM((owned, count, width), jnp.float32),
            pltpu.VMEM((owned, count, width), jnp.float32),
        ],
        compiler_params=pltpu.CompilerParams(vmem_limit_bytes=12 * 1024 * 1024),
        cost_estimate=pl.CostEstimate(
            flops=4 * owned * count * slots * width,
            bytes_accessed=4 * owned * slots * width,
            transcendentals=owned * count * slots,
        ),
        name="attend",
    )(place, lengths, jnp.cos(angles), jnp.sin(angles), cache_keys, cache_values, blocks[0], *blocks[:0:-1])


def order_kernel(place_ref, *refs):
    blocks, (out_ref, sorted_ref) = refs[:-2], refs[-2:]
    for k, block in enumerate(blocks):
        sorted_ref[place_ref[0] ^ k] = block[...].astype(jnp.float32)
    parts = [sorted_ref[g] for g in range(len(blocks))]
    out_ref[...] = jnp.concatenate(parts, axis=0).astype(out_ref.dtype)


def order(blocks, place):
    vmem = pl.BlockSpec(memory_space=pltpu.VMEM)
    rows, cols = blocks[0].shape
    count = len(blocks)
    turn = lambda place_ref, *refs: order_kernel(place_ref, refs[0], *refs[count - 1 : 0 : -1], *refs[count:])
    return pl.pallas_call(
        turn,
        out_shape=jax.ShapeDtypeStruct((count * rows, cols), blocks[0].dtype),
        in_specs=[pl.BlockSpec(memory_space=pltpu.SMEM)] + [vmem] * count,
        out_specs=vmem,
        scratch_shapes=[pltpu.VMEM((count, rows, cols), jnp.float32)],
        compiler_params=pltpu.CompilerParams(vmem_limit_bytes=8 * 1024 * 1024),
        name="order",
    )(place, blocks[0], *blocks[:0:-1])


def mix_kernel(dims, chunk, where_ref, weight_ref, *refs):
    batch_count, gx_count, high_count, block = dims
    count = 2 * batch_count * high_count
    blocks, own_ref, sends, (rows_ref, sum_ref) = refs[:count], refs[count], refs[count + 1 : -2], refs[-2:]
    shards = gx_count // batch_count
    group = block // shards
    for relative in range(2):
        for db in range(batch_count):
            for dh in range(high_count):
                b, h = where_ref[1] ^ db, where_ref[2] ^ dh
                at = ((relative * batch_count + b) * high_count + h) * block
                source = blocks[(relative * batch_count + db) * high_count + dh]
                rows_ref[pl.ds(pl.multiple_of(at, block), block)] = source[...]
    lhs = rows_ref[...]
    out_cols = weight_ref.shape[1]
    for start in range(0, out_cols, chunk):
        size = min(chunk, out_cols - start)
        window = pl.ds(start, size)
        sum_ref[:, pl.ds(0, size)] = jnp.dot(
            lhs, weight_ref[:, window], preferred_element_type=jnp.float32
        )
        for k in range(gx_count):
            shard = where_ref[0] ^ k
            b, hi = shard // shards, shard % shards
            parts = []
            for relative in range(2):
                for h in range(high_count):
                    at = ((relative * batch_count + b) * high_count + h) * block + hi * group
                    at = pl.multiple_of(at, group)
                    parts.append(sum_ref[pl.ds(at, group), pl.ds(0, size)])
            piece = jnp.concatenate(parts, axis=0)
            target = own_ref if k == 0 else sends[k - 1]
            target[:, window] = piece.astype(target.dtype)


def mix(blocks, w_out, where, dims):
    batch_count, gx_count, high_count, block = dims
    depth, out_cols = w_out.shape
    rows = len(blocks) * block
    chunk = min(768, out_cols)
    vmem = pl.BlockSpec(memory_space=pltpu.VMEM)
    shapes = [jax.ShapeDtypeStruct((rows // gx_count, out_cols), jnp.float32)]
    shapes += [jax.ShapeDtypeStruct((rows // gx_count, out_cols), jnp.bfloat16)] * (gx_count - 1)
    return pl.pallas_call(
        functools.partial(mix_kernel, dims, chunk),
        out_shape=shapes,
        in_specs=[pl.BlockSpec(memory_space=pltpu.SMEM)] + [vmem] * (1 + len(blocks)),
        out_specs=[vmem] * gx_count,
        scratch_shapes=[pltpu.VMEM((rows, depth), jnp.bfloat16), pltpu.VMEM((rows, chunk), jnp.float32)],
        compiler_params=pltpu.CompilerParams(vmem_limit_bytes=20 * 1024 * 1024),
        cost_estimate=pl.CostEstimate(
            flops=2 * rows * depth * out_cols, bytes_accessed=2 * depth * out_cols, transcendentals=0
        ),
        name="mix",
    )(where, w_out, *blocks)


def finish_kernel(dims, place_ref, own_ref, *refs):
    received, out_ref = refs[:-1], refs[-1]
    batch_count, high_count, owned = dims
    steps, out_cols = out_ref.shape[1:]
    size = batch_count * owned * steps
    for relative in range(2):
        low = place_ref[3] if relative == 0 else 1 - place_ref[3]
        for h in range(high_count):
            window = pl.ds((relative * high_count + h) * size, size)
            total = own_ref[window]
            for other in received:
                total = total + other[window].astype(jnp.float32)
            total = total.reshape(batch_count, owned, steps, out_cols).astype(jnp.bfloat16)
            for g in range(batch_count):
                first = ((g * high_count + h) * 2 + low) * owned
                out_ref[pl.ds(first, owned)] = total[g]


def finish(own, received, place, dims, steps):
    rows, out_cols = own.shape
    vmem = pl.BlockSpec(memory_space=pltpu.VMEM)
    return pl.pallas_call(
        functools.partial(finish_kernel, dims),
        out_shape=jax.ShapeDtypeStruct((rows // steps, steps, out_cols), jnp.bfloat16),
        in_specs=[pl.BlockSpec(memory_space=pltpu.SMEM)] + [vmem] * (1 + len(received)),
        out_specs=vmem,
        compiler_params=pltpu.CompilerParams(vmem_limit_bytes=16 * 1024 * 1024),
        name="finish",
    )(place, own, *received)


def local(tokens, w_query, w_keyval, w_out, cache_keys, cache_values, lengths):
    batch_count = lax.axis_size("batch")
    gx_count = lax.axis_size("gx")
    high_count = lax.axis_size("gh")
    sizes = (batch_count, high_count, 2)
    here_batch = lax.axis_index("batch")
    here_gx = lax.axis_index("gx")
    here_high = lax.axis_index("gh")
    here_low = lax.axis_index("gl")
    place = jnp.stack([here_gx, here_batch, here_high, here_low]).astype(jnp.int32)
    owned = cache_keys.shape[0]
    sequences, steps, width = tokens.shape
    query_cols = w_query.shape[1]
    rows = owned * steps
    rows_here = gx_count * rows

    kept, given = project(tokens, w_query, w_keyval, place, (batch_count, gx_count, high_count, owned))
    taken = swapped_with(given, PLANE, sizes, (0, 0, 1))
    far = [(db, dh) for db in range(batch_count) for dh in range(high_count)][1:]
    own, *sends = combine(staged(kept), taken, place, (batch_count, high_count, rows_here))
    received = [
        swapped_with(block, PLANE, sizes, (db, dh, 0)) for block, (db, dh) in zip(sends, far)
    ]
    w_out, token = near(own, w_out)
    blocks = collect(own, received, place, token, gx_count)
    blocks = [blocks[0]] + [
        swapped_with(blocks[k], "gx", (gx_count,), (k,)) for k in range(1, gx_count)
    ]
    blocks = attend(blocks, cache_keys, cache_values, lengths, place, query_cols)
    blocks = [blocks[0]] + [
        swapped_with(blocks[k], "gx", (gx_count,), (k,)) for k in range(1, gx_count)
    ]
    grouped = order(blocks, place)

    ours = [grouped] + [swapped_with(grouped, PLANE, sizes, (db, dh, 0)) for db, dh in far]
    theirs = [swapped_with(block, PLANE, sizes, (0, 0, 1)) for block in ours]
    own, *sends = mix(ours + theirs, w_out, place, (batch_count, gx_count, high_count, rows_here))
    sequence = [*range(2, gx_count), 1]
    received = [swapped_with(sends[k - 1], "gx", (gx_count,), (k,)) for k in sequence]
    return finish(own, received, place, (batch_count, high_count, owned), steps)


def solution(mesh):
    batch_count, gx_count, gy_count = mesh.devices.shape
    split = Mesh(
        mesh.devices.reshape(batch_count, gx_count, gy_count // 2, 2), ("batch", "gx", "gh", "gl")
    )
    plane = ("batch", "gh", "gl")
    placed = (
        P(None, None, plane),
        P(plane, "gx"),
        P(plane, "gx"),
        P("gx", plane),
        P(("batch", "gx", "gh", "gl"), None, None),
        P(("batch", "gx", "gh", "gl"), None, None),
        P(("batch", "gx", "gh", "gl")),
    )
    return jax.shard_map(
        local, mesh=split, in_specs=placed, out_specs=P("gx", None, plane), check_vma=False
    )
```

```python
import functools

import jax
import jax.numpy as jnp
import numpy as np
from jax import lax
from jax.experimental import pallas as pl
from jax.experimental.pallas import tpu as pltpu
from jax.sharding import Mesh
from jax.sharding import PartitionSpec as P

PLANE = ("batch", "gh", "gl")


def swapped_with(value, axes, sizes, differs):
    pairs = []
    for place in np.ndindex(*sizes):
        target = tuple(p ^ d for p, d in zip(place, differs))
        pairs.append((int(np.ravel_multi_index(place, sizes)), int(np.ravel_multi_index(target, sizes))))
    return lax.ppermute(value, axes, pairs)


def unxored(blocks, here):
    count = len(blocks)
    bit = 1
    while bit < count:
        turn = (here & bit) != 0
        blocks = [jnp.where(turn, blocks[k ^ bit], blocks[k]) for k in range(count)]
        bit *= 2
    return blocks


def farther_first(count):
    return [0, *range(2, count), 1]


def project_kernel(
    dims, chunks, tokens_hbm, query_hbm, pair_hbm, kept_out, given_out, tokens_ref, rows_ref, query_ref, pair_ref, kept_ref, given_ref, sems, out_sems
):
    batch_count, gx_count, high_count, owned = dims
    query_cols = query_ref.shape[1]
    copies = [
        pltpu.make_async_copy(tokens_hbm, tokens_ref, sems.at[0]),
        pltpu.make_async_copy(pair_hbm, pair_ref, sems.at[1]),
    ]
    for place, (start, size) in enumerate(chunks):
        window = pl.ds(start, size)
        copies.append(
            pltpu.make_async_copy(query_hbm.at[:, window], query_ref.at[:, window], sems.at[place + 2])
        )
    for copy in copies:
        copy.start()
    steps, width = tokens_ref.shape[1:]
    block = gx_count * owned * steps
    half = rows_ref.shape[0] // 2
    copies[0].wait()
    for relative in range(2):
        low = lax.axis_index("gl") ^ relative
        for b in range(batch_count):
            for h in range(high_count):
                parts = []
                for g in range(gx_count):
                    first = (((b * gx_count + g) * high_count + h) * 2 + low) * owned
                    parts.append(tokens_ref[pl.ds(first, owned)])
                joined = jnp.concatenate(parts, axis=0).reshape(block, width)
                at = ((relative * batch_count + b) * high_count + h) * block
                rows_ref[pl.ds(at, block)] = joined

    def emit(weights, start):
        product = jnp.dot(rows_ref[...], weights, preferred_element_type=jnp.float32)
        product = product.astype(jnp.bfloat16)
        window = pl.ds(start, product.shape[1])
        kept_ref[:, window] = product[:half]
        given_ref[:, window] = product[half:]
        for source, target in ((given_ref, given_out), (kept_ref, kept_out)):
            copy = pltpu.make_async_copy(source.at[:, window], target.at[:, window], out_sems.at[len(writes)])
            copy.start()
            writes.append(copy)

    writes = []
    copies[1].wait()
    emit(pair_ref[...], query_cols)
    for copy, (start, size) in zip(copies[2:], chunks):
        copy.wait()
        emit(query_ref[:, pl.ds(start, size)], start)
    for copy in writes:
        copy.wait()


def project(tokens, w_query, w_keyval, dims):
    sequences, steps, width = tokens.shape
    query_cols, pair_cols = w_query.shape[1], w_keyval.shape[1]
    rows = sequences * steps
    chunks, start = [], 0
    while start < query_cols:
        size = min(512 if query_cols - start > 512 else 256, query_cols - start)
        chunks.append((start, size))
        start += size
    hbm = pl.BlockSpec(memory_space=pltpu.HBM)
    shape = jax.ShapeDtypeStruct((rows // 2, query_cols + pair_cols), jnp.bfloat16)
    return pl.pallas_call(
        functools.partial(project_kernel, dims, chunks),
        out_shape=(shape, shape),
        in_specs=[hbm, hbm, hbm],
        out_specs=(hbm, hbm),
        scratch_shapes=[
            pltpu.VMEM(tokens.shape, jnp.bfloat16),
            pltpu.VMEM((rows, width), jnp.bfloat16),
            pltpu.VMEM((width, query_cols), jnp.bfloat16),
            pltpu.VMEM((width, pair_cols), jnp.bfloat16),
            pltpu.VMEM((rows // 2, query_cols + pair_cols), jnp.bfloat16),
            pltpu.VMEM((rows // 2, query_cols + pair_cols), jnp.bfloat16),
            pltpu.SemaphoreType.DMA((2 + len(chunks),)),
            pltpu.SemaphoreType.DMA((2 * (1 + len(chunks)),)),
        ],
        compiler_params=pltpu.CompilerParams(vmem_limit_bytes=62 * 1024 * 1024),
        cost_estimate=pl.CostEstimate(
            flops=2 * rows * width * (query_cols + pair_cols),
            bytes_accessed=2 * width * (query_cols + pair_cols),
            transcendentals=0,
        ),
        name="project",
    )(tokens, w_query, w_keyval)


def near_kernel(after_ref, source_ref, target_ref, token_ref, sem):
    copy = pltpu.make_async_copy(source_ref, target_ref, sem)
    copy.start()
    copy.wait()
    token_ref[...] = jnp.zeros_like(token_ref)


def near(after, array):
    anywhere = pl.BlockSpec(memory_space=pl.ANY)
    return pl.pallas_call(
        near_kernel,
        out_shape=(
            jax.ShapeDtypeStruct(array.shape, array.dtype),
            jax.ShapeDtypeStruct((8, 128), jnp.float32),
        ),
        in_specs=[anywhere, anywhere],
        out_specs=(anywhere, pl.BlockSpec(memory_space=pltpu.VMEM)),
        scratch_shapes=[pltpu.SemaphoreType.DMA],
        compiler_params=pltpu.CompilerParams(vmem_limit_bytes=36 * 1024 * 1024),
        cost_estimate=pl.CostEstimate(
            flops=0, bytes_accessed=2 * array.size * array.dtype.itemsize, transcendentals=0
        ),
        name="near",
    )(after, array)


def staged_kernel(source_ref, target_ref):
    target_ref[...] = source_ref[...]


def staged(array):
    vmem = pl.BlockSpec(memory_space=pltpu.VMEM)
    return pl.pallas_call(
        staged_kernel,
        out_shape=jax.ShapeDtypeStruct(array.shape, array.dtype),
        in_specs=[vmem],
        out_specs=vmem,
        compiler_params=pltpu.CompilerParams(vmem_limit_bytes=8 * 1024 * 1024),
        name="staged",
    )(array)


def combine_kernel(dims, kept_ref, taken_ref, own_ref, *sends):
    batch_count, high_count, block = dims
    for db in range(batch_count):
        for dh in range(high_count):
            at = ((lax.axis_index("batch") ^ db) * high_count + (lax.axis_index("gh") ^ dh)) * block
            window = pl.ds(pl.multiple_of(at, block), block)
            total = kept_ref[window].astype(jnp.float32) + taken_ref[window].astype(jnp.float32)
            target = sends[db * high_count + dh - 1] if db or dh else own_ref
            target[...] = total.astype(target.dtype)


def combine(kept, taken, dims):
    batch_count, high_count, block = dims
    cols = kept.shape[1]
    vmem = pl.BlockSpec(memory_space=pltpu.VMEM)
    count = batch_count * high_count
    return pl.pallas_call(
        functools.partial(combine_kernel, dims),
        out_shape=[jax.ShapeDtypeStruct((block, cols), jnp.float32)]
        + [jax.ShapeDtypeStruct((block, cols), jnp.bfloat16)] * (count - 1),
        in_specs=[vmem, vmem],
        out_specs=[vmem] * count,
        compiler_params=pltpu.CompilerParams(vmem_limit_bytes=8 * 1024 * 1024),
        name="combine",
    )(kept, taken)


def collect_kernel(count, own_ref, after_ref, *refs):
    received, outs, total_ref = refs[: -count - 1], refs[-count - 1 : -1], refs[-1]
    total = own_ref[...]
    for other in received:
        total = total + other[...].astype(jnp.float32)
    rows = outs[0].shape[0]
    for g in range(count):
        total_ref[g] = total[g * rows : (g + 1) * rows]
    for k in range(count):
        outs[k][...] = total_ref[lax.axis_index("gx") ^ k].astype(jnp.bfloat16)


def collect(own, received, after, gx_count):
    block, cols = own.shape
    rows = block // gx_count
    vmem = pl.BlockSpec(memory_space=pltpu.VMEM)
    return pl.pallas_call(
        functools.partial(collect_kernel, gx_count),
        out_shape=[jax.ShapeDtypeStruct((rows, cols), jnp.bfloat16)] * gx_count,
        in_specs=[vmem, pl.BlockSpec(memory_space=pl.ANY)]
        + [vmem] * len(received),
        out_specs=[vmem] * gx_count,
        scratch_shapes=[pltpu.VMEM((gx_count, rows, cols), jnp.float32)],
        compiler_params=pltpu.CompilerParams(vmem_limit_bytes=8 * 1024 * 1024),
        name="collect",
    )(own, after, *received)


def attend_kernel(dims, lengths_ref, cos_ref, sin_ref, keys_ref, values_ref, *refs):
    gx_count, owned, steps, heads, width = dims
    blocks, outs = [None] * gx_count, refs[gx_count:-2]
    for k, ref in zip(farther_first(gx_count), refs):
        blocks[k] = ref
    rows_ref, result_ref = refs[-2:]
    query_cols = heads * width
    half = width // 2
    scaling = 1.0 / width**0.5
    slots = keys_ref.shape[1]
    count = gx_count * heads * steps
    cosine = jnp.concatenate([cos_ref[s] for s in range(owned)], axis=0)
    sine = jnp.concatenate([sin_ref[s] for s in range(owned)], axis=0)

    def turn(first, second):
        return first * cosine - second * sine, second * cosine + first * sine

    key_value = [ref[:, pl.ds(query_cols, ref.shape[1] - query_cols)].astype(jnp.float32) for ref in blocks]
    key_value = jnp.concatenate(unxored(key_value, lax.axis_index("gx")), axis=1)
    new_values = key_value[:, width:]
    new_keys = turn(key_value[:, :half], key_value[:, half:width])
    new_keys = jnp.concatenate(new_keys, axis=1).astype(jnp.bfloat16).astype(jnp.float32)
    for k in range(gx_count):
        for h in range(heads):
            first = blocks[k][:, pl.ds(h * width, half)].astype(jnp.float32)
            second = blocks[k][:, pl.ds(h * width + half, half)].astype(jnp.float32)
            for part, value in enumerate(turn(first, second)):
                for s in range(owned):
                    window = pl.ds((k * heads + h) * steps, steps)
                    rows_ref[s, window, pl.ds(part * half, half)] = value[s * steps : (s + 1) * steps]
    step_of = lax.broadcasted_iota(jnp.int32, (count, 1), 0) % steps
    slot_of = lax.broadcasted_iota(jnp.int32, (1, slots), 1)
    for s in range(owned):
        queries = rows_ref[s].astype(jnp.bfloat16)
        cached = lax.dot_general(
            queries, keys_ref[s], (((1,), (1,)), ((), ())), preferred_element_type=jnp.float32
        )
        cached = jnp.where(slot_of < lengths_ref[s], cached * scaling, -1e30)
        highest = cached.max(-1, keepdims=True)
        wide = queries.astype(jnp.float32)
        fresh = []
        for u in range(steps):
            row = s * steps + u
            score = (wide * new_keys[row : row + 1]).sum(-1, keepdims=True) * scaling
            fresh.append(jnp.where(step_of >= u, score, -1e30))
            highest = jnp.maximum(highest, fresh[-1])
        exp_cached = jnp.exp(cached - highest)
        denom = exp_cached.sum(-1, keepdims=True)
        total = jnp.dot(
            exp_cached.astype(jnp.bfloat16), values_ref[s], preferred_element_type=jnp.float32
        )
        for u in range(steps):
            row = s * steps + u
            exp_fresh = jnp.exp(fresh[u] - highest)
            denom = denom + exp_fresh
            total = total + exp_fresh * new_values[row : row + 1]
        result_ref[s] = total / denom
    for k in range(gx_count):
        for h in range(heads):
            window = pl.ds((k * heads + h) * steps, steps)
            value = jnp.concatenate([result_ref[s, window] for s in range(owned)], axis=0)
            outs[k][:, pl.ds(h * width, width)] = value.astype(jnp.bfloat16)


def attend(blocks, cache_keys, cache_values, lengths, query_cols):
    gx_count = len(blocks)
    owned, slots, width = cache_keys.shape
    rows = blocks[0].shape[0]
    steps = rows // owned
    heads = query_cols // width
    count = gx_count * heads * steps
    freqs = 10000.0 ** (-(jnp.arange(width // 2, dtype=jnp.float32) * 2.0 / width))
    positions = lengths[:, None, None] + jnp.arange(steps, dtype=jnp.int32)[None, :, None]
    angles = positions.astype(jnp.float32) * freqs
    vmem = pl.BlockSpec(memory_space=pltpu.VMEM)
    smem = pl.BlockSpec(memory_space=pltpu.SMEM)
    return pl.pallas_call(
        functools.partial(attend_kernel, (gx_count, owned, steps, heads, width)),
        out_shape=[jax.ShapeDtypeStruct((rows, query_cols), jnp.bfloat16)] * gx_count,
        in_specs=[smem] + [vmem] * (4 + gx_count),
        out_specs=[vmem] * gx_count,
        scratch_shapes=[
            pltpu.VMEM((owned, count, width), jnp.float32),
            pltpu.VMEM((owned, count, width), jnp.float32),
        ],
        compiler_params=pltpu.CompilerParams(vmem_limit_bytes=12 * 1024 * 1024),
        cost_estimate=pl.CostEstimate(
            flops=4 * owned * count * slots * width,
            bytes_accessed=4 * owned * slots * width,
            transcendentals=owned * count * slots,
        ),
        name="attend",
    )(lengths, jnp.cos(angles), jnp.sin(angles), cache_keys, cache_values, *[blocks[k] for k in farther_first(gx_count)])


def order_kernel(*refs):
    blocks, (out_ref, sorted_ref) = refs[:-2], refs[-2:]
    for k, block in enumerate(blocks):
        sorted_ref[lax.axis_index("gx") ^ k] = block[...].astype(jnp.float32)
    parts = [sorted_ref[g] for g in range(len(blocks))]
    out_ref[...] = jnp.concatenate(parts, axis=0).astype(out_ref.dtype)


def order(blocks):
    vmem = pl.BlockSpec(memory_space=pltpu.VMEM)
    rows, cols = blocks[0].shape
    count = len(blocks)
    turn = lambda *refs: order_kernel(refs[0], *refs[count - 1 : 0 : -1], *refs[count:])
    return pl.pallas_call(
        turn,
        out_shape=jax.ShapeDtypeStruct((count * rows, cols), blocks[0].dtype),
        in_specs=[vmem] * count,
        out_specs=vmem,
        scratch_shapes=[pltpu.VMEM((count, rows, cols), jnp.float32)],
        compiler_params=pltpu.CompilerParams(vmem_limit_bytes=8 * 1024 * 1024),
        name="order",
    )(blocks[0], *blocks[:0:-1])


def mix_kernel(dims, chunk, weight_ref, *refs):
    batch_count, gx_count, high_count, block = dims
    count = 2 * batch_count * high_count
    blocks, own_ref, sends, (rows_ref, sum_ref) = refs[:count], refs[count], refs[count + 1 : -2], refs[-2:]
    shards = gx_count // batch_count
    group = block // shards
    for relative in range(2):
        for db in range(batch_count):
            for dh in range(high_count):
                b, h = lax.axis_index("batch") ^ db, lax.axis_index("gh") ^ dh
                at = ((relative * batch_count + b) * high_count + h) * block
                source = blocks[(relative * batch_count + db) * high_count + dh]
                rows_ref[pl.ds(pl.multiple_of(at, block), block)] = source[...]
    lhs = rows_ref[...]
    out_cols = weight_ref.shape[1]
    for start in range(0, out_cols, chunk):
        size = min(chunk, out_cols - start)
        window = pl.ds(start, size)
        sum_ref[:, pl.ds(0, size)] = jnp.dot(
            lhs, weight_ref[:, window], preferred_element_type=jnp.float32
        )
        for k in range(gx_count):
            shard = lax.axis_index("gx") ^ k
            b, hi = shard // shards, shard % shards
            parts = []
            for relative in range(2):
                for h in range(high_count):
                    at = ((relative * batch_count + b) * high_count + h) * block + hi * group
                    at = pl.multiple_of(at, group)
                    parts.append(sum_ref[pl.ds(at, group), pl.ds(0, size)])
            piece = jnp.concatenate(parts, axis=0)
            target = own_ref if k == 0 else sends[k - 1]
            target[:, window] = piece.astype(target.dtype)


def mix(blocks, w_out, dims):
    batch_count, gx_count, high_count, block = dims
    depth, out_cols = w_out.shape
    rows = len(blocks) * block
    chunk = min(768, out_cols)
    vmem = pl.BlockSpec(memory_space=pltpu.VMEM)
    shapes = [jax.ShapeDtypeStruct((rows // gx_count, out_cols), jnp.float32)]
    shapes += [jax.ShapeDtypeStruct((rows // gx_count, out_cols), jnp.bfloat16)] * (gx_count - 1)
    return pl.pallas_call(
        functools.partial(mix_kernel, dims, chunk),
        out_shape=shapes,
        in_specs=[vmem] * (1 + len(blocks)),
        out_specs=[vmem] * gx_count,
        scratch_shapes=[pltpu.VMEM((rows, depth), jnp.bfloat16), pltpu.VMEM((rows, chunk), jnp.float32)],
        compiler_params=pltpu.CompilerParams(vmem_limit_bytes=20 * 1024 * 1024),
        cost_estimate=pl.CostEstimate(
            flops=2 * rows * depth * out_cols, bytes_accessed=2 * depth * out_cols, transcendentals=0
        ),
        name="mix",
    )(w_out, *blocks)


def finish_kernel(dims, own_ref, *refs):
    received, out_ref = refs[:-1], refs[-1]
    batch_count, high_count, owned = dims
    steps, out_cols = out_ref.shape[1:]
    size = batch_count * owned * steps
    for relative in range(2):
        low = lax.axis_index("gl") ^ relative
        for h in range(high_count):
            window = pl.ds((relative * high_count + h) * size, size)
            total = own_ref[window]
            for other in received:
                total = total + other[window].astype(jnp.float32)
            total = total.reshape(batch_count, owned, steps, out_cols).astype(jnp.bfloat16)
            for g in range(batch_count):
                first = ((g * high_count + h) * 2 + low) * owned
                out_ref[pl.ds(first, owned)] = total[g]


def finish(own, received, dims, steps):
    rows, out_cols = own.shape
    vmem = pl.BlockSpec(memory_space=pltpu.VMEM)
    return pl.pallas_call(
        functools.partial(finish_kernel, dims),
        out_shape=jax.ShapeDtypeStruct((rows // steps, steps, out_cols), jnp.bfloat16),
        in_specs=[vmem] * (1 + len(received)),
        out_specs=vmem,
        compiler_params=pltpu.CompilerParams(vmem_limit_bytes=16 * 1024 * 1024),
        name="finish",
    )(own, *received)


def local(tokens, w_query, w_keyval, w_out, cache_keys, cache_values, lengths):
    batch_count = lax.axis_size("batch")
    gx_count = lax.axis_size("gx")
    high_count = lax.axis_size("gh")
    sizes = (batch_count, high_count, 2)
    owned = cache_keys.shape[0]
    sequences, steps, width = tokens.shape
    query_cols = w_query.shape[1]
    rows = owned * steps
    rows_here = gx_count * rows

    kept, given = project(tokens, w_query, w_keyval, (batch_count, gx_count, high_count, owned))
    taken = swapped_with(given, PLANE, sizes, (0, 0, 1))
    far = [(db, dh) for db in range(batch_count) for dh in range(high_count)][1:]
    own, *sends = combine(staged(kept), taken, (batch_count, high_count, rows_here))
    received = [
        swapped_with(block, PLANE, sizes, (db, dh, 0)) for block, (db, dh) in zip(sends, far)
    ]
    w_out, token = near(own, w_out)
    blocks = collect(own, received, token, gx_count)
    blocks = [blocks[0]] + [
        swapped_with(blocks[k], "gx", (gx_count,), (k,)) for k in range(1, gx_count)
    ]
    blocks = attend(blocks, cache_keys, cache_values, lengths, query_cols)
    blocks = [blocks[0]] + [
        swapped_with(blocks[k], "gx", (gx_count,), (k,)) for k in range(1, gx_count)
    ]
    grouped = order(blocks)

    ours = [grouped] + [swapped_with(grouped, PLANE, sizes, (db, dh, 0)) for db, dh in far]
    theirs = [swapped_with(block, PLANE, sizes, (0, 0, 1)) for block in ours]
    own, *sends = mix(ours + theirs, w_out, (batch_count, gx_count, high_count, rows_here))
    received = [
        swapped_with(sends[k - 1], "gx", (gx_count,), (k,)) for k in reversed(range(1, gx_count))
    ]
    return finish(own, received, (batch_count, high_count, owned), steps)


def solution(mesh):
    batch_count, gx_count, gy_count = mesh.devices.shape
    split = Mesh(
        mesh.devices.reshape(batch_count, gx_count, gy_count // 2, 2), ("batch", "gx", "gh", "gl")
    )
    plane = ("batch", "gh", "gl")
    placed = (
        P(None, None, plane),
        P(plane, "gx"),
        P(plane, "gx"),
        P("gx", plane),
        P(("batch", "gx", "gh", "gl"), None, None),
        P(("batch", "gx", "gh", "gl"), None, None),
        P(("batch", "gx", "gh", "gl")),
    )
    return jax.shard_map(
        local, mesh=split, in_specs=placed, out_specs=P("gx", None, plane), check_vma=False
    )
```

```python
import functools

import jax
import jax.numpy as jnp
import numpy as np
from jax import lax
from jax.experimental import pallas as pl
from jax.experimental.pallas import tpu as pltpu
from jax.sharding import Mesh
from jax.sharding import PartitionSpec as P

PLANE = ("batch", "gh", "gl")


def swapped_with(value, axes, sizes, differs):
    pairs = []
    for place in np.ndindex(*sizes):
        target = tuple(p ^ d for p, d in zip(place, differs))
        pairs.append((int(np.ravel_multi_index(place, sizes)), int(np.ravel_multi_index(target, sizes))))
    return lax.ppermute(value, axes, pairs)


def unxored(blocks, here):
    count = len(blocks)
    bit = 1
    while bit < count:
        turn = (here & bit) != 0
        blocks = [jnp.where(turn, blocks[k ^ bit], blocks[k]) for k in range(count)]
        bit *= 2
    return blocks


def farther_first(count):
    return [0, *range(2, count), 1]


def project_kernel(
    dims, chunks, tokens_hbm, query_hbm, pair_hbm, kept_out, given_out, tokens_ref, rows_ref, query_ref, pair_ref, kept_ref, given_ref, sems, out_sems
):
    batch_count, gx_count, high_count, owned = dims
    query_cols = query_ref.shape[1]
    copies = [
        pltpu.make_async_copy(tokens_hbm, tokens_ref, sems.at[0]),
        pltpu.make_async_copy(pair_hbm, pair_ref, sems.at[1]),
    ]
    for place, (start, size) in enumerate(chunks):
        window = pl.ds(start, size)
        copies.append(
            pltpu.make_async_copy(query_hbm.at[:, window], query_ref.at[:, window], sems.at[place + 2])
        )
    ahead = 2
    for copy in copies[: 2 + ahead]:
        copy.start()
    steps, width = tokens_ref.shape[1:]
    block = gx_count * owned * steps
    half = rows_ref.shape[0] // 2
    copies[0].wait()
    for relative in range(2):
        low = lax.axis_index("gl") ^ relative
        for b in range(batch_count):
            for h in range(high_count):
                parts = []
                for g in range(gx_count):
                    first = (((b * gx_count + g) * high_count + h) * 2 + low) * owned
                    parts.append(tokens_ref[pl.ds(first, owned)])
                joined = jnp.concatenate(parts, axis=0).reshape(block, width)
                at = ((relative * batch_count + b) * high_count + h) * block
                rows_ref[pl.ds(at, block)] = joined

    def emit(weights, start):
        product = jnp.dot(rows_ref[...], weights, preferred_element_type=jnp.float32)
        product = product.astype(jnp.bfloat16)
        window = pl.ds(start, product.shape[1])
        kept_ref[:, window] = product[:half]
        given_ref[:, window] = product[half:]
        for source, target in ((given_ref, given_out), (kept_ref, kept_out)):
            copy = pltpu.make_async_copy(source.at[:, window], target.at[:, window], out_sems.at[len(writes)])
            copy.start()
            writes.append(copy)

    writes = []
    copies[1].wait()
    emit(pair_ref[...], query_cols)
    for place, (start, size) in enumerate(chunks):
        copies[2 + place].wait()
        if place + ahead < len(chunks):
            copies[2 + place + ahead].start()
        emit(query_ref[:, pl.ds(start, size)], start)
    for copy in writes:
        copy.wait()


def project(tokens, w_query, w_keyval, dims):
    sequences, steps, width = tokens.shape
    query_cols, pair_cols = w_query.shape[1], w_keyval.shape[1]
    rows = sequences * steps
    chunks, start = [], 0
    while start < query_cols:
        size = min(512 if query_cols - start > 512 else 256, query_cols - start)
        chunks.append((start, size))
        start += size
    hbm = pl.BlockSpec(memory_space=pltpu.HBM)
    shape = jax.ShapeDtypeStruct((rows // 2, query_cols + pair_cols), jnp.bfloat16)
    return pl.pallas_call(
        functools.partial(project_kernel, dims, chunks),
        out_shape=(shape, shape),
        in_specs=[hbm, hbm, hbm],
        out_specs=(hbm, hbm),
        scratch_shapes=[
            pltpu.VMEM(tokens.shape, jnp.bfloat16),
            pltpu.VMEM((rows, width), jnp.bfloat16),
            pltpu.VMEM((width, query_cols), jnp.bfloat16),
            pltpu.VMEM((width, pair_cols), jnp.bfloat16),
            pltpu.VMEM((rows // 2, query_cols + pair_cols), jnp.bfloat16),
            pltpu.VMEM((rows // 2, query_cols + pair_cols), jnp.bfloat16),
            pltpu.SemaphoreType.DMA((2 + len(chunks),)),
            pltpu.SemaphoreType.DMA((2 * (1 + len(chunks)),)),
        ],
        compiler_params=pltpu.CompilerParams(vmem_limit_bytes=62 * 1024 * 1024),
        cost_estimate=pl.CostEstimate(
            flops=2 * rows * width * (query_cols + pair_cols),
            bytes_accessed=2 * width * (query_cols + pair_cols),
            transcendentals=0,
        ),
        name="project",
    )(tokens, w_query, w_keyval)


def near_kernel(after_ref, source_ref, target_ref, token_ref, sem):
    copy = pltpu.make_async_copy(source_ref, target_ref, sem)
    copy.start()
    copy.wait()
    token_ref[...] = jnp.zeros_like(token_ref)


def near(after, array):
    anywhere = pl.BlockSpec(memory_space=pl.ANY)
    return pl.pallas_call(
        near_kernel,
        out_shape=(
            jax.ShapeDtypeStruct(array.shape, array.dtype),
            jax.ShapeDtypeStruct((8, 128), jnp.float32),
        ),
        in_specs=[anywhere, anywhere],
        out_specs=(anywhere, pl.BlockSpec(memory_space=pltpu.VMEM)),
        scratch_shapes=[pltpu.SemaphoreType.DMA],
        compiler_params=pltpu.CompilerParams(vmem_limit_bytes=36 * 1024 * 1024),
        cost_estimate=pl.CostEstimate(
            flops=0, bytes_accessed=2 * array.size * array.dtype.itemsize, transcendentals=0
        ),
        name="near",
    )(after, array)


def staged_kernel(source_ref, target_ref):
    target_ref[...] = source_ref[...]


def staged(array):
    vmem = pl.BlockSpec(memory_space=pltpu.VMEM)
    return pl.pallas_call(
        staged_kernel,
        out_shape=jax.ShapeDtypeStruct(array.shape, array.dtype),
        in_specs=[vmem],
        out_specs=vmem,
        compiler_params=pltpu.CompilerParams(vmem_limit_bytes=8 * 1024 * 1024),
        name="staged",
    )(array)


def combine_kernel(dims, kept_ref, taken_ref, own_ref, *sends):
    batch_count, high_count, block = dims
    for db in range(batch_count):
        for dh in range(high_count):
            at = ((lax.axis_index("batch") ^ db) * high_count + (lax.axis_index("gh") ^ dh)) * block
            window = pl.ds(pl.multiple_of(at, block), block)
            total = kept_ref[window].astype(jnp.float32) + taken_ref[window].astype(jnp.float32)
            target = sends[db * high_count + dh - 1] if db or dh else own_ref
            target[...] = total.astype(target.dtype)


def combine(kept, taken, dims):
    batch_count, high_count, block = dims
    cols = kept.shape[1]
    vmem = pl.BlockSpec(memory_space=pltpu.VMEM)
    count = batch_count * high_count
    return pl.pallas_call(
        functools.partial(combine_kernel, dims),
        out_shape=[jax.ShapeDtypeStruct((block, cols), jnp.float32)]
        + [jax.ShapeDtypeStruct((block, cols), jnp.bfloat16)] * (count - 1),
        in_specs=[vmem, vmem],
        out_specs=[vmem] * count,
        compiler_params=pltpu.CompilerParams(vmem_limit_bytes=8 * 1024 * 1024),
        name="combine",
    )(kept, taken)


def collect_kernel(count, own_ref, after_ref, *refs):
    received, outs, total_ref = refs[: -count - 1], refs[-count - 1 : -1], refs[-1]
    total = own_ref[...]
    for other in received:
        total = total + other[...].astype(jnp.float32)
    rows = outs[0].shape[0]
    for g in range(count):
        total_ref[g] = total[g * rows : (g + 1) * rows]
    for k in range(count):
        outs[k][...] = total_ref[lax.axis_index("gx") ^ k].astype(jnp.bfloat16)


def collect(own, received, after, gx_count):
    block, cols = own.shape
    rows = block // gx_count
    vmem = pl.BlockSpec(memory_space=pltpu.VMEM)
    return pl.pallas_call(
        functools.partial(collect_kernel, gx_count),
        out_shape=[jax.ShapeDtypeStruct((rows, cols), jnp.bfloat16)] * gx_count,
        in_specs=[vmem, pl.BlockSpec(memory_space=pl.ANY)]
        + [vmem] * len(received),
        out_specs=[vmem] * gx_count,
        scratch_shapes=[pltpu.VMEM((gx_count, rows, cols), jnp.float32)],
        compiler_params=pltpu.CompilerParams(vmem_limit_bytes=8 * 1024 * 1024),
        name="collect",
    )(own, after, *received)


def attend_kernel(dims, lengths_ref, cos_ref, sin_ref, keys_ref, values_ref, *refs):
    gx_count, owned, steps, heads, width = dims
    blocks, outs = [None] * gx_count, refs[gx_count:-2]
    for k, ref in zip(farther_first(gx_count), refs):
        blocks[k] = ref
    rows_ref, result_ref = refs[-2:]
    query_cols = heads * width
    half = width // 2
    scaling = 1.0 / width**0.5
    slots = keys_ref.shape[1]
    count = gx_count * heads * steps
    cosine = jnp.concatenate([cos_ref[s] for s in range(owned)], axis=0)
    sine = jnp.concatenate([sin_ref[s] for s in range(owned)], axis=0)

    def turn(first, second):
        return first * cosine - second * sine, second * cosine + first * sine

    key_value = [ref[:, pl.ds(query_cols, ref.shape[1] - query_cols)].astype(jnp.float32) for ref in blocks]
    key_value = jnp.concatenate(unxored(key_value, lax.axis_index("gx")), axis=1)
    new_values = key_value[:, width:]
    new_keys = turn(key_value[:, :half], key_value[:, half:width])
    new_keys = jnp.concatenate(new_keys, axis=1).astype(jnp.bfloat16).astype(jnp.float32)
    for k in range(gx_count):
        for h in range(heads):
            first = blocks[k][:, pl.ds(h * width, half)].astype(jnp.float32)
            second = blocks[k][:, pl.ds(h * width + half, half)].astype(jnp.float32)
            for part, value in enumerate(turn(first, second)):
                for s in range(owned):
                    window = pl.ds((k * heads + h) * steps, steps)
                    rows_ref[s, window, pl.ds(part * half, half)] = value[s * steps : (s + 1) * steps]
    step_of = lax.broadcasted_iota(jnp.int32, (count, 1), 0) % steps
    slot_of = lax.broadcasted_iota(jnp.int32, (1, slots), 1)
    for s in range(owned):
        queries = rows_ref[s].astype(jnp.bfloat16)
        cached = lax.dot_general(
            queries, keys_ref[s], (((1,), (1,)), ((), ())), preferred_element_type=jnp.float32
        )
        cached = jnp.where(slot_of < lengths_ref[s], cached * scaling, -1e30)
        highest = cached.max(-1, keepdims=True)
        wide = queries.astype(jnp.float32)
        fresh = []
        for u in range(steps):
            row = s * steps + u
            score = (wide * new_keys[row : row + 1]).sum(-1, keepdims=True) * scaling
            fresh.append(jnp.where(step_of >= u, score, -1e30))
            highest = jnp.maximum(highest, fresh[-1])
        exp_cached = jnp.exp(cached - highest)
        denom = exp_cached.sum(-1, keepdims=True)
        total = jnp.dot(
            exp_cached.astype(jnp.bfloat16), values_ref[s], preferred_element_type=jnp.float32
        )
        for u in range(steps):
            row = s * steps + u
            exp_fresh = jnp.exp(fresh[u] - highest)
            denom = denom + exp_fresh
            total = total + exp_fresh * new_values[row : row + 1]
        result_ref[s] = total / denom
    for k in range(gx_count):
        for h in range(heads):
            window = pl.ds((k * heads + h) * steps, steps)
            value = jnp.concatenate([result_ref[s, window] for s in range(owned)], axis=0)
            outs[k][:, pl.ds(h * width, width)] = value.astype(jnp.bfloat16)


def attend(blocks, cache_keys, cache_values, lengths, query_cols):
    gx_count = len(blocks)
    owned, slots, width = cache_keys.shape
    rows = blocks[0].shape[0]
    steps = rows // owned
    heads = query_cols // width
    count = gx_count * heads * steps
    freqs = 10000.0 ** (-(jnp.arange(width // 2, dtype=jnp.float32) * 2.0 / width))
    positions = lengths[:, None, None] + jnp.arange(steps, dtype=jnp.int32)[None, :, None]
    angles = positions.astype(jnp.float32) * freqs
    vmem = pl.BlockSpec(memory_space=pltpu.VMEM)
    smem = pl.BlockSpec(memory_space=pltpu.SMEM)
    return pl.pallas_call(
        functools.partial(attend_kernel, (gx_count, owned, steps, heads, width)),
        out_shape=[jax.ShapeDtypeStruct((rows, query_cols), jnp.bfloat16)] * gx_count,
        in_specs=[smem] + [vmem] * (4 + gx_count),
        out_specs=[vmem] * gx_count,
        scratch_shapes=[
            pltpu.VMEM((owned, count, width), jnp.float32),
            pltpu.VMEM((owned, count, width), jnp.float32),
        ],
        compiler_params=pltpu.CompilerParams(vmem_limit_bytes=12 * 1024 * 1024),
        cost_estimate=pl.CostEstimate(
            flops=4 * owned * count * slots * width,
            bytes_accessed=4 * owned * slots * width,
            transcendentals=owned * count * slots,
        ),
        name="attend",
    )(lengths, jnp.cos(angles), jnp.sin(angles), cache_keys, cache_values, *[blocks[k] for k in farther_first(gx_count)])


def order_kernel(*refs):
    blocks, (out_ref, sorted_ref) = refs[:-2], refs[-2:]
    for k, block in enumerate(blocks):
        sorted_ref[lax.axis_index("gx") ^ k] = block[...].astype(jnp.float32)
    parts = [sorted_ref[g] for g in range(len(blocks))]
    out_ref[...] = jnp.concatenate(parts, axis=0).astype(out_ref.dtype)


def order(blocks):
    vmem = pl.BlockSpec(memory_space=pltpu.VMEM)
    rows, cols = blocks[0].shape
    count = len(blocks)
    turn = lambda *refs: order_kernel(refs[0], *refs[count - 1 : 0 : -1], *refs[count:])
    return pl.pallas_call(
        turn,
        out_shape=jax.ShapeDtypeStruct((count * rows, cols), blocks[0].dtype),
        in_specs=[vmem] * count,
        out_specs=vmem,
        scratch_shapes=[pltpu.VMEM((count, rows, cols), jnp.float32)],
        compiler_params=pltpu.CompilerParams(vmem_limit_bytes=8 * 1024 * 1024),
        name="order",
    )(blocks[0], *blocks[:0:-1])


def mix_kernel(dims, chunk, part, weight_ref, *refs):
    batch_count, gx_count, high_count, block = dims
    count = 2 * batch_count * high_count
    blocks, own_ref, sends, (rows_ref, sum_ref) = refs[:count], refs[count], refs[count + 1 : -2], refs[-2:]
    shards = gx_count // batch_count
    group = block // shards
    for relative in range(2):
        for db in range(batch_count):
            for dh in range(high_count):
                b, h = lax.axis_index("batch") ^ db, lax.axis_index("gh") ^ dh
                at = ((relative * batch_count + b) * high_count + h) * block
                source = blocks[(relative * batch_count + db) * high_count + dh]
                rows_ref[pl.ds(pl.multiple_of(at, block), block)] = source[...]
    lhs = rows_ref[...]
    first, out_cols = part
    for start in range(0, out_cols, chunk):
        size = min(chunk, out_cols - start)
        window = pl.ds(start, size)
        sum_ref[:, pl.ds(0, size)] = jnp.dot(
            lhs, weight_ref[:, pl.ds(first + start, size)], preferred_element_type=jnp.float32
        )
        for k in range(gx_count):
            shard = lax.axis_index("gx") ^ k
            b, hi = shard // shards, shard % shards
            parts = []
            for relative in range(2):
                for h in range(high_count):
                    at = ((relative * batch_count + b) * high_count + h) * block + hi * group
                    at = pl.multiple_of(at, group)
                    parts.append(sum_ref[pl.ds(at, group), pl.ds(0, size)])
            piece = jnp.concatenate(parts, axis=0)
            target = own_ref if k == 0 else sends[k - 1]
            target[:, window] = piece.astype(target.dtype)


def mix(blocks, w_out, dims, part):
    batch_count, gx_count, high_count, block = dims
    depth = w_out.shape[0]
    out_cols = part[1]
    rows = len(blocks) * block
    chunk = min(768, out_cols)
    vmem = pl.BlockSpec(memory_space=pltpu.VMEM)
    shapes = [jax.ShapeDtypeStruct((rows // gx_count, out_cols), jnp.float32)]
    shapes += [jax.ShapeDtypeStruct((rows // gx_count, out_cols), jnp.bfloat16)] * (gx_count - 1)
    return pl.pallas_call(
        functools.partial(mix_kernel, dims, chunk, part),
        out_shape=shapes,
        in_specs=[vmem] * (1 + len(blocks)),
        out_specs=[vmem] * gx_count,
        scratch_shapes=[pltpu.VMEM((rows, depth), jnp.bfloat16), pltpu.VMEM((rows, chunk), jnp.float32)],
        compiler_params=pltpu.CompilerParams(vmem_limit_bytes=20 * 1024 * 1024),
        cost_estimate=pl.CostEstimate(
            flops=2 * rows * depth * out_cols, bytes_accessed=2 * depth * out_cols, transcendentals=0
        ),
        name="mix",
    )(w_out, *blocks)


def finish_kernel(dims, own_ref, *refs):
    received, out_ref = refs[: len(refs) - 1], refs[-1]
    batch_count, high_count, owned = dims
    steps, out_cols = out_ref.shape[1:]
    size = batch_count * owned * steps
    received = [ref for ref in received if ref.shape == own_ref.shape]
    for relative in range(2):
        low = lax.axis_index("gl") ^ relative
        for h in range(high_count):
            window = pl.ds((relative * high_count + h) * size, size)
            total = own_ref[window]
            for other in received:
                total = total + other[window].astype(jnp.float32)
            total = total.reshape(batch_count, owned, steps, out_cols).astype(jnp.bfloat16)
            for g in range(batch_count):
                first = ((g * high_count + h) * 2 + low) * owned
                out_ref[pl.ds(first, owned)] = total[g]


def finish(own, received, dims, steps, part, parts, before):
    rows, out_cols = own.shape
    whole = pl.BlockSpec((rows, out_cols), lambda step: (0, 0))
    operands = [own, *received]
    in_specs = [whole] * len(operands)
    aliases = {}
    if before is not None:
        aliases[len(operands)] = 0
        operands.append(before)
        in_specs.append(pl.BlockSpec(memory_space=pl.ANY))
    return pl.pallas_call(
        functools.partial(finish_kernel, dims),
        grid=(1,),
        out_shape=jax.ShapeDtypeStruct((rows // steps, steps, out_cols * parts), jnp.bfloat16),
        in_specs=in_specs,
        out_specs=pl.BlockSpec((rows // steps, steps, out_cols), lambda step: (0, 0, part)),
        input_output_aliases=aliases,
        compiler_params=pltpu.CompilerParams(vmem_limit_bytes=16 * 1024 * 1024),
        name="finish",
    )(*operands)


def local(tokens, w_query, w_keyval, w_out, cache_keys, cache_values, lengths):
    batch_count = lax.axis_size("batch")
    gx_count = lax.axis_size("gx")
    high_count = lax.axis_size("gh")
    sizes = (batch_count, high_count, 2)
    owned = cache_keys.shape[0]
    sequences, steps, width = tokens.shape
    query_cols = w_query.shape[1]
    rows = owned * steps
    rows_here = gx_count * rows

    kept, given = project(tokens, w_query, w_keyval, (batch_count, gx_count, high_count, owned))
    taken = swapped_with(given, PLANE, sizes, (0, 0, 1))
    far = [(db, dh) for db in range(batch_count) for dh in range(high_count)][1:]
    own, *sends = combine(staged(kept), taken, (batch_count, high_count, rows_here))
    received = [
        swapped_with(block, PLANE, sizes, (db, dh, 0)) for block, (db, dh) in zip(sends, far)
    ]
    w_out, token = near(own, w_out)
    blocks = collect(own, received, token, gx_count)
    blocks = [blocks[0]] + [
        swapped_with(blocks[k], "gx", (gx_count,), (k,)) for k in range(1, gx_count)
    ]
    blocks = attend(blocks, cache_keys, cache_values, lengths, query_cols)
    blocks = [blocks[0]] + [
        swapped_with(blocks[k], "gx", (gx_count,), (k,)) for k in range(1, gx_count)
    ]
    grouped = order(blocks)

    ours = [grouped] + [swapped_with(grouped, PLANE, sizes, (db, dh, 0)) for db, dh in far]
    theirs = [swapped_with(block, PLANE, sizes, (0, 0, 1)) for block in ours]
    out_cols = w_out.shape[1]
    parts = 2 if out_cols % 256 == 0 else 1
    size = out_cols // parts
    mixed = None
    products = [
        mix(ours + theirs, w_out, (batch_count, gx_count, high_count, rows_here), (part * size, size))
        for part in range(parts)
    ]
    for part, (own, *sends) in enumerate(products):
        received = [
            swapped_with(sends[k - 1], "gx", (gx_count,), (k,)) for k in farther_first(gx_count)[1:]
        ]
        mixed = finish(own, received, (batch_count, high_count, owned), steps, part, parts, mixed)
    return mixed


def solution(mesh):
    batch_count, gx_count, gy_count = mesh.devices.shape
    split = Mesh(
        mesh.devices.reshape(batch_count, gx_count, gy_count // 2, 2), ("batch", "gx", "gh", "gl")
    )
    plane = ("batch", "gh", "gl")
    placed = (
        P(None, None, plane),
        P(plane, "gx"),
        P(plane, "gx"),
        P("gx", plane),
        P(("batch", "gx", "gh", "gl"), None, None),
        P(("batch", "gx", "gh", "gl"), None, None),
        P(("batch", "gx", "gh", "gl")),
    )
    return jax.shard_map(
        local, mesh=split, in_specs=placed, out_specs=P("gx", None, plane), check_vma=False
    )
```

```python
import functools

import jax
import jax.numpy as jnp
import numpy as np
from jax import lax
from jax.experimental import pallas as pl
from jax.experimental.pallas import tpu as pltpu
from jax.sharding import Mesh
from jax.sharding import PartitionSpec as P

PLANE = ("batch", "gh", "gl")


def swapped_with(value, axes, sizes, differs):
    pairs = []
    for place in np.ndindex(*sizes):
        target = tuple(p ^ d for p, d in zip(place, differs))
        pairs.append((int(np.ravel_multi_index(place, sizes)), int(np.ravel_multi_index(target, sizes))))
    return lax.ppermute(value, axes, pairs)


def unxored(blocks, here):
    count = len(blocks)
    bit = 1
    while bit < count:
        turn = (here & bit) != 0
        blocks = [jnp.where(turn, blocks[k ^ bit], blocks[k]) for k in range(count)]
        bit *= 2
    return blocks


def farther_first(count):
    return [0, *range(2, count), 1]


def project_kernel(
    dims, blocks, chunks, tokens_hbm, query_hbm, pair_hbm, kept_out, given_out,
    tokens_ref, rows_ref, query_ref, pair_ref, kept_ref, given_ref, sum_ref, sems, out_sems,
):
    batch_count, gx_count, high_count, owned = dims
    query_cols = query_ref.shape[1]
    copies = [
        pltpu.make_async_copy(tokens_hbm, tokens_ref, sems.at[0]),
        pltpu.make_async_copy(pair_hbm, pair_ref, sems.at[1]),
    ]
    for place, (start, size) in enumerate(blocks):
        window = pl.ds(start, size)
        copies.append(pltpu.make_async_copy(query_hbm.at[window], query_ref.at[window], sems.at[place + 2]))
    for copy in copies:
        copy.start()
    steps, width = tokens_ref.shape[1:]
    block = gx_count * owned * steps
    half = rows_ref.shape[0] // 2
    copies[0].wait()
    for relative in range(2):
        low = lax.axis_index("gl") ^ relative
        for b in range(batch_count):
            for h in range(high_count):
                parts = []
                for g in range(gx_count):
                    first = (((b * gx_count + g) * high_count + h) * 2 + low) * owned
                    parts.append(tokens_ref[pl.ds(first, owned)])
                joined = jnp.concatenate(parts, axis=0).reshape(block, width)
                at = ((relative * batch_count + b) * high_count + h) * block
                rows_ref[pl.ds(at, block)] = joined
    writes = []

    def emit(product, start):
        product = product.astype(jnp.bfloat16)
        window = pl.ds(start, product.shape[1])
        kept_ref[:, window] = product[:half]
        given_ref[:, window] = product[half:]
        for source, target in ((given_ref, given_out), (kept_ref, kept_out)):
            copy = pltpu.make_async_copy(source.at[:, window], target.at[:, window], out_sems.at[len(writes)])
            copy.start()
            writes.append(copy)

    copies[1].wait()
    emit(jnp.dot(rows_ref[...], pair_ref[...], preferred_element_type=jnp.float32), query_cols)
    for place, (depth_at, depth) in enumerate(blocks):
        copies[2 + place].wait()
        rows = rows_ref[:, pl.ds(depth_at, depth)]
        for start, size in chunks:
            window = pl.ds(start, size)
            term = jnp.dot(
                rows, query_ref[pl.ds(depth_at, depth), window], preferred_element_type=jnp.float32
            )
            if place > 0:
                term = term + sum_ref[:, window]
            if place < len(blocks) - 1:
                sum_ref[:, window] = term
            else:
                emit(term, start)
    for copy in writes:
        copy.wait()


def cut(total, sizes):
    windows, start = [], 0
    while start < total:
        size = min(sizes[min(len(windows), len(sizes) - 1)], total - start)
        windows.append((start, size))
        start += size
    return windows


def project(tokens, w_query, w_keyval, dims):
    sequences, steps, width = tokens.shape
    query_cols, pair_cols = w_query.shape[1], w_keyval.shape[1]
    rows = sequences * steps
    blocks = cut(width, (768, 768, 512, 256))
    chunks = cut(query_cols, (768,))
    hbm = pl.BlockSpec(memory_space=pltpu.HBM)
    shape = jax.ShapeDtypeStruct((rows // 2, query_cols + pair_cols), jnp.bfloat16)
    return pl.pallas_call(
        functools.partial(project_kernel, dims, blocks, chunks),
        out_shape=(shape, shape),
        in_specs=[hbm, hbm, hbm],
        out_specs=(hbm, hbm),
        scratch_shapes=[
            pltpu.VMEM(tokens.shape, jnp.bfloat16),
            pltpu.VMEM((rows, width), jnp.bfloat16),
            pltpu.VMEM((width, query_cols), jnp.bfloat16),
            pltpu.VMEM((width, pair_cols), jnp.bfloat16),
            pltpu.VMEM((rows // 2, query_cols + pair_cols), jnp.bfloat16),
            pltpu.VMEM((rows // 2, query_cols + pair_cols), jnp.bfloat16),
            pltpu.VMEM((rows, query_cols), jnp.float32),
            pltpu.SemaphoreType.DMA((2 + len(blocks),)),
            pltpu.SemaphoreType.DMA((2 * (1 + len(chunks)),)),
        ],
        compiler_params=pltpu.CompilerParams(vmem_limit_bytes=62 * 1024 * 1024),
        cost_estimate=pl.CostEstimate(
            flops=2 * rows * width * (query_cols + pair_cols),
            bytes_accessed=2 * width * (query_cols + pair_cols),
            transcendentals=0,
        ),
        name="project",
    )(tokens, w_query, w_keyval)


def near_kernel(after_ref, source_ref, target_ref, token_ref, sem):
    copy = pltpu.make_async_copy(source_ref, target_ref, sem)
    copy.start()
    copy.wait()
    token_ref[...] = jnp.zeros_like(token_ref)


def near(after, array):
    anywhere = pl.BlockSpec(memory_space=pl.ANY)
    return pl.pallas_call(
        near_kernel,
        out_shape=(
            jax.ShapeDtypeStruct(array.shape, array.dtype),
            jax.ShapeDtypeStruct((8, 128), jnp.float32),
        ),
        in_specs=[anywhere, anywhere],
        out_specs=(anywhere, pl.BlockSpec(memory_space=pltpu.VMEM)),
        scratch_shapes=[pltpu.SemaphoreType.DMA],
        compiler_params=pltpu.CompilerParams(vmem_limit_bytes=36 * 1024 * 1024),
        cost_estimate=pl.CostEstimate(
            flops=0, bytes_accessed=2 * array.size * array.dtype.itemsize, transcendentals=0
        ),
        name="near",
    )(after, array)


def staged_kernel(source_ref, target_ref):
    target_ref[...] = source_ref[...]


def staged(array):
    vmem = pl.BlockSpec(memory_space=pltpu.VMEM)
    return pl.pallas_call(
        staged_kernel,
        out_shape=jax.ShapeDtypeStruct(array.shape, array.dtype),
        in_specs=[vmem],
        out_specs=vmem,
        compiler_params=pltpu.CompilerParams(vmem_limit_bytes=8 * 1024 * 1024),
        name="staged",
    )(array)


def combine_kernel(dims, kept_ref, taken_ref, own_ref, *sends):
    batch_count, high_count, block = dims
    for db in range(batch_count):
        for dh in range(high_count):
            at = ((lax.axis_index("batch") ^ db) * high_count + (lax.axis_index("gh") ^ dh)) * block
            window = pl.ds(pl.multiple_of(at, block), block)
            total = kept_ref[window].astype(jnp.float32) + taken_ref[window].astype(jnp.float32)
            target = sends[db * high_count + dh - 1] if db or dh else own_ref
            target[...] = total.astype(target.dtype)


def combine(kept, taken, dims):
    batch_count, high_count, block = dims
    cols = kept.shape[1]
    vmem = pl.BlockSpec(memory_space=pltpu.VMEM)
    count = batch_count * high_count
    return pl.pallas_call(
        functools.partial(combine_kernel, dims),
        out_shape=[jax.ShapeDtypeStruct((block, cols), jnp.float32)]
        + [jax.ShapeDtypeStruct((block, cols), jnp.bfloat16)] * (count - 1),
        in_specs=[vmem, vmem],
        out_specs=[vmem] * count,
        compiler_params=pltpu.CompilerParams(vmem_limit_bytes=8 * 1024 * 1024),
        name="combine",
    )(kept, taken)


def collect_kernel(count, own_ref, after_ref, *refs):
    received, outs, total_ref = refs[: -count - 1], refs[-count - 1 : -1], refs[-1]
    total = own_ref[...]
    for other in received:
        total = total + other[...].astype(jnp.float32)
    rows = outs[0].shape[0]
    for g in range(count):
        total_ref[g] = total[g * rows : (g + 1) * rows]
    for k in range(count):
        outs[k][...] = total_ref[lax.axis_index("gx") ^ k].astype(jnp.bfloat16)


def collect(own, received, after, gx_count):
    block, cols = own.shape
    rows = block // gx_count
    vmem = pl.BlockSpec(memory_space=pltpu.VMEM)
    return pl.pallas_call(
        functools.partial(collect_kernel, gx_count),
        out_shape=[jax.ShapeDtypeStruct((rows, cols), jnp.bfloat16)] * gx_count,
        in_specs=[vmem, pl.BlockSpec(memory_space=pl.ANY)]
        + [vmem] * len(received),
        out_specs=[vmem] * gx_count,
        scratch_shapes=[pltpu.VMEM((gx_count, rows, cols), jnp.float32)],
        compiler_params=pltpu.CompilerParams(vmem_limit_bytes=8 * 1024 * 1024),
        name="collect",
    )(own, after, *received)


def attend_kernel(dims, groups, lengths_ref, cos_ref, sin_ref, keys_ref, values_ref, after_ref, *refs):
    gx_count, owned, steps, heads, width = dims
    blocks, outs = [None] * gx_count, refs[gx_count:-2]
    for k, ref in zip(farther_first(gx_count), refs):
        blocks[k] = ref
    rows_ref, result_ref = refs[-2:]
    query_cols = heads * width
    half = width // 2
    scaling = 1.0 / width**0.5
    slots = keys_ref.shape[1]
    count = len(groups) * heads * steps
    cosine = jnp.concatenate([cos_ref[s] for s in range(owned)], axis=0)
    sine = jnp.concatenate([sin_ref[s] for s in range(owned)], axis=0)

    def turn(first, second):
        return first * cosine - second * sine, second * cosine + first * sine

    key_value = [ref[:, pl.ds(query_cols, ref.shape[1] - query_cols)].astype(jnp.float32) for ref in blocks]
    key_value = jnp.concatenate(unxored(key_value, lax.axis_index("gx")), axis=1)
    new_values = key_value[:, width:]
    new_keys = turn(key_value[:, :half], key_value[:, half:width])
    new_keys = jnp.concatenate(new_keys, axis=1).astype(jnp.bfloat16).astype(jnp.float32)
    for i, k in enumerate(groups):
        for h in range(heads):
            first = blocks[k][:, pl.ds(h * width, half)].astype(jnp.float32)
            second = blocks[k][:, pl.ds(h * width + half, half)].astype(jnp.float32)
            for part, value in enumerate(turn(first, second)):
                for s in range(owned):
                    window = pl.ds((i * heads + h) * steps, steps)
                    rows_ref[s, window, pl.ds(part * half, half)] = value[s * steps : (s + 1) * steps]
    step_of = lax.broadcasted_iota(jnp.int32, (count, 1), 0) % steps
    slot_of = lax.broadcasted_iota(jnp.int32, (1, slots), 1)
    for s in range(owned):
        queries = rows_ref[s].astype(jnp.bfloat16)
        cached = lax.dot_general(
            queries, keys_ref[s], (((1,), (1,)), ((), ())), preferred_element_type=jnp.float32
        )
        cached = jnp.where(slot_of < lengths_ref[s], cached * scaling, -1e30)
        highest = cached.max(-1, keepdims=True)
        wide = queries.astype(jnp.float32)
        fresh = []
        for u in range(steps):
            row = s * steps + u
            score = (wide * new_keys[row : row + 1]).sum(-1, keepdims=True) * scaling
            fresh.append(jnp.where(step_of >= u, score, -1e30))
            highest = jnp.maximum(highest, fresh[-1])
        exp_cached = jnp.exp(cached - highest)
        denom = exp_cached.sum(-1, keepdims=True)
        total = jnp.dot(
            exp_cached.astype(jnp.bfloat16), values_ref[s], preferred_element_type=jnp.float32
        )
        for u in range(steps):
            row = s * steps + u
            exp_fresh = jnp.exp(fresh[u] - highest)
            denom = denom + exp_fresh
            total = total + exp_fresh * new_values[row : row + 1]
        result_ref[s] = total / denom
    for i in range(len(groups)):
        for h in range(heads):
            window = pl.ds((i * heads + h) * steps, steps)
            value = jnp.concatenate([result_ref[s, window] for s in range(owned)], axis=0)
            outs[i][:, pl.ds(h * width, width)] = value.astype(jnp.bfloat16)


def attend(blocks, groups, cache_keys, cache_values, lengths, after, query_cols):
    gx_count = len(blocks)
    owned, slots, width = cache_keys.shape
    rows = blocks[0].shape[0]
    steps = rows // owned
    heads = query_cols // width
    count = len(groups) * heads * steps
    freqs = 10000.0 ** (-(jnp.arange(width // 2, dtype=jnp.float32) * 2.0 / width))
    positions = lengths[:, None, None] + jnp.arange(steps, dtype=jnp.int32)[None, :, None]
    angles = positions.astype(jnp.float32) * freqs
    vmem = pl.BlockSpec(memory_space=pltpu.VMEM)
    smem = pl.BlockSpec(memory_space=pltpu.SMEM)
    return pl.pallas_call(
        functools.partial(attend_kernel, (gx_count, owned, steps, heads, width), groups),
        out_shape=[jax.ShapeDtypeStruct((rows, query_cols), jnp.bfloat16)] * len(groups),
        in_specs=[smem] + [vmem] * 4 + [pl.BlockSpec(memory_space=pl.ANY)] + [vmem] * gx_count,
        out_specs=[vmem] * len(groups),
        scratch_shapes=[
            pltpu.VMEM((owned, count, width), jnp.float32),
            pltpu.VMEM((owned, count, width), jnp.float32),
        ],
        compiler_params=pltpu.CompilerParams(vmem_limit_bytes=12 * 1024 * 1024),
        cost_estimate=pl.CostEstimate(
            flops=4 * owned * count * slots * width,
            bytes_accessed=4 * owned * slots * width,
            transcendentals=owned * count * slots,
        ),
        name="attend",
    )(lengths, jnp.cos(angles), jnp.sin(angles), cache_keys, cache_values, after, *[blocks[k] for k in farther_first(gx_count)])


def order_kernel(*refs):
    blocks, (out_ref, sorted_ref) = refs[:-2], refs[-2:]
    for k, block in enumerate(blocks):
        sorted_ref[lax.axis_index("gx") ^ k] = block[...].astype(jnp.float32)
    parts = [sorted_ref[g] for g in range(len(blocks))]
    out_ref[...] = jnp.concatenate(parts, axis=0).astype(out_ref.dtype)


def order(blocks):
    vmem = pl.BlockSpec(memory_space=pltpu.VMEM)
    rows, cols = blocks[0].shape
    count = len(blocks)
    turn = lambda *refs: order_kernel(refs[0], *refs[count - 1 : 0 : -1], *refs[count:])
    return pl.pallas_call(
        turn,
        out_shape=jax.ShapeDtypeStruct((count * rows, cols), blocks[0].dtype),
        in_specs=[vmem] * count,
        out_specs=vmem,
        scratch_shapes=[pltpu.VMEM((count, rows, cols), jnp.float32)],
        compiler_params=pltpu.CompilerParams(vmem_limit_bytes=8 * 1024 * 1024),
        name="order",
    )(blocks[0], *blocks[:0:-1])


def mix_kernel(dims, chunk, weight_ref, *refs):
    batch_count, gx_count, high_count, block = dims
    count = 2 * batch_count * high_count
    blocks, own_ref, sends, (rows_ref, sum_ref) = refs[:count], refs[count], refs[count + 1 : -2], refs[-2:]
    shards = gx_count // batch_count
    group = block // shards
    for relative in range(2):
        for db in range(batch_count):
            for dh in range(high_count):
                b, h = lax.axis_index("batch") ^ db, lax.axis_index("gh") ^ dh
                at = ((relative * batch_count + b) * high_count + h) * block
                source = blocks[(relative * batch_count + db) * high_count + dh]
                rows_ref[pl.ds(pl.multiple_of(at, block), block)] = source[...]
    lhs = rows_ref[...]
    out_cols = weight_ref.shape[1]
    for start in range(0, out_cols, chunk):
        size = min(chunk, out_cols - start)
        window = pl.ds(start, size)
        sum_ref[:, pl.ds(0, size)] = jnp.dot(
            lhs, weight_ref[:, window], preferred_element_type=jnp.float32
        )
        for k in range(gx_count):
            shard = lax.axis_index("gx") ^ k
            b, hi = shard // shards, shard % shards
            parts = []
            for relative in range(2):
                for h in range(high_count):
                    at = ((relative * batch_count + b) * high_count + h) * block + hi * group
                    at = pl.multiple_of(at, group)
                    parts.append(sum_ref[pl.ds(at, group), pl.ds(0, size)])
            piece = jnp.concatenate(parts, axis=0)
            target = own_ref if k == 0 else sends[k - 1]
            target[:, window] = piece.astype(target.dtype)


def mix(blocks, w_out, dims):
    batch_count, gx_count, high_count, block = dims
    depth, out_cols = w_out.shape
    rows = len(blocks) * block
    chunk = min(768, out_cols)
    vmem = pl.BlockSpec(memory_space=pltpu.VMEM)
    shapes = [jax.ShapeDtypeStruct((rows // gx_count, out_cols), jnp.float32)]
    shapes += [jax.ShapeDtypeStruct((rows // gx_count, out_cols), jnp.bfloat16)] * (gx_count - 1)
    return pl.pallas_call(
        functools.partial(mix_kernel, dims, chunk),
        out_shape=shapes,
        in_specs=[vmem] * (1 + len(blocks)),
        out_specs=[vmem] * gx_count,
        scratch_shapes=[pltpu.VMEM((rows, depth), jnp.bfloat16), pltpu.VMEM((rows, chunk), jnp.float32)],
        compiler_params=pltpu.CompilerParams(vmem_limit_bytes=20 * 1024 * 1024),
        cost_estimate=pl.CostEstimate(
            flops=2 * rows * depth * out_cols, bytes_accessed=2 * depth * out_cols, transcendentals=0
        ),
        name="mix",
    )(w_out, *blocks)


def finish_kernel(dims, own_ref, *refs):
    received, out_ref = refs[:-1], refs[-1]
    batch_count, high_count, owned = dims
    steps, out_cols = out_ref.shape[1:]
    size = batch_count * owned * steps
    for relative in range(2):
        low = lax.axis_index("gl") ^ relative
        for h in range(high_count):
            window = pl.ds((relative * high_count + h) * size, size)
            total = own_ref[window]
            for other in received:
                total = total + other[window].astype(jnp.float32)
            total = total.reshape(batch_count, owned, steps, out_cols).astype(jnp.bfloat16)
            for g in range(batch_count):
                first = ((g * high_count + h) * 2 + low) * owned
                out_ref[pl.ds(first, owned)] = total[g]


def finish(own, received, dims, steps):
    rows, out_cols = own.shape
    vmem = pl.BlockSpec(memory_space=pltpu.VMEM)
    return pl.pallas_call(
        functools.partial(finish_kernel, dims),
        out_shape=jax.ShapeDtypeStruct((rows // steps, steps, out_cols), jnp.bfloat16),
        in_specs=[vmem] * (1 + len(received)),
        out_specs=vmem,
        compiler_params=pltpu.CompilerParams(vmem_limit_bytes=16 * 1024 * 1024),
        name="finish",
    )(own, *received)


def local(tokens, w_query, w_keyval, w_out, cache_keys, cache_values, lengths):
    batch_count = lax.axis_size("batch")
    gx_count = lax.axis_size("gx")
    high_count = lax.axis_size("gh")
    sizes = (batch_count, high_count, 2)
    owned = cache_keys.shape[0]
    sequences, steps, width = tokens.shape
    query_cols = w_query.shape[1]
    rows = owned * steps
    rows_here = gx_count * rows

    kept, given = project(tokens, w_query, w_keyval, (batch_count, gx_count, high_count, owned))
    taken = swapped_with(given, PLANE, sizes, (0, 0, 1))
    far = [(db, dh) for db in range(batch_count) for dh in range(high_count)][1:]
    own, *sends = combine(staged(kept), taken, (batch_count, high_count, rows_here))
    received = [
        swapped_with(block, PLANE, sizes, (db, dh, 0)) for block, (db, dh) in zip(sends, far)
    ]
    w_out, token = near(own, w_out)
    blocks = collect(own, received, token, gx_count)
    blocks = [blocks[0]] + [
        swapped_with(blocks[k], "gx", (gx_count,), (k,)) for k in range(1, gx_count)
    ]
    distances = list(range(1, gx_count))
    others = attend(blocks, distances, cache_keys, cache_values, lengths, token, query_cols)
    own_heads = attend(blocks, [0], cache_keys, cache_values, lengths, others[0], query_cols)
    blocks = [*own_heads, *others]
    blocks = [blocks[0]] + [
        swapped_with(blocks[k], "gx", (gx_count,), (k,)) for k in range(1, gx_count)
    ]
    grouped = order(blocks)

    ours = [grouped] + [swapped_with(grouped, PLANE, sizes, (db, dh, 0)) for db, dh in far]
    theirs = [swapped_with(block, PLANE, sizes, (0, 0, 1)) for block in ours]
    own, *sends = mix(ours + theirs, w_out, (batch_count, gx_count, high_count, rows_here))
    received = [
        swapped_with(sends[k - 1], "gx", (gx_count,), (k,)) for k in farther_first(gx_count)[1:]
    ]
    return finish(own, received, (batch_count, high_count, owned), steps)


def solution(mesh):
    batch_count, gx_count, gy_count = mesh.devices.shape
    split = Mesh(
        mesh.devices.reshape(batch_count, gx_count, gy_count // 2, 2), ("batch", "gx", "gh", "gl")
    )
    plane = ("batch", "gh", "gl")
    placed = (
        P(None, None, plane),
        P(plane, "gx"),
        P(plane, "gx"),
        P("gx", plane),
        P(("batch", "gx", "gh", "gl"), None, None),
        P(("batch", "gx", "gh", "gl"), None, None),
        P(("batch", "gx", "gh", "gl")),
    )
    return jax.shard_map(
        local, mesh=split, in_specs=placed, out_specs=P("gx", None, plane), check_vma=False
    )
```

```python
import functools

import jax
import jax.numpy as jnp
import numpy as np
from jax import lax
from jax.experimental import pallas as pl
from jax.experimental.pallas import tpu as pltpu
from jax.sharding import Mesh
from jax.sharding import PartitionSpec as P

PLANE = ("batch", "gh", "gl")


def swapped_with(value, axes, sizes, differs):
    pairs = []
    for place in np.ndindex(*sizes):
        target = tuple(p ^ d for p, d in zip(place, differs))
        pairs.append((int(np.ravel_multi_index(place, sizes)), int(np.ravel_multi_index(target, sizes))))
    return lax.ppermute(value, axes, pairs)


def unxored(blocks, here):
    count = len(blocks)
    bit = 1
    while bit < count:
        turn = (here & bit) != 0
        blocks = [jnp.where(turn, blocks[k ^ bit], blocks[k]) for k in range(count)]
        bit *= 2
    return blocks


def farther_first(count):
    return [0, *range(2, count), 1]


def project_kernel(
    dims, blocks, chunks, tokens_hbm, query_hbm, pair_hbm, kept_out, given_out,
    tokens_ref, rows_ref, query_ref, pair_ref, kept_ref, given_ref, sum_ref, sems, out_sems,
):
    batch_count, gx_count, high_count, owned = dims
    query_cols = query_ref.shape[1]
    copies = [
        pltpu.make_async_copy(tokens_hbm, tokens_ref, sems.at[0]),
        pltpu.make_async_copy(pair_hbm, pair_ref, sems.at[1]),
    ]
    for place, (start, size) in enumerate(blocks):
        window = pl.ds(start, size)
        copies.append(pltpu.make_async_copy(query_hbm.at[window], query_ref.at[window], sems.at[place + 2]))
    for copy in copies:
        copy.start()
    steps, width = tokens_ref.shape[1:]
    block = gx_count * owned * steps
    half = rows_ref.shape[0] // 2
    copies[0].wait()
    for relative in range(2):
        low = lax.axis_index("gl") ^ relative
        for b in range(batch_count):
            for h in range(high_count):
                parts = []
                for g in range(gx_count):
                    first = (((b * gx_count + g) * high_count + h) * 2 + low) * owned
                    parts.append(tokens_ref[pl.ds(first, owned)])
                joined = jnp.concatenate(parts, axis=0).reshape(block, width)
                at = ((relative * batch_count + b) * high_count + h) * block
                rows_ref[pl.ds(at, block)] = joined
    writes = []

    def emit(product, start):
        product = product.astype(jnp.bfloat16)
        window = pl.ds(start, product.shape[1])
        kept_ref[:, window] = product[:half]
        given_ref[:, window] = product[half:]
        for source, target in ((given_ref, given_out), (kept_ref, kept_out)):
            copy = pltpu.make_async_copy(source.at[:, window], target.at[:, window], out_sems.at[len(writes)])
            copy.start()
            writes.append(copy)

    copies[1].wait()
    emit(jnp.dot(rows_ref[...], pair_ref[...], preferred_element_type=jnp.float32), query_cols)
    for place, (depth_at, depth) in enumerate(blocks):
        copies[2 + place].wait()
        rows = rows_ref[:, pl.ds(depth_at, depth)]
        for start, size in chunks:
            window = pl.ds(start, size)
            term = jnp.dot(
                rows, query_ref[pl.ds(depth_at, depth), window], preferred_element_type=jnp.float32
            )
            if place > 0:
                term = term + sum_ref[:, window]
            if place < len(blocks) - 1:
                sum_ref[:, window] = term
            else:
                emit(term, start)
    for copy in writes:
        copy.wait()


def cut(total, sizes):
    windows, start = [], 0
    while start < total:
        size = min(sizes[min(len(windows), len(sizes) - 1)], total - start)
        windows.append((start, size))
        start += size
    return windows


def project(tokens, w_query, w_keyval, dims):
    sequences, steps, width = tokens.shape
    query_cols, pair_cols = w_query.shape[1], w_keyval.shape[1]
    rows = sequences * steps
    blocks = cut(width, (768, 768, 512, 256))
    chunks = cut(query_cols, (768,))
    hbm = pl.BlockSpec(memory_space=pltpu.HBM)
    shape = jax.ShapeDtypeStruct((rows // 2, query_cols + pair_cols), jnp.bfloat16)
    return pl.pallas_call(
        functools.partial(project_kernel, dims, blocks, chunks),
        out_shape=(shape, shape),
        in_specs=[hbm, hbm, hbm],
        out_specs=(hbm, hbm),
        scratch_shapes=[
            pltpu.VMEM(tokens.shape, jnp.bfloat16),
            pltpu.VMEM((rows, width), jnp.bfloat16),
            pltpu.VMEM((width, query_cols), jnp.bfloat16),
            pltpu.VMEM((width, pair_cols), jnp.bfloat16),
            pltpu.VMEM((rows // 2, query_cols + pair_cols), jnp.bfloat16),
            pltpu.VMEM((rows // 2, query_cols + pair_cols), jnp.bfloat16),
            pltpu.VMEM((rows, query_cols), jnp.float32),
            pltpu.SemaphoreType.DMA((2 + len(blocks),)),
            pltpu.SemaphoreType.DMA((2 * (1 + len(chunks)),)),
        ],
        compiler_params=pltpu.CompilerParams(vmem_limit_bytes=62 * 1024 * 1024),
        cost_estimate=pl.CostEstimate(
            flops=2 * rows * width * (query_cols + pair_cols),
            bytes_accessed=2 * width * (query_cols + pair_cols),
            transcendentals=0,
        ),
        name="project",
    )(tokens, w_query, w_keyval)


def near_kernel(after_ref, source_ref, target_ref, token_ref, sem):
    copy = pltpu.make_async_copy(source_ref, target_ref, sem)
    copy.start()
    copy.wait()
    token_ref[...] = jnp.zeros_like(token_ref)


def near(after, array):
    anywhere = pl.BlockSpec(memory_space=pl.ANY)
    return pl.pallas_call(
        near_kernel,
        out_shape=(
            jax.ShapeDtypeStruct(array.shape, array.dtype),
            jax.ShapeDtypeStruct((8, 128), jnp.float32),
        ),
        in_specs=[anywhere, anywhere],
        out_specs=(anywhere, pl.BlockSpec(memory_space=pltpu.VMEM)),
        scratch_shapes=[pltpu.SemaphoreType.DMA],
        compiler_params=pltpu.CompilerParams(vmem_limit_bytes=36 * 1024 * 1024),
        cost_estimate=pl.CostEstimate(
            flops=0, bytes_accessed=2 * array.size * array.dtype.itemsize, transcendentals=0
        ),
        name="near",
    )(after, array)


def staged_kernel(source_ref, target_ref):
    target_ref[...] = source_ref[...]


def staged(array):
    vmem = pl.BlockSpec(memory_space=pltpu.VMEM)
    return pl.pallas_call(
        staged_kernel,
        out_shape=jax.ShapeDtypeStruct(array.shape, array.dtype),
        in_specs=[vmem],
        out_specs=vmem,
        compiler_params=pltpu.CompilerParams(vmem_limit_bytes=8 * 1024 * 1024),
        name="staged",
    )(array)


def combine_kernel(dims, kept_ref, taken_ref, own_ref, *sends):
    batch_count, high_count, block = dims
    for db in range(batch_count):
        for dh in range(high_count):
            at = ((lax.axis_index("batch") ^ db) * high_count + (lax.axis_index("gh") ^ dh)) * block
            window = pl.ds(pl.multiple_of(at, block), block)
            total = kept_ref[window].astype(jnp.float32) + taken_ref[window].astype(jnp.float32)
            target = sends[db * high_count + dh - 1] if db or dh else own_ref
            target[...] = total.astype(target.dtype)


def combine(kept, taken, dims):
    batch_count, high_count, block = dims
    cols = kept.shape[1]
    vmem = pl.BlockSpec(memory_space=pltpu.VMEM)
    count = batch_count * high_count
    return pl.pallas_call(
        functools.partial(combine_kernel, dims),
        out_shape=[jax.ShapeDtypeStruct((block, cols), jnp.float32)]
        + [jax.ShapeDtypeStruct((block, cols), jnp.bfloat16)] * (count - 1),
        in_specs=[vmem, vmem],
        out_specs=[vmem] * count,
        compiler_params=pltpu.CompilerParams(vmem_limit_bytes=8 * 1024 * 1024),
        name="combine",
    )(kept, taken)


def collect_kernel(count, own_ref, after_ref, *refs):
    received, outs, total_ref = refs[: -count - 1], refs[-count - 1 : -1], refs[-1]
    total = own_ref[...]
    for other in received:
        total = total + other[...].astype(jnp.float32)
    rows = outs[0].shape[0]
    for g in range(count):
        total_ref[g] = total[g * rows : (g + 1) * rows]
    for k in range(count):
        outs[k][...] = total_ref[lax.axis_index("gx") ^ k].astype(jnp.bfloat16)


def collect(own, received, after, gx_count):
    block, cols = own.shape
    rows = block // gx_count
    vmem = pl.BlockSpec(memory_space=pltpu.VMEM)
    return pl.pallas_call(
        functools.partial(collect_kernel, gx_count),
        out_shape=[jax.ShapeDtypeStruct((rows, cols), jnp.bfloat16)] * gx_count,
        in_specs=[vmem, pl.BlockSpec(memory_space=pl.ANY)]
        + [vmem] * len(received),
        out_specs=[vmem] * gx_count,
        scratch_shapes=[pltpu.VMEM((gx_count, rows, cols), jnp.float32)],
        compiler_params=pltpu.CompilerParams(vmem_limit_bytes=8 * 1024 * 1024),
        name="collect",
    )(own, after, *received)


def attend_kernel(dims, mask_ref, cos_ref, sin_ref, keys_ref, values_ref, *refs):
    gx_count, owned, steps, heads, width = dims
    blocks, outs = [None] * gx_count, refs[gx_count:-2]
    for k, ref in zip(farther_first(gx_count), refs):
        blocks[k] = ref
    rows_ref, result_ref = refs[-2:]
    query_cols = heads * width
    half = width // 2
    scaling = 1.0 / width**0.5
    count = gx_count * heads * steps
    cosine = jnp.concatenate([cos_ref[s] for s in range(owned)], axis=0)
    sine = jnp.concatenate([sin_ref[s] for s in range(owned)], axis=0)

    def turn(first, second):
        return first * cosine - second * sine, second * cosine + first * sine

    key_value = [ref[:, pl.ds(query_cols, ref.shape[1] - query_cols)].astype(jnp.float32) for ref in blocks]
    key_value = jnp.concatenate(unxored(key_value, lax.axis_index("gx")), axis=1)
    new_values = key_value[:, width:]
    new_keys = turn(key_value[:, :half], key_value[:, half:width])
    new_keys = jnp.concatenate(new_keys, axis=1).astype(jnp.bfloat16).astype(jnp.float32)
    for k in range(gx_count):
        for h in range(heads):
            first = blocks[k][:, pl.ds(h * width, half)].astype(jnp.float32)
            second = blocks[k][:, pl.ds(h * width + half, half)].astype(jnp.float32)
            for part, value in enumerate(turn(first, second)):
                for s in range(owned):
                    window = pl.ds((k * heads + h) * steps, steps)
                    rows_ref[s, window, pl.ds(part * half, half)] = value[s * steps : (s + 1) * steps]
    step_of = lax.broadcasted_iota(jnp.int32, (count, 1), 0) % steps
    for s in range(owned):
        queries = rows_ref[s].astype(jnp.bfloat16)
        cached = lax.dot_general(
            queries, keys_ref[s], (((1,), (1,)), ((), ())), preferred_element_type=jnp.float32
        )
        cached = cached * scaling + mask_ref[s]
        highest = cached.max(-1, keepdims=True)
        wide = queries.astype(jnp.float32)
        fresh = []
        for u in range(steps):
            row = s * steps + u
            score = (wide * new_keys[row : row + 1]).sum(-1, keepdims=True) * scaling
            fresh.append(jnp.where(step_of >= u, score, -1e30))
            highest = jnp.maximum(highest, fresh[-1])
        exp_cached = jnp.exp(cached - highest)
        denom = exp_cached.sum(-1, keepdims=True)
        total = jnp.dot(
            exp_cached.astype(jnp.bfloat16), values_ref[s], preferred_element_type=jnp.float32
        )
        for u in range(steps):
            row = s * steps + u
            exp_fresh = jnp.exp(fresh[u] - highest)
            denom = denom + exp_fresh
            total = total + exp_fresh * new_values[row : row + 1]
        result_ref[s] = total / denom
    for k in range(gx_count):
        for h in range(heads):
            window = pl.ds((k * heads + h) * steps, steps)
            value = jnp.concatenate([result_ref[s, window] for s in range(owned)], axis=0)
            outs[k][:, pl.ds(h * width, width)] = value.astype(jnp.bfloat16)


def attend(blocks, cache_keys, cache_values, lengths, query_cols):
    gx_count = len(blocks)
    owned, slots, width = cache_keys.shape
    rows = blocks[0].shape[0]
    steps = rows // owned
    heads = query_cols // width
    count = gx_count * heads * steps
    freqs = 10000.0 ** (-(jnp.arange(width // 2, dtype=jnp.float32) * 2.0 / width))
    positions = lengths[:, None, None] + jnp.arange(steps, dtype=jnp.int32)[None, :, None]
    angles = positions.astype(jnp.float32) * freqs
    mask = jnp.where(jnp.arange(slots)[None, None, :] < lengths[:, None, None], 0.0, -1e30)
    vmem = pl.BlockSpec(memory_space=pltpu.VMEM)
    return pl.pallas_call(
        functools.partial(attend_kernel, (gx_count, owned, steps, heads, width)),
        out_shape=[jax.ShapeDtypeStruct((rows, query_cols), jnp.bfloat16)] * gx_count,
        in_specs=[vmem] * (5 + gx_count),
        out_specs=[vmem] * gx_count,
        scratch_shapes=[
            pltpu.VMEM((owned, count, width), jnp.float32),
            pltpu.VMEM((owned, count, width), jnp.float32),
        ],
        compiler_params=pltpu.CompilerParams(vmem_limit_bytes=12 * 1024 * 1024),
        cost_estimate=pl.CostEstimate(
            flops=4 * owned * count * slots * width,
            bytes_accessed=4 * owned * slots * width,
            transcendentals=owned * count * slots,
        ),
        name="attend",
    )(mask, jnp.cos(angles), jnp.sin(angles), cache_keys, cache_values, *[blocks[k] for k in farther_first(gx_count)])


def order_kernel(*refs):
    blocks, (out_ref, sorted_ref) = refs[:-2], refs[-2:]
    for k, block in enumerate(blocks):
        sorted_ref[lax.axis_index("gx") ^ k] = block[...].astype(jnp.float32)
    parts = [sorted_ref[g] for g in range(len(blocks))]
    out_ref[...] = jnp.concatenate(parts, axis=0).astype(out_ref.dtype)


def order(blocks):
    vmem = pl.BlockSpec(memory_space=pltpu.VMEM)
    rows, cols = blocks[0].shape
    count = len(blocks)
    turn = lambda *refs: order_kernel(refs[0], *refs[count - 1 : 0 : -1], *refs[count:])
    return pl.pallas_call(
        turn,
        out_shape=jax.ShapeDtypeStruct((count * rows, cols), blocks[0].dtype),
        in_specs=[vmem] * count,
        out_specs=vmem,
        scratch_shapes=[pltpu.VMEM((count, rows, cols), jnp.float32)],
        compiler_params=pltpu.CompilerParams(vmem_limit_bytes=8 * 1024 * 1024),
        name="order",
    )(blocks[0], *blocks[:0:-1])


def mix_kernel(dims, chunk, part, weight_ref, *refs):
    batch_count, gx_count, high_count, block = dims
    count = 2 * batch_count * high_count
    blocks, own_ref, sends, (rows_ref, sum_ref) = refs[:count][::-1], refs[count], refs[count + 1 : -2], refs[-2:]
    shards = gx_count // batch_count
    group = block // shards
    for relative in range(2):
        for db in range(batch_count):
            for dh in range(high_count):
                b, h = lax.axis_index("batch") ^ db, lax.axis_index("gh") ^ dh
                at = ((relative * batch_count + b) * high_count + h) * block
                source = blocks[(relative * batch_count + db) * high_count + dh]
                rows_ref[pl.ds(pl.multiple_of(at, block), block)] = source[...]
    lhs = rows_ref[...]
    first, out_cols = part
    for start in range(0, out_cols, chunk):
        size = min(chunk, out_cols - start)
        window = pl.ds(start, size)
        sum_ref[:, pl.ds(0, size)] = jnp.dot(
            lhs, weight_ref[:, pl.ds(first + start, size)], preferred_element_type=jnp.float32
        )
        for k in range(gx_count):
            shard = lax.axis_index("gx") ^ k
            b, hi = shard // shards, shard % shards
            parts = []
            for relative in range(2):
                for h in range(high_count):
                    at = ((relative * batch_count + b) * high_count + h) * block + hi * group
                    at = pl.multiple_of(at, group)
                    parts.append(sum_ref[pl.ds(at, group), pl.ds(0, size)])
            piece = jnp.concatenate(parts, axis=0)
            target = own_ref if k == 0 else sends[k - 1]
            target[:, window] = piece.astype(target.dtype)


def mix(blocks, w_out, dims, part):
    batch_count, gx_count, high_count, block = dims
    depth = w_out.shape[0]
    out_cols = part[1]
    rows = len(blocks) * block
    chunk = min(768, out_cols)
    vmem = pl.BlockSpec(memory_space=pltpu.VMEM)
    kept = (0, 2) if gx_count == 4 else (0,)
    shapes = [
        jax.ShapeDtypeStruct((rows // gx_count, out_cols), jnp.float32 if k in kept else jnp.bfloat16)
        for k in range(gx_count)
    ]
    return pl.pallas_call(
        functools.partial(mix_kernel, dims, chunk, part),
        out_shape=shapes,
        in_specs=[vmem] * (1 + len(blocks)),
        out_specs=[vmem] * gx_count,
        scratch_shapes=[pltpu.VMEM((rows, depth), jnp.bfloat16), pltpu.VMEM((rows, chunk), jnp.float32)],
        compiler_params=pltpu.CompilerParams(vmem_limit_bytes=20 * 1024 * 1024),
        cost_estimate=pl.CostEstimate(
            flops=2 * rows * depth * out_cols, bytes_accessed=2 * depth * out_cols, transcendentals=0
        ),
        name="mix",
    )(w_out, *blocks[::-1])


def relay_kernel(own_ref, taken_ref, near_ref, sum_ref, copy_ref):
    total = own_ref[...] + taken_ref[...].astype(jnp.float32)
    sum_ref[...] = total.astype(sum_ref.dtype)
    copy_ref[...] = near_ref[...]


def relay(own, taken, near):
    vmem = pl.BlockSpec(memory_space=pltpu.VMEM)
    return pl.pallas_call(
        relay_kernel,
        out_shape=[jax.ShapeDtypeStruct(near.shape, near.dtype)] * 2,
        in_specs=[vmem] * 3,
        out_specs=[vmem] * 2,
        compiler_params=pltpu.CompilerParams(vmem_limit_bytes=8 * 1024 * 1024),
        name="relay",
    )(own, taken, near)


def summed_terms(sends):
    count = len(sends) + 1
    if count != 4:
        return [swapped_with(sends[k - 1], "gx", (count,), (k,)) for k in farther_first(count)[1:]]
    near, far, farthest = sends
    taken = swapped_with(farthest, "gx", (count,), (1,))
    both, near = relay(far, taken, near)
    return [swapped_with(both, "gx", (count,), (2,)), swapped_with(near, "gx", (count,), (1,))]


def finish_kernel(dims, own_ref, *refs):
    received, out_ref = refs[: len(refs) - 1], refs[-1]
    batch_count, high_count, owned = dims
    steps, out_cols = out_ref.shape[1:]
    size = batch_count * owned * steps
    received = [ref for ref in received if ref.shape == own_ref.shape]
    for relative in range(2):
        low = lax.axis_index("gl") ^ relative
        for h in range(high_count):
            window = pl.ds((relative * high_count + h) * size, size)
            total = own_ref[window]
            for other in received:
                total = total + other[window].astype(jnp.float32)
            total = total.reshape(batch_count, owned, steps, out_cols).astype(jnp.bfloat16)
            for g in range(batch_count):
                first = ((g * high_count + h) * 2 + low) * owned
                out_ref[pl.ds(first, owned)] = total[g]


def finish(own, received, dims, steps, part, parts, before):
    rows, out_cols = own.shape
    whole = pl.BlockSpec((rows, out_cols), lambda step: (0, 0))
    operands = [own, *received]
    in_specs = [whole] * len(operands)
    aliases = {}
    if before is not None:
        aliases[len(operands)] = 0
        operands.append(before)
        in_specs.append(pl.BlockSpec(memory_space=pl.ANY))
    return pl.pallas_call(
        functools.partial(finish_kernel, dims),
        grid=(1,),
        out_shape=jax.ShapeDtypeStruct((rows // steps, steps, out_cols * parts), jnp.bfloat16),
        in_specs=in_specs,
        out_specs=pl.BlockSpec((rows // steps, steps, out_cols), lambda step: (0, 0, part)),
        input_output_aliases=aliases,
        compiler_params=pltpu.CompilerParams(vmem_limit_bytes=16 * 1024 * 1024),
        name="finish",
    )(*operands)


def local(tokens, w_query, w_keyval, w_out, cache_keys, cache_values, lengths):
    batch_count = lax.axis_size("batch")
    gx_count = lax.axis_size("gx")
    high_count = lax.axis_size("gh")
    sizes = (batch_count, high_count, 2)
    owned = cache_keys.shape[0]
    sequences, steps, width = tokens.shape
    query_cols = w_query.shape[1]
    rows = owned * steps
    rows_here = gx_count * rows

    kept, given = project(tokens, w_query, w_keyval, (batch_count, gx_count, high_count, owned))
    taken = swapped_with(given, PLANE, sizes, (0, 0, 1))
    far = [(db, dh) for db in range(batch_count) for dh in range(high_count)][1:]
    own, *sends = combine(staged(kept), taken, (batch_count, high_count, rows_here))
    received = [
        swapped_with(block, PLANE, sizes, (db, dh, 0)) for block, (db, dh) in zip(sends, far)
    ]
    w_out, token = near(own, w_out)
    blocks = collect(own, received, token, gx_count)
    blocks = [blocks[0]] + [
        swapped_with(blocks[k], "gx", (gx_count,), (k,)) for k in range(1, gx_count)
    ]
    blocks = attend(blocks, cache_keys, cache_values, lengths, query_cols)
    blocks = [blocks[0]] + [
        swapped_with(blocks[k], "gx", (gx_count,), (k,)) for k in range(1, gx_count)
    ]
    grouped = order(blocks)

    ours = [grouped] + [swapped_with(grouped, PLANE, sizes, (db, dh, 0)) for db, dh in far]
    theirs = [swapped_with(block, PLANE, sizes, (0, 0, 1)) for block in ours]
    out_cols = w_out.shape[1]
    parts = 2 if out_cols % 256 == 0 else 1
    size = out_cols // parts
    mixed = None
    products = [
        mix(ours + theirs, w_out, (batch_count, gx_count, high_count, rows_here), (part * size, size))
        for part in range(parts)
    ]
    for part, (own, *sends) in enumerate(products):
        received = summed_terms(sends)
        mixed = finish(own, received, (batch_count, high_count, owned), steps, part, parts, mixed)
    return mixed


def solution(mesh):
    batch_count, gx_count, gy_count = mesh.devices.shape
    split = Mesh(
        mesh.devices.reshape(batch_count, gx_count, gy_count // 2, 2), ("batch", "gx", "gh", "gl")
    )
    plane = ("batch", "gh", "gl")
    placed = (
        P(None, None, plane),
        P(plane, "gx"),
        P(plane, "gx"),
        P("gx", plane),
        P(("batch", "gx", "gh", "gl"), None, None),
        P(("batch", "gx", "gh", "gl"), None, None),
        P(("batch", "gx", "gh", "gl")),
    )
    return jax.shard_map(
        local, mesh=split, in_specs=placed, out_specs=P("gx", None, plane), check_vma=False
    )
```

```python
import functools
import math

import jax
import jax.numpy as jnp
import numpy as np
from jax import lax
from jax.experimental import pallas as pl
from jax.experimental.pallas import tpu as pltpu
from jax.sharding import Mesh
from jax.sharding import PartitionSpec as P

PLANE = ("batch", "gh", "gl")


def swapped_with(value, axes, sizes, differs):
    pairs = []
    for place in np.ndindex(*sizes):
        target = tuple(p ^ d for p, d in zip(place, differs))
        pairs.append((int(np.ravel_multi_index(place, sizes)), int(np.ravel_multi_index(target, sizes))))
    return lax.ppermute(value, axes, pairs)


def unxored(blocks, here):
    count = len(blocks)
    bit = 1
    while bit < count:
        turn = (here & bit) != 0
        blocks = [jnp.where(turn, blocks[k ^ bit], blocks[k]) for k in range(count)]
        bit *= 2
    return blocks


def farther_first(count):
    return [0, *range(2, count), 1]


def project_kernel(
    dims, blocks, chunks, tokens_hbm, query_hbm, pair_hbm, kept_out, given_out,
    tokens_ref, rows_ref, query_ref, pair_ref, kept_ref, given_ref, sum_ref, sems, out_sems,
):
    batch_count, gx_count, high_count, owned = dims
    query_cols = query_ref.shape[1]
    copies = [
        pltpu.make_async_copy(tokens_hbm, tokens_ref, sems.at[0]),
        pltpu.make_async_copy(pair_hbm, pair_ref, sems.at[1]),
    ]
    for place, (start, size) in enumerate(blocks):
        window = pl.ds(start, size)
        copies.append(pltpu.make_async_copy(query_hbm.at[window], query_ref.at[window], sems.at[place + 2]))
    for copy in copies:
        copy.start()
    steps, width = tokens_ref.shape[1:]
    block = gx_count * owned * steps
    half = rows_ref.shape[0] // 2
    copies[0].wait()
    for relative in range(2):
        low = lax.axis_index("gl") ^ relative
        for b in range(batch_count):
            for h in range(high_count):
                parts = []
                for g in range(gx_count):
                    first = (((b * gx_count + g) * high_count + h) * 2 + low) * owned
                    parts.append(tokens_ref[pl.ds(first, owned)])
                joined = jnp.concatenate(parts, axis=0).reshape(block, width)
                at = ((relative * batch_count + b) * high_count + h) * block
                rows_ref[pl.ds(at, block)] = joined
    writes = []

    def emit(product, start):
        product = product.astype(jnp.bfloat16)
        window = pl.ds(start, product.shape[1])
        kept_ref[:, window] = product[:half]
        given_ref[:, window] = product[half:]
        for source, target in ((given_ref, given_out), (kept_ref, kept_out)):
            copy = pltpu.make_async_copy(source.at[:, window], target.at[:, window], out_sems.at[len(writes)])
            copy.start()
            writes.append(copy)

    copies[1].wait()
    emit(jnp.dot(rows_ref[...], pair_ref[...], preferred_element_type=jnp.float32), query_cols)
    for place, (depth_at, depth) in enumerate(blocks):
        copies[2 + place].wait()
        rows = rows_ref[:, pl.ds(depth_at, depth)]
        for start, size in chunks:
            window = pl.ds(start, size)
            term = jnp.dot(
                rows, query_ref[pl.ds(depth_at, depth), window], preferred_element_type=jnp.float32
            )
            if place > 0:
                term = term + sum_ref[:, window]
            if place < len(blocks) - 1:
                sum_ref[:, window] = term
            else:
                emit(term, start)
    for copy in writes:
        copy.wait()


def cut(total, sizes):
    windows, start = [], 0
    while start < total:
        size = min(sizes[min(len(windows), len(sizes) - 1)], total - start)
        windows.append((start, size))
        start += size
    return windows


def project(tokens, w_query, w_keyval, dims):
    sequences, steps, width = tokens.shape
    query_cols, pair_cols = w_query.shape[1], w_keyval.shape[1]
    rows = sequences * steps
    blocks = cut(width, (768, 768, 512, 256))
    chunks = cut(query_cols, (768,))
    hbm = pl.BlockSpec(memory_space=pltpu.HBM)
    shape = jax.ShapeDtypeStruct((rows // 2, query_cols + pair_cols), jnp.bfloat16)
    return pl.pallas_call(
        functools.partial(project_kernel, dims, blocks, chunks),
        out_shape=(shape, shape),
        in_specs=[hbm, hbm, hbm],
        out_specs=(hbm, hbm),
        scratch_shapes=[
            pltpu.VMEM(tokens.shape, jnp.bfloat16),
            pltpu.VMEM((rows, width), jnp.bfloat16),
            pltpu.VMEM((width, query_cols), jnp.bfloat16),
            pltpu.VMEM((width, pair_cols), jnp.bfloat16),
            pltpu.VMEM((rows // 2, query_cols + pair_cols), jnp.bfloat16),
            pltpu.VMEM((rows // 2, query_cols + pair_cols), jnp.bfloat16),
            pltpu.VMEM((rows, query_cols), jnp.float32),
            pltpu.SemaphoreType.DMA((2 + len(blocks),)),
            pltpu.SemaphoreType.DMA((2 * (1 + len(chunks)),)),
        ],
        compiler_params=pltpu.CompilerParams(vmem_limit_bytes=62 * 1024 * 1024),
        cost_estimate=pl.CostEstimate(
            flops=2 * rows * width * (query_cols + pair_cols),
            bytes_accessed=2 * width * (query_cols + pair_cols),
            transcendentals=0,
        ),
        name="project",
    )(tokens, w_query, w_keyval)


def near_kernel(after_ref, source_ref, target_ref, token_ref, sem):
    copy = pltpu.make_async_copy(source_ref, target_ref, sem)
    copy.start()
    copy.wait()
    token_ref[...] = jnp.zeros_like(token_ref)


def near(after, array):
    anywhere = pl.BlockSpec(memory_space=pl.ANY)
    return pl.pallas_call(
        near_kernel,
        out_shape=(
            jax.ShapeDtypeStruct(array.shape, array.dtype),
            jax.ShapeDtypeStruct((8, 128), jnp.float32),
        ),
        in_specs=[anywhere, anywhere],
        out_specs=(anywhere, pl.BlockSpec(memory_space=pltpu.VMEM)),
        scratch_shapes=[pltpu.SemaphoreType.DMA],
        compiler_params=pltpu.CompilerParams(vmem_limit_bytes=36 * 1024 * 1024),
        cost_estimate=pl.CostEstimate(
            flops=0, bytes_accessed=2 * array.size * array.dtype.itemsize, transcendentals=0
        ),
        name="near",
    )(after, array)


def staged_kernel(source_ref, target_ref):
    target_ref[...] = source_ref[...]


def staged(array):
    vmem = pl.BlockSpec(memory_space=pltpu.VMEM)
    return pl.pallas_call(
        staged_kernel,
        out_shape=jax.ShapeDtypeStruct(array.shape, array.dtype),
        in_specs=[vmem],
        out_specs=vmem,
        compiler_params=pltpu.CompilerParams(vmem_limit_bytes=8 * 1024 * 1024),
        name="staged",
    )(array)


def combine_kernel(dims, kept_ref, taken_ref, own_ref, *sends):
    batch_count, high_count, block = dims
    for db in range(batch_count):
        for dh in range(high_count):
            at = ((lax.axis_index("batch") ^ db) * high_count + (lax.axis_index("gh") ^ dh)) * block
            window = pl.ds(pl.multiple_of(at, block), block)
            total = kept_ref[window].astype(jnp.float32) + taken_ref[window].astype(jnp.float32)
            target = sends[db * high_count + dh - 1] if db or dh else own_ref
            target[...] = total.astype(target.dtype)


def combine(kept, taken, dims):
    batch_count, high_count, block = dims
    cols = kept.shape[1]
    vmem = pl.BlockSpec(memory_space=pltpu.VMEM)
    count = batch_count * high_count
    return pl.pallas_call(
        functools.partial(combine_kernel, dims),
        out_shape=[jax.ShapeDtypeStruct((block, cols), jnp.float32)]
        + [jax.ShapeDtypeStruct((block, cols), jnp.bfloat16)] * (count - 1),
        in_specs=[vmem, vmem],
        out_specs=[vmem] * count,
        compiler_params=pltpu.CompilerParams(vmem_limit_bytes=8 * 1024 * 1024),
        name="combine",
    )(kept, taken)


def collect_kernel(layout, own_ref, after_ref, *refs):
    outs, total_ref = refs[-1 - len(layout) : -1], refs[-1]
    total = own_ref[...]
    for other in refs[: -1 - len(layout)]:
        total = total + other[...].astype(jnp.float32)
    count, rows = total_ref.shape[:2]
    for g in range(count):
        total_ref[g] = total[g * rows : (g + 1) * rows]
    for distances, out_ref in zip(layout, outs):
        for i, k in enumerate(distances):
            out_ref[i] = total_ref[lax.axis_index("gx") ^ k].astype(out_ref.dtype)


def collect(own, received, after, gx_count, layout):
    block, cols = own.shape
    rows = block // gx_count
    vmem = pl.BlockSpec(memory_space=pltpu.VMEM)
    return pl.pallas_call(
        functools.partial(collect_kernel, layout),
        out_shape=[jax.ShapeDtypeStruct((len(ks), rows, cols), jnp.bfloat16) for ks in layout],
        in_specs=[vmem, pl.BlockSpec(memory_space=pl.ANY)] + [vmem] * len(received),
        out_specs=[vmem] * len(layout),
        scratch_shapes=[pltpu.VMEM((gx_count, rows, cols), jnp.float32)],
        compiler_params=pltpu.CompilerParams(vmem_limit_bytes=8 * 1024 * 1024),
        name="collect",
    )(own, after, *received)


def join_kernel(first_ref, second_ref, out_ref):
    out_ref[0] = first_ref[0]
    out_ref[1] = second_ref[1]


def join(first, second):
    vmem = pl.BlockSpec(memory_space=pltpu.VMEM)
    return pl.pallas_call(
        join_kernel,
        out_shape=jax.ShapeDtypeStruct(second.shape, second.dtype),
        in_specs=[vmem] * 2,
        out_specs=vmem,
        compiler_params=pltpu.CompilerParams(vmem_limit_bytes=8 * 1024 * 1024),
        name="join",
    )(first, second)


def spread(own, received, after, gx_count):
    if gx_count != 4:
        layout = [[k] for k in farther_first(gx_count)]
        arrays = collect(own, received, after, gx_count, layout)
        swaps = [swapped_with(a, "gx", (gx_count,), (k,)) for a, (k,) in zip(arrays[1:], layout[1:])]
        return [arrays[0], *swaps], layout
    here, far, near = collect(own, received, after, gx_count, [[0], [2], [1, 3]])
    near = swapped_with(near, "gx", (gx_count,), (1,))
    far = swapped_with(join(far, near), "gx", (gx_count,), (2,))
    return [here, far, near], [[0], [2, 3], [1]]


def attend_kernel(dims, layout, mask_ref, cos_ref, sin_ref, keys_ref, values_ref, *refs):
    gx_count, owned, steps, heads, width = dims
    blocks, outs = [None] * gx_count, refs[len(layout) : -2]
    for distances, ref in zip(layout, refs):
        for i, k in enumerate(distances):
            blocks[k] = ref.at[i]
    rows_ref, result_ref = refs[-2:]
    query_cols = heads * width
    half = width // 2
    scaling = 1.0 / width**0.5
    count = gx_count * heads * steps
    cosine = jnp.concatenate([cos_ref[s] for s in range(owned)], axis=0)
    sine = jnp.concatenate([sin_ref[s] for s in range(owned)], axis=0)

    def turn(first, second):
        return first * cosine - second * sine, second * cosine + first * sine

    key_value = [ref[:, pl.ds(query_cols, ref.shape[1] - query_cols)].astype(jnp.float32) for ref in blocks]
    key_value = jnp.concatenate(unxored(key_value, lax.axis_index("gx")), axis=1)
    new_values = key_value[:, width:]
    new_keys = turn(key_value[:, :half], key_value[:, half:width])
    new_keys = jnp.concatenate(new_keys, axis=1).astype(jnp.bfloat16).astype(jnp.float32)
    for k in range(gx_count):
        for h in range(heads):
            first = blocks[k][:, pl.ds(h * width, half)].astype(jnp.float32)
            second = blocks[k][:, pl.ds(h * width + half, half)].astype(jnp.float32)
            for part, value in enumerate(turn(first, second)):
                for s in range(owned):
                    window = pl.ds((k * heads + h) * steps, steps)
                    rows_ref[s, window, pl.ds(part * half, half)] = value[s * steps : (s + 1) * steps]
    step_of = lax.broadcasted_iota(jnp.int32, (count, 1), 0) % steps
    for s in range(owned):
        queries = rows_ref[s].astype(jnp.bfloat16)
        cached = lax.dot_general(
            queries, keys_ref[s], (((1,), (1,)), ((), ())), preferred_element_type=jnp.float32
        )
        cached = cached * scaling + mask_ref[s]
        highest = cached.max(-1, keepdims=True)
        wide = queries.astype(jnp.float32)
        fresh = []
        for u in range(steps):
            row = s * steps + u
            score = (wide * new_keys[row : row + 1]).sum(-1, keepdims=True) * scaling
            fresh.append(jnp.where(step_of >= u, score, -1e30))
            highest = jnp.maximum(highest, fresh[-1])
        exp_cached = jnp.exp(cached - highest)
        denom = exp_cached.sum(-1, keepdims=True)
        total = jnp.dot(
            exp_cached.astype(jnp.bfloat16), values_ref[s], preferred_element_type=jnp.float32
        )
        for u in range(steps):
            row = s * steps + u
            exp_fresh = jnp.exp(fresh[u] - highest)
            denom = denom + exp_fresh
            total = total + exp_fresh * new_values[row : row + 1]
        result_ref[s] = total / denom
    for k in range(gx_count):
        for h in range(heads):
            window = pl.ds((k * heads + h) * steps, steps)
            value = jnp.concatenate([result_ref[s, window] for s in range(owned)], axis=0)
            outs[k][:, pl.ds(h * width, width)] = value.astype(jnp.bfloat16)


def attend(arrays, layout, cache_keys, cache_values, lengths, query_cols):
    gx_count = max(map(max, layout)) + 1
    owned, slots, width = cache_keys.shape
    rows = arrays[0].shape[1]
    steps = rows // owned
    heads = query_cols // width
    count = gx_count * heads * steps
    freqs = 10000.0 ** (-(jnp.arange(width // 2, dtype=jnp.float32) * 2.0 / width))
    positions = lengths[:, None, None] + jnp.arange(steps, dtype=jnp.int32)[None, :, None]
    angles = positions.astype(jnp.float32) * freqs
    mask = jnp.where(jnp.arange(slots)[None, None, :] < lengths[:, None, None], 0.0, -1e30)
    vmem = pl.BlockSpec(memory_space=pltpu.VMEM)
    return pl.pallas_call(
        functools.partial(attend_kernel, (gx_count, owned, steps, heads, width), layout),
        out_shape=[jax.ShapeDtypeStruct((rows, query_cols), jnp.bfloat16)] * gx_count,
        in_specs=[vmem] * (5 + len(arrays)),
        out_specs=[vmem] * gx_count,
        scratch_shapes=[
            pltpu.VMEM((owned, count, width), jnp.float32),
            pltpu.VMEM((owned, count, width), jnp.float32),
        ],
        compiler_params=pltpu.CompilerParams(vmem_limit_bytes=12 * 1024 * 1024),
        cost_estimate=pl.CostEstimate(
            flops=4 * owned * count * slots * width,
            bytes_accessed=4 * owned * slots * width,
            transcendentals=owned * count * slots,
        ),
        name="attend",
    )(mask, jnp.cos(angles), jnp.sin(angles), cache_keys, cache_values, *arrays)


def order_kernel(*refs):
    blocks, (out_ref, sorted_ref) = refs[:-2], refs[-2:]
    for k, block in enumerate(blocks):
        sorted_ref[lax.axis_index("gx") ^ k] = block[...].astype(jnp.float32)
    parts = [sorted_ref[g] for g in range(len(blocks))]
    out_ref[...] = jnp.concatenate(parts, axis=0).astype(out_ref.dtype)


def order(blocks):
    vmem = pl.BlockSpec(memory_space=pltpu.VMEM)
    rows, cols = blocks[0].shape
    count = len(blocks)
    turn = lambda *refs: order_kernel(refs[0], *refs[count - 1 : 0 : -1], *refs[count:])
    return pl.pallas_call(
        turn,
        out_shape=jax.ShapeDtypeStruct((count * rows, cols), blocks[0].dtype),
        in_specs=[vmem] * count,
        out_specs=vmem,
        scratch_shapes=[pltpu.VMEM((count, rows, cols), jnp.float32)],
        compiler_params=pltpu.CompilerParams(vmem_limit_bytes=8 * 1024 * 1024),
        name="order",
    )(blocks[0], *blocks[:0:-1])


def mix_kernel(dims, chunk, part, weight_ref, *refs):
    batch_count, gx_count, high_count, block = dims
    count = 2 * batch_count * high_count
    blocks, own_ref, sends, (rows_ref, sum_ref) = refs[:count][::-1], refs[count], refs[count + 1 : -2], refs[-2:]
    shards = gx_count // batch_count
    group = block // shards
    for relative in range(2):
        for db in range(batch_count):
            for dh in range(high_count):
                b, h = lax.axis_index("batch") ^ db, lax.axis_index("gh") ^ dh
                at = ((relative * batch_count + b) * high_count + h) * block
                source = blocks[(relative * batch_count + db) * high_count + dh]
                rows_ref[pl.ds(pl.multiple_of(at, block), block)] = source[...]
    lhs = rows_ref[...]
    first, out_cols = part
    for start in range(0, out_cols, chunk):
        size = min(chunk, out_cols - start)
        window = pl.ds(start, size)
        sum_ref[:, pl.ds(0, size)] = jnp.dot(
            lhs, weight_ref[:, pl.ds(first + start, size)], preferred_element_type=jnp.float32
        )
        for k in range(gx_count):
            shard = lax.axis_index("gx") ^ k
            b, hi = shard // shards, shard % shards
            parts = []
            for relative in range(2):
                for h in range(high_count):
                    at = ((relative * batch_count + b) * high_count + h) * block + hi * group
                    at = pl.multiple_of(at, group)
                    parts.append(sum_ref[pl.ds(at, group), pl.ds(0, size)])
            piece = jnp.concatenate(parts, axis=0)
            target = own_ref if k == 0 else sends[k - 1]
            target[:, window] = piece.astype(target.dtype)


def mix(blocks, w_out, dims, part):
    batch_count, gx_count, high_count, block = dims
    depth = w_out.shape[0]
    out_cols = part[1]
    rows = len(blocks) * block
    chunk = min(768, out_cols)
    vmem = pl.BlockSpec(memory_space=pltpu.VMEM)
    kept = (0, 2) if gx_count == 4 else (0,)
    shapes = [
        jax.ShapeDtypeStruct((rows // gx_count, out_cols), jnp.float32 if k in kept else jnp.bfloat16)
        for k in range(gx_count)
    ]
    return pl.pallas_call(
        functools.partial(mix_kernel, dims, chunk, part),
        out_shape=shapes,
        in_specs=[vmem] * (1 + len(blocks)),
        out_specs=[vmem] * gx_count,
        scratch_shapes=[pltpu.VMEM((rows, depth), jnp.bfloat16), pltpu.VMEM((rows, chunk), jnp.float32)],
        compiler_params=pltpu.CompilerParams(vmem_limit_bytes=20 * 1024 * 1024),
        cost_estimate=pl.CostEstimate(
            flops=2 * rows * depth * out_cols, bytes_accessed=2 * depth * out_cols, transcendentals=0
        ),
        name="mix",
    )(w_out, *blocks[::-1])


def relay_kernel(own_ref, taken_ref, near_ref, sum_ref, copy_ref):
    total = own_ref[...] + taken_ref[...].astype(jnp.float32)
    sum_ref[...] = total.astype(sum_ref.dtype)
    copy_ref[...] = near_ref[...]


def relay(own, taken, near):
    vmem = pl.BlockSpec(memory_space=pltpu.VMEM)
    return pl.pallas_call(
        relay_kernel,
        out_shape=[jax.ShapeDtypeStruct(near.shape, near.dtype)] * 2,
        in_specs=[vmem] * 3,
        out_specs=[vmem] * 2,
        compiler_params=pltpu.CompilerParams(vmem_limit_bytes=8 * 1024 * 1024),
        name="relay",
    )(own, taken, near)


def summed_terms(sends):
    count = len(sends) + 1
    if count != 4:
        return [swapped_with(sends[k - 1], "gx", (count,), (k,)) for k in farther_first(count)[1:]]
    near, far, farthest = sends
    taken = swapped_with(farthest, "gx", (count,), (1,))
    both, near = relay(far, taken, near)
    return [swapped_with(both, "gx", (count,), (2,)), swapped_with(near, "gx", (count,), (1,))]


def finish_kernel(dims, own_ref, *refs):
    received, out_ref = refs[: len(refs) - 1], refs[-1]
    batch_count, high_count, owned = dims
    steps, out_cols = out_ref.shape[1:]
    size = batch_count * owned * steps
    received = [ref for ref in received if ref.shape == own_ref.shape]
    for relative in range(2):
        low = lax.axis_index("gl") ^ relative
        for h in range(high_count):
            window = pl.ds((relative * high_count + h) * size, size)
            total = own_ref[window]
            for other in received:
                total = total + other[window].astype(jnp.float32)
            total = total.reshape(batch_count, owned, steps, out_cols).astype(jnp.bfloat16)
            for g in range(batch_count):
                first = ((g * high_count + h) * 2 + low) * owned
                out_ref[pl.ds(first, owned)] = total[g]


def finish(own, received, dims, steps, part, out_cols, before):
    rows = own.shape[0]
    first, count = part
    unit = math.gcd(first, count)
    whole = pl.BlockSpec((rows, unit), lambda step: (0, step))
    operands = [own, *received]
    in_specs = [whole] * len(operands)
    aliases = {}
    if before is not None:
        aliases[len(operands)] = 0
        operands.append(before)
        in_specs.append(pl.BlockSpec(memory_space=pl.ANY))
    return pl.pallas_call(
        functools.partial(finish_kernel, dims),
        grid=(count // unit,),
        out_shape=jax.ShapeDtypeStruct((rows // steps, steps, out_cols), jnp.bfloat16),
        in_specs=in_specs,
        out_specs=pl.BlockSpec((rows // steps, steps, unit), lambda step: (0, 0, first // unit + step)),
        input_output_aliases=aliases,
        compiler_params=pltpu.CompilerParams(vmem_limit_bytes=16 * 1024 * 1024),
        name="finish",
    )(*operands)


def local(tokens, w_query, w_keyval, w_out, cache_keys, cache_values, lengths):
    batch_count = lax.axis_size("batch")
    gx_count = lax.axis_size("gx")
    high_count = lax.axis_size("gh")
    sizes = (batch_count, high_count, 2)
    owned = cache_keys.shape[0]
    sequences, steps, width = tokens.shape
    query_cols = w_query.shape[1]
    rows = owned * steps
    rows_here = gx_count * rows

    kept, given = project(tokens, w_query, w_keyval, (batch_count, gx_count, high_count, owned))
    taken = swapped_with(given, PLANE, sizes, (0, 0, 1))
    far = [(db, dh) for db in range(batch_count) for dh in range(high_count)][1:]
    own, *sends = combine(staged(kept), taken, (batch_count, high_count, rows_here))
    received = [
        swapped_with(block, PLANE, sizes, (db, dh, 0)) for block, (db, dh) in zip(sends, far)
    ]
    w_out, token = near(own, w_out)
    arrays, layout = spread(own, received, token, gx_count)
    blocks = attend(arrays, layout, cache_keys, cache_values, lengths, query_cols)
    blocks = [blocks[0]] + [
        swapped_with(blocks[k], "gx", (gx_count,), (k,)) for k in range(1, gx_count)
    ]
    grouped = order(blocks)

    ours = [grouped] + [swapped_with(grouped, PLANE, sizes, (db, dh, 0)) for db, dh in far]
    theirs = [swapped_with(block, PLANE, sizes, (0, 0, 1)) for block in ours]
    out_cols = w_out.shape[1]
    parts = [(0, out_cols)]
    if out_cols % 256 == 0:
        parts = [(0, out_cols // 2), (out_cols // 2, out_cols // 2)]
    mixed = None
    products = [
        mix(ours + theirs, w_out, (batch_count, gx_count, high_count, rows_here), part) for part in parts
    ]
    for part, (own, *sends) in zip(parts, products):
        received = summed_terms(sends)
        mixed = finish(own, received, (batch_count, high_count, owned), steps, part, out_cols, mixed)
    return mixed


def solution(mesh):
    batch_count, gx_count, gy_count = mesh.devices.shape
    split = Mesh(
        mesh.devices.reshape(batch_count, gx_count, gy_count // 2, 2), ("batch", "gx", "gh", "gl")
    )
    plane = ("batch", "gh", "gl")
    placed = (
        P(None, None, plane),
        P(plane, "gx"),
        P(plane, "gx"),
        P("gx", plane),
        P(("batch", "gx", "gh", "gl"), None, None),
        P(("batch", "gx", "gh", "gl"), None, None),
        P(("batch", "gx", "gh", "gl")),
    )
    return jax.shard_map(
        local, mesh=split, in_specs=placed, out_specs=P("gx", None, plane), check_vma=False
    )
```

```python
import functools

import jax
import jax.numpy as jnp
import numpy as np
from jax import lax
from jax.experimental import pallas as pl
from jax.experimental.pallas import tpu as pltpu
from jax.sharding import Mesh
from jax.sharding import PartitionSpec as P

PLANE = ("batch", "gh", "gl")


def swapped_with(value, axes, sizes, differs):
    pairs = []
    for place in np.ndindex(*sizes):
        target = tuple(p ^ d for p, d in zip(place, differs))
        pairs.append((int(np.ravel_multi_index(place, sizes)), int(np.ravel_multi_index(target, sizes))))
    return lax.ppermute(value, axes, pairs)


def unxored(blocks, here):
    count = len(blocks)
    bit = 1
    while bit < count:
        turn = (here & bit) != 0
        blocks = [jnp.where(turn, blocks[k ^ bit], blocks[k]) for k in range(count)]
        bit *= 2
    return blocks


def farther_first(count):
    return [0, *range(2, count), 1]


def project_kernel(
    dims, blocks, chunks, tokens_hbm, query_hbm, pair_hbm, kept_out, given_out,
    tokens_ref, rows_ref, query_ref, pair_ref, kept_ref, given_ref, sum_ref, sems, out_sems,
):
    batch_count, gx_count, high_count, owned = dims
    query_cols = query_ref.shape[1]
    copies = [
        pltpu.make_async_copy(tokens_hbm, tokens_ref, sems.at[0]),
        pltpu.make_async_copy(pair_hbm, pair_ref, sems.at[1]),
    ]
    for place, (start, size) in enumerate(blocks):
        window = pl.ds(start, size)
        copies.append(pltpu.make_async_copy(query_hbm.at[window], query_ref.at[window], sems.at[place + 2]))
    for copy in copies:
        copy.start()
    steps, width = tokens_ref.shape[1:]
    block = gx_count * owned * steps
    half = rows_ref.shape[0] // 2
    copies[0].wait()
    for relative in range(2):
        low = lax.axis_index("gl") ^ relative
        for b in range(batch_count):
            for h in range(high_count):
                parts = []
                for g in range(gx_count):
                    first = (((b * gx_count + g) * high_count + h) * 2 + low) * owned
                    parts.append(tokens_ref[pl.ds(first, owned)])
                joined = jnp.concatenate(parts, axis=0).reshape(block, width)
                at = ((relative * batch_count + b) * high_count + h) * block
                rows_ref[pl.ds(at, block)] = joined
    writes = []

    def emit(product, start):
        product = product.astype(jnp.bfloat16)
        window = pl.ds(start, product.shape[1])
        kept_ref[:, window] = product[:half]
        given_ref[:, window] = product[half:]
        for source, target in ((given_ref, given_out), (kept_ref, kept_out)):
            copy = pltpu.make_async_copy(source.at[:, window], target.at[:, window], out_sems.at[len(writes)])
            copy.start()
            writes.append(copy)

    copies[1].wait()
    emit(jnp.dot(rows_ref[...], pair_ref[...], preferred_element_type=jnp.float32), query_cols)
    for place, (depth_at, depth) in enumerate(blocks):
        copies[2 + place].wait()
        rows = rows_ref[:, pl.ds(depth_at, depth)]
        for start, size in chunks:
            window = pl.ds(start, size)
            term = jnp.dot(
                rows, query_ref[pl.ds(depth_at, depth), window], preferred_element_type=jnp.float32
            )
            if place > 0:
                term = term + sum_ref[:, window]
            if place < len(blocks) - 1:
                sum_ref[:, window] = term
            else:
                emit(term, start)
    for copy in writes:
        copy.wait()


def cut(total, sizes):
    windows, start = [], 0
    while start < total:
        size = min(sizes[min(len(windows), len(sizes) - 1)], total - start)
        windows.append((start, size))
        start += size
    return windows


def project(tokens, w_query, w_keyval, dims):
    sequences, steps, width = tokens.shape
    query_cols, pair_cols = w_query.shape[1], w_keyval.shape[1]
    rows = sequences * steps
    blocks = cut(width, (1024, 768, 384, 128))
    chunks = cut(query_cols, (768,))
    hbm = pl.BlockSpec(memory_space=pltpu.HBM)
    shape = jax.ShapeDtypeStruct((rows // 2, query_cols + pair_cols), jnp.bfloat16)
    return pl.pallas_call(
        functools.partial(project_kernel, dims, blocks, chunks),
        out_shape=(shape, shape),
        in_specs=[hbm, hbm, hbm],
        out_specs=(hbm, hbm),
        scratch_shapes=[
            pltpu.VMEM(tokens.shape, jnp.bfloat16),
            pltpu.VMEM((rows, width), jnp.bfloat16),
            pltpu.VMEM((width, query_cols), jnp.bfloat16),
            pltpu.VMEM((width, pair_cols), jnp.bfloat16),
            pltpu.VMEM((rows // 2, query_cols + pair_cols), jnp.bfloat16),
            pltpu.VMEM((rows // 2, query_cols + pair_cols), jnp.bfloat16),
            pltpu.VMEM((rows, query_cols), jnp.float32),
            pltpu.SemaphoreType.DMA((2 + len(blocks),)),
            pltpu.SemaphoreType.DMA((2 * (1 + len(chunks)),)),
        ],
        compiler_params=pltpu.CompilerParams(vmem_limit_bytes=62 * 1024 * 1024),
        cost_estimate=pl.CostEstimate(
            flops=2 * rows * width * (query_cols + pair_cols),
            bytes_accessed=2 * width * (query_cols + pair_cols),
            transcendentals=0,
        ),
        name="project",
    )(tokens, w_query, w_keyval)


def near_kernel(after_ref, source_ref, target_ref, token_ref, sem):
    copy = pltpu.make_async_copy(source_ref, target_ref, sem)
    copy.start()
    copy.wait()
    token_ref[...] = jnp.zeros_like(token_ref)


def near(after, array):
    anywhere = pl.BlockSpec(memory_space=pl.ANY)
    return pl.pallas_call(
        near_kernel,
        out_shape=(
            jax.ShapeDtypeStruct(array.shape, array.dtype),
            jax.ShapeDtypeStruct((8, 128), jnp.float32),
        ),
        in_specs=[anywhere, anywhere],
        out_specs=(anywhere, pl.BlockSpec(memory_space=pltpu.VMEM)),
        scratch_shapes=[pltpu.SemaphoreType.DMA],
        compiler_params=pltpu.CompilerParams(vmem_limit_bytes=36 * 1024 * 1024),
        cost_estimate=pl.CostEstimate(
            flops=0, bytes_accessed=2 * array.size * array.dtype.itemsize, transcendentals=0
        ),
        name="near",
    )(after, array)


def staged_kernel(source_ref, target_ref):
    target_ref[...] = source_ref[...]


def staged(array):
    vmem = pl.BlockSpec(memory_space=pltpu.VMEM)
    return pl.pallas_call(
        staged_kernel,
        out_shape=jax.ShapeDtypeStruct(array.shape, array.dtype),
        in_specs=[vmem],
        out_specs=vmem,
        compiler_params=pltpu.CompilerParams(vmem_limit_bytes=8 * 1024 * 1024),
        name="staged",
    )(array)


def combine_kernel(dims, kept_ref, taken_ref, own_ref, *sends):
    batch_count, high_count, block = dims
    for db in range(batch_count):
        for dh in range(high_count):
            at = ((lax.axis_index("batch") ^ db) * high_count + (lax.axis_index("gh") ^ dh)) * block
            window = pl.ds(pl.multiple_of(at, block), block)
            total = kept_ref[window].astype(jnp.float32) + taken_ref[window].astype(jnp.float32)
            target = sends[db * high_count + dh - 1] if db or dh else own_ref
            target[...] = total.astype(target.dtype)


def combine(kept, taken, dims):
    batch_count, high_count, block = dims
    cols = kept.shape[1]
    vmem = pl.BlockSpec(memory_space=pltpu.VMEM)
    count = batch_count * high_count
    return pl.pallas_call(
        functools.partial(combine_kernel, dims),
        out_shape=[jax.ShapeDtypeStruct((block, cols), jnp.float32)]
        + [jax.ShapeDtypeStruct((block, cols), jnp.bfloat16)] * (count - 1),
        in_specs=[vmem, vmem],
        out_specs=[vmem] * count,
        compiler_params=pltpu.CompilerParams(vmem_limit_bytes=8 * 1024 * 1024),
        name="combine",
    )(kept, taken)


def collect_kernel(count, own_ref, after_ref, *refs):
    received, outs, total_ref = refs[: -count - 1], refs[-count - 1 : -1], refs[-1]
    total = own_ref[...]
    for other in received:
        total = total + other[...].astype(jnp.float32)
    rows = outs[0].shape[0]
    for g in range(count):
        total_ref[g] = total[g * rows : (g + 1) * rows]
    for k in range(count):
        outs[k][...] = total_ref[lax.axis_index("gx") ^ k].astype(jnp.bfloat16)


def collect(own, received, after, gx_count):
    block, cols = own.shape
    rows = block // gx_count
    vmem = pl.BlockSpec(memory_space=pltpu.VMEM)
    return pl.pallas_call(
        functools.partial(collect_kernel, gx_count),
        out_shape=[jax.ShapeDtypeStruct((rows, cols), jnp.bfloat16)] * gx_count,
        in_specs=[vmem, pl.BlockSpec(memory_space=pl.ANY)]
        + [vmem] * len(received),
        out_specs=[vmem] * gx_count,
        scratch_shapes=[pltpu.VMEM((gx_count, rows, cols), jnp.float32)],
        compiler_params=pltpu.CompilerParams(vmem_limit_bytes=8 * 1024 * 1024),
        name="collect",
    )(own, after, *received[::-1])


def attend_kernel(dims, mask_ref, cos_ref, sin_ref, keys_ref, values_ref, *refs):
    gx_count, owned, steps, heads, width = dims
    blocks, outs = [None] * gx_count, refs[gx_count:-2]
    for k, ref in zip(farther_first(gx_count), refs):
        blocks[k] = ref
    rows_ref, result_ref = refs[-2:]
    query_cols = heads * width
    half = width // 2
    scaling = 1.0 / width**0.5
    count = gx_count * heads * steps
    cosine = jnp.concatenate([cos_ref[s] for s in range(owned)], axis=0)
    sine = jnp.concatenate([sin_ref[s] for s in range(owned)], axis=0)

    def turn(first, second):
        return first * cosine - second * sine, second * cosine + first * sine

    key_value = [ref[:, pl.ds(query_cols, ref.shape[1] - query_cols)].astype(jnp.float32) for ref in blocks]
    key_value = jnp.concatenate(unxored(key_value, lax.axis_index("gx")), axis=1)
    new_values = key_value[:, width:]
    new_keys = turn(key_value[:, :half], key_value[:, half:width])
    new_keys = jnp.concatenate(new_keys, axis=1).astype(jnp.bfloat16).astype(jnp.float32)
    for k in range(gx_count):
        for h in range(heads):
            first = blocks[k][:, pl.ds(h * width, half)].astype(jnp.float32)
            second = blocks[k][:, pl.ds(h * width + half, half)].astype(jnp.float32)
            for part, value in enumerate(turn(first, second)):
                for s in range(owned):
                    window = pl.ds((k * heads + h) * steps, steps)
                    rows_ref[s, window, pl.ds(part * half, half)] = value[s * steps : (s + 1) * steps]
    step_of = lax.broadcasted_iota(jnp.int32, (count, 1), 0) % steps
    for s in range(owned):
        queries = rows_ref[s].astype(jnp.bfloat16)
        cached = lax.dot_general(
            queries, keys_ref[s], (((1,), (1,)), ((), ())), preferred_element_type=jnp.float32
        )
        cached = cached * scaling + mask_ref[s]
        highest = cached.max(-1, keepdims=True)
        wide = queries.astype(jnp.float32)
        fresh = []
        for u in range(steps):
            row = s * steps + u
            score = (wide * new_keys[row : row + 1]).sum(-1, keepdims=True) * scaling
            fresh.append(jnp.where(step_of >= u, score, -1e30))
            highest = jnp.maximum(highest, fresh[-1])
        exp_cached = jnp.exp(cached - highest)
        denom = exp_cached.sum(-1, keepdims=True)
        total = jnp.dot(
            exp_cached.astype(jnp.bfloat16), values_ref[s], preferred_element_type=jnp.float32
        )
        for u in range(steps):
            row = s * steps + u
            exp_fresh = jnp.exp(fresh[u] - highest)
            denom = denom + exp_fresh
            total = total + exp_fresh * new_values[row : row + 1]
        result_ref[s] = total / denom
    for k in range(gx_count):
        for h in range(heads):
            window = pl.ds((k * heads + h) * steps, steps)
            value = jnp.concatenate([result_ref[s, window] for s in range(owned)], axis=0)
            outs[k][:, pl.ds(h * width, width)] = value.astype(jnp.bfloat16)


def attend(blocks, cache_keys, cache_values, lengths, query_cols):
    gx_count = len(blocks)
    owned, slots, width = cache_keys.shape
    rows = blocks[0].shape[0]
    steps = rows // owned
    heads = query_cols // width
    count = gx_count * heads * steps
    freqs = 10000.0 ** (-(jnp.arange(width // 2, dtype=jnp.float32) * 2.0 / width))
    positions = lengths[:, None, None] + jnp.arange(steps, dtype=jnp.int32)[None, :, None]
    angles = positions.astype(jnp.float32) * freqs
    mask = jnp.where(jnp.arange(slots)[None, None, :] < lengths[:, None, None], 0.0, -1e30)
    vmem = pl.BlockSpec(memory_space=pltpu.VMEM)
    return pl.pallas_call(
        functools.partial(attend_kernel, (gx_count, owned, steps, heads, width)),
        out_shape=[jax.ShapeDtypeStruct((rows, query_cols), jnp.bfloat16)] * gx_count,
        in_specs=[vmem] * (5 + gx_count),
        out_specs=[vmem] * gx_count,
        scratch_shapes=[
            pltpu.VMEM((owned, count, width), jnp.float32),
            pltpu.VMEM((owned, count, width), jnp.float32),
        ],
        compiler_params=pltpu.CompilerParams(vmem_limit_bytes=12 * 1024 * 1024),
        cost_estimate=pl.CostEstimate(
            flops=4 * owned * count * slots * width,
            bytes_accessed=4 * owned * slots * width,
            transcendentals=owned * count * slots,
        ),
        name="attend",
    )(mask, jnp.cos(angles), jnp.sin(angles), cache_keys, cache_values, *[blocks[k] for k in farther_first(gx_count)])


def order_kernel(*refs):
    blocks, (out_ref, sorted_ref) = refs[:-2], refs[-2:]
    for k, block in enumerate(blocks):
        sorted_ref[lax.axis_index("gx") ^ k] = block[...].astype(jnp.float32)
    parts = [sorted_ref[g] for g in range(len(blocks))]
    out_ref[...] = jnp.concatenate(parts, axis=0).astype(out_ref.dtype)


def order(blocks):
    vmem = pl.BlockSpec(memory_space=pltpu.VMEM)
    rows, cols = blocks[0].shape
    count = len(blocks)
    turn = lambda *refs: order_kernel(refs[0], *refs[count - 1 : 0 : -1], *refs[count:])
    return pl.pallas_call(
        turn,
        out_shape=jax.ShapeDtypeStruct((count * rows, cols), blocks[0].dtype),
        in_specs=[vmem] * count,
        out_specs=vmem,
        scratch_shapes=[pltpu.VMEM((count, rows, cols), jnp.float32)],
        compiler_params=pltpu.CompilerParams(vmem_limit_bytes=8 * 1024 * 1024),
        name="order",
    )(blocks[0], *blocks[:0:-1])


def mix_kernel(dims, chunk, part, weight_ref, *refs):
    batch_count, gx_count, high_count, block = dims
    count = 2 * batch_count * high_count
    blocks, own_ref, sends, (rows_ref, sum_ref) = refs[:count][::-1], refs[count], refs[count + 1 : -2], refs[-2:]
    shards = gx_count // batch_count
    group = block // shards
    for relative in range(2):
        for db in range(batch_count):
            for dh in range(high_count):
                b, h = lax.axis_index("batch") ^ db, lax.axis_index("gh") ^ dh
                at = ((relative * batch_count + b) * high_count + h) * block
                source = blocks[(relative * batch_count + db) * high_count + dh]
                rows_ref[pl.ds(pl.multiple_of(at, block), block)] = source[...]
    lhs = rows_ref[...]
    first, out_cols = part
    for start in range(0, out_cols, chunk):
        size = min(chunk, out_cols - start)
        window = pl.ds(start, size)
        sum_ref[:, pl.ds(0, size)] = jnp.dot(
            lhs, weight_ref[:, pl.ds(first + start, size)], preferred_element_type=jnp.float32
        )
        for k in range(gx_count):
            shard = lax.axis_index("gx") ^ k
            b, hi = shard // shards, shard % shards
            parts = []
            for relative in range(2):
                for h in range(high_count):
                    at = ((relative * batch_count + b) * high_count + h) * block + hi * group
                    at = pl.multiple_of(at, group)
                    parts.append(sum_ref[pl.ds(at, group), pl.ds(0, size)])
            piece = jnp.concatenate(parts, axis=0)
            target = own_ref if k == 0 else sends[k - 1]
            target[:, window] = piece.astype(target.dtype)


def mix(blocks, w_out, dims, part):
    batch_count, gx_count, high_count, block = dims
    depth = w_out.shape[0]
    out_cols = part[1]
    rows = len(blocks) * block
    chunk = min(768, out_cols)
    vmem = pl.BlockSpec(memory_space=pltpu.VMEM)
    kept = (0, 2) if gx_count == 4 else (0,)
    shapes = [
        jax.ShapeDtypeStruct((rows // gx_count, out_cols), jnp.float32 if k in kept else jnp.bfloat16)
        for k in range(gx_count)
    ]
    return pl.pallas_call(
        functools.partial(mix_kernel, dims, chunk, part),
        out_shape=shapes,
        in_specs=[vmem] * (1 + len(blocks)),
        out_specs=[vmem] * gx_count,
        scratch_shapes=[pltpu.VMEM((rows, depth), jnp.bfloat16), pltpu.VMEM((rows, chunk), jnp.float32)],
        compiler_params=pltpu.CompilerParams(vmem_limit_bytes=20 * 1024 * 1024),
        cost_estimate=pl.CostEstimate(
            flops=2 * rows * depth * out_cols, bytes_accessed=2 * depth * out_cols, transcendentals=0
        ),
        name="mix",
    )(w_out, *blocks[::-1])


def relay_kernel(own_ref, taken_ref, near_ref, sum_ref, copy_ref):
    total = own_ref[...] + taken_ref[...].astype(jnp.float32)
    sum_ref[...] = total.astype(sum_ref.dtype)
    copy_ref[...] = near_ref[...]


def relay(own, taken, near):
    vmem = pl.BlockSpec(memory_space=pltpu.VMEM)
    return pl.pallas_call(
        relay_kernel,
        out_shape=[jax.ShapeDtypeStruct(near.shape, near.dtype)] * 2,
        in_specs=[vmem] * 3,
        out_specs=[vmem] * 2,
        compiler_params=pltpu.CompilerParams(vmem_limit_bytes=8 * 1024 * 1024),
        name="relay",
    )(own, taken, near)


def summed_terms(sends):
    count = len(sends) + 1
    if count != 4:
        return [swapped_with(sends[k - 1], "gx", (count,), (k,)) for k in farther_first(count)[1:]]
    near, far, farthest = sends
    taken = swapped_with(farthest, "gx", (count,), (1,))
    both, near = relay(far, taken, near)
    return [swapped_with(both, "gx", (count,), (2,)), swapped_with(near, "gx", (count,), (1,))]


def finish_kernel(dims, own_ref, *refs):
    received, out_ref = refs[: len(refs) - 1], refs[-1]
    batch_count, high_count, owned = dims
    steps, out_cols = out_ref.shape[1:]
    size = batch_count * owned * steps
    received = [ref for ref in received if ref.shape == own_ref.shape]
    for relative in range(2):
        low = lax.axis_index("gl") ^ relative
        for h in range(high_count):
            window = pl.ds((relative * high_count + h) * size, size)
            total = own_ref[window]
            for other in received:
                total = total + other[window].astype(jnp.float32)
            total = total.reshape(batch_count, owned, steps, out_cols).astype(jnp.bfloat16)
            for g in range(batch_count):
                first = ((g * high_count + h) * 2 + low) * owned
                out_ref[pl.ds(first, owned)] = total[g]


def finish(own, received, dims, steps, part, parts, before):
    rows, out_cols = own.shape
    whole = pl.BlockSpec((rows, out_cols), lambda step: (0, 0))
    operands = [own, *received]
    in_specs = [whole] * len(operands)
    aliases = {}
    if before is not None:
        aliases[len(operands)] = 0
        operands.append(before)
        in_specs.append(pl.BlockSpec(memory_space=pl.ANY))
    return pl.pallas_call(
        functools.partial(finish_kernel, dims),
        grid=(1,),
        out_shape=jax.ShapeDtypeStruct((rows // steps, steps, out_cols * parts), jnp.bfloat16),
        in_specs=in_specs,
        out_specs=pl.BlockSpec((rows // steps, steps, out_cols), lambda step: (0, 0, part)),
        input_output_aliases=aliases,
        compiler_params=pltpu.CompilerParams(vmem_limit_bytes=16 * 1024 * 1024),
        name="finish",
    )(*operands)


def local(tokens, w_query, w_keyval, w_out, cache_keys, cache_values, lengths):
    batch_count = lax.axis_size("batch")
    gx_count = lax.axis_size("gx")
    high_count = lax.axis_size("gh")
    sizes = (batch_count, high_count, 2)
    owned = cache_keys.shape[0]
    sequences, steps, width = tokens.shape
    query_cols = w_query.shape[1]
    rows = owned * steps
    rows_here = gx_count * rows

    kept, given = project(tokens, w_query, w_keyval, (batch_count, gx_count, high_count, owned))
    taken = swapped_with(given, PLANE, sizes, (0, 0, 1))
    far = [(db, dh) for db in range(batch_count) for dh in range(high_count)][1:]
    own, *sends = combine(staged(kept), taken, (batch_count, high_count, rows_here))
    received = [
        swapped_with(block, PLANE, sizes, (db, dh, 0)) for block, (db, dh) in zip(sends, far)
    ]
    w_out, token = near(own, w_out)
    blocks = collect(own, received, token, gx_count)
    blocks = [blocks[0]] + [
        swapped_with(blocks[k], "gx", (gx_count,), (k,)) for k in range(1, gx_count)
    ]
    blocks = attend(blocks, cache_keys, cache_values, lengths, query_cols)
    blocks = [blocks[0]] + [
        swapped_with(blocks[k], "gx", (gx_count,), (k,)) for k in range(1, gx_count)
    ]
    grouped = order(blocks)

    ours = [grouped] + [swapped_with(grouped, PLANE, sizes, (db, dh, 0)) for db, dh in far]
    theirs = [swapped_with(block, PLANE, sizes, (0, 0, 1)) for block in ours]
    out_cols = w_out.shape[1]
    parts = 2 if out_cols % (2 * 128) == 0 else 1
    size = out_cols // parts
    mixed = None
    products = [
        mix(ours + theirs, w_out, (batch_count, gx_count, high_count, rows_here), (part * size, size))
        for part in range(parts)
    ]
    for part, (own, *sends) in enumerate(products):
        received = summed_terms(sends)
        mixed = finish(own, received, (batch_count, high_count, owned), steps, part, parts, mixed)
    return mixed


def solution(mesh):
    batch_count, gx_count, gy_count = mesh.devices.shape
    split = Mesh(
        mesh.devices.reshape(batch_count, gx_count, gy_count // 2, 2), ("batch", "gx", "gh", "gl")
    )
    plane = ("batch", "gh", "gl")
    placed = (
        P(None, None, plane),
        P(plane, "gx"),
        P(plane, "gx"),
        P("gx", plane),
        P(("batch", "gx", "gh", "gl"), None, None),
        P(("batch", "gx", "gh", "gl"), None, None),
        P(("batch", "gx", "gh", "gl")),
    )
    return jax.shard_map(
        local, mesh=split, in_specs=placed, out_specs=P("gx", None, plane), check_vma=False
    )
```

```python
import functools

import jax
import jax.numpy as jnp
import numpy as np
from jax import lax
from jax.experimental import pallas as pl
from jax.experimental.pallas import tpu as pltpu
from jax.sharding import Mesh
from jax.sharding import PartitionSpec as P

PLANE = ("batch", "gh", "gl")


def swapped_with(value, axes, sizes, differs):
    pairs = []
    for place in np.ndindex(*sizes):
        target = tuple(p ^ d for p, d in zip(place, differs))
        pairs.append((int(np.ravel_multi_index(place, sizes)), int(np.ravel_multi_index(target, sizes))))
    return lax.ppermute(value, axes, pairs)


def unxored(blocks, here):
    count = len(blocks)
    bit = 1
    while bit < count:
        turn = (here & bit) != 0
        blocks = [jnp.where(turn, blocks[k ^ bit], blocks[k]) for k in range(count)]
        bit *= 2
    return blocks


def farther_first(count):
    return [0, *range(2, count), 1]


def project_kernel(
    dims, blocks, chunks, tokens_hbm, query_hbm, pair_hbm, kept_out, given_out,
    tokens_ref, rows_ref, query_ref, pair_ref, kept_ref, given_ref, sum_ref, sems, out_sems,
):
    batch_count, gx_count, high_count, owned = dims
    query_cols = query_ref.shape[1]
    copies = [
        pltpu.make_async_copy(tokens_hbm, tokens_ref, sems.at[0]),
        pltpu.make_async_copy(pair_hbm, pair_ref, sems.at[1]),
    ]
    for place, (start, size) in enumerate(blocks):
        window = pl.ds(start, size)
        copies.append(pltpu.make_async_copy(query_hbm.at[window], query_ref.at[window], sems.at[place + 2]))
    for copy in copies:
        copy.start()
    steps, width = tokens_ref.shape[1:]
    block = gx_count * owned * steps
    half = rows_ref.shape[0] // 2
    copies[0].wait()
    for relative in range(2):
        low = lax.axis_index("gl") ^ relative
        for b in range(batch_count):
            for h in range(high_count):
                parts = []
                for g in range(gx_count):
                    first = (((b * gx_count + g) * high_count + h) * 2 + low) * owned
                    parts.append(tokens_ref[pl.ds(first, owned)])
                joined = jnp.concatenate(parts, axis=0).reshape(block, width)
                at = ((relative * batch_count + b) * high_count + h) * block
                rows_ref[pl.ds(at, block)] = joined
    writes = []

    def emit(product, start):
        product = product.astype(jnp.bfloat16)
        window = pl.ds(start, product.shape[1])
        kept_ref[:, window] = product[:half]
        given_ref[:, window] = product[half:]
        for source, target in ((given_ref, given_out), (kept_ref, kept_out)):
            copy = pltpu.make_async_copy(source.at[:, window], target.at[:, window], out_sems.at[len(writes)])
            copy.start()
            writes.append(copy)

    copies[1].wait()
    emit(jnp.dot(rows_ref[...], pair_ref[...], preferred_element_type=jnp.float32), query_cols)
    for place, (depth_at, depth) in enumerate(blocks):
        copies[2 + place].wait()
        rows = rows_ref[:, pl.ds(depth_at, depth)]
        for start, size in chunks:
            window = pl.ds(start, size)
            term = jnp.dot(
                rows, query_ref[pl.ds(depth_at, depth), window], preferred_element_type=jnp.float32
            )
            if place > 0:
                term = term + sum_ref[:, window]
            if place < len(blocks) - 1:
                sum_ref[:, window] = term
            else:
                emit(term, start)
    for copy in writes:
        copy.wait()


def cut(total, sizes):
    windows, start = [], 0
    while start < total:
        size = min(sizes[min(len(windows), len(sizes) - 1)], total - start)
        windows.append((start, size))
        start += size
    return windows


def project(tokens, w_query, w_keyval, dims):
    sequences, steps, width = tokens.shape
    query_cols, pair_cols = w_query.shape[1], w_keyval.shape[1]
    rows = sequences * steps
    blocks = cut(width, (768, 768, 512, 256))
    chunks = cut(query_cols, (768,))
    hbm = pl.BlockSpec(memory_space=pltpu.HBM)
    shape = jax.ShapeDtypeStruct((rows // 2, query_cols + pair_cols), jnp.bfloat16)
    return pl.pallas_call(
        functools.partial(project_kernel, dims, blocks, chunks),
        out_shape=(shape, shape),
        in_specs=[hbm, hbm, hbm],
        out_specs=(hbm, hbm),
        scratch_shapes=[
            pltpu.VMEM(tokens.shape, jnp.bfloat16),
            pltpu.VMEM((rows, width), jnp.bfloat16),
            pltpu.VMEM((width, query_cols), jnp.bfloat16),
            pltpu.VMEM((width, pair_cols), jnp.bfloat16),
            pltpu.VMEM((rows // 2, query_cols + pair_cols), jnp.bfloat16),
            pltpu.VMEM((rows // 2, query_cols + pair_cols), jnp.bfloat16),
            pltpu.VMEM((rows, query_cols), jnp.float32),
            pltpu.SemaphoreType.DMA((2 + len(blocks),)),
            pltpu.SemaphoreType.DMA((2 * (1 + len(chunks)),)),
        ],
        compiler_params=pltpu.CompilerParams(vmem_limit_bytes=62 * 1024 * 1024),
        cost_estimate=pl.CostEstimate(
            flops=2 * rows * width * (query_cols + pair_cols),
            bytes_accessed=2 * width * (query_cols + pair_cols),
            transcendentals=0,
        ),
        name="project",
    )(tokens, w_query, w_keyval)


def near_kernel(after_ref, source_ref, target_ref, token_ref, sem):
    copy = pltpu.make_async_copy(source_ref, target_ref, sem)
    copy.start()
    copy.wait()
    token_ref[...] = jnp.zeros_like(token_ref)


def near(after, array):
    anywhere = pl.BlockSpec(memory_space=pl.ANY)
    return pl.pallas_call(
        near_kernel,
        out_shape=(
            jax.ShapeDtypeStruct(array.shape, array.dtype),
            jax.ShapeDtypeStruct((8, 128), jnp.float32),
        ),
        in_specs=[anywhere, anywhere],
        out_specs=(anywhere, pl.BlockSpec(memory_space=pltpu.VMEM)),
        scratch_shapes=[pltpu.SemaphoreType.DMA],
        compiler_params=pltpu.CompilerParams(vmem_limit_bytes=36 * 1024 * 1024),
        cost_estimate=pl.CostEstimate(
            flops=0, bytes_accessed=2 * array.size * array.dtype.itemsize, transcendentals=0
        ),
        name="near",
    )(after, array)


def staged_kernel(source_ref, target_ref):
    target_ref[...] = source_ref[...]


def staged(array):
    vmem = pl.BlockSpec(memory_space=pltpu.VMEM)
    return pl.pallas_call(
        staged_kernel,
        out_shape=jax.ShapeDtypeStruct(array.shape, array.dtype),
        in_specs=[vmem],
        out_specs=vmem,
        compiler_params=pltpu.CompilerParams(vmem_limit_bytes=8 * 1024 * 1024),
        name="staged",
    )(array)


def combine_kernel(dims, kept_ref, taken_ref, own_ref, *sends):
    batch_count, high_count, block = dims
    for db in range(batch_count):
        for dh in range(high_count):
            at = ((lax.axis_index("batch") ^ db) * high_count + (lax.axis_index("gh") ^ dh)) * block
            window = pl.ds(pl.multiple_of(at, block), block)
            total = kept_ref[window].astype(jnp.float32) + taken_ref[window].astype(jnp.float32)
            target = sends[db * high_count + dh - 1] if db or dh else own_ref
            target[...] = total.astype(target.dtype)


def combine(kept, taken, dims):
    batch_count, high_count, block = dims
    cols = kept.shape[1]
    vmem = pl.BlockSpec(memory_space=pltpu.VMEM)
    count = batch_count * high_count
    return pl.pallas_call(
        functools.partial(combine_kernel, dims),
        out_shape=[jax.ShapeDtypeStruct((block, cols), jnp.float32)]
        + [jax.ShapeDtypeStruct((block, cols), jnp.bfloat16)] * (count - 1),
        in_specs=[vmem, vmem],
        out_specs=[vmem] * count,
        compiler_params=pltpu.CompilerParams(vmem_limit_bytes=8 * 1024 * 1024),
        name="combine",
    )(kept, taken)


def collect_kernel(count, own_ref, after_ref, *refs):
    received, outs, total_ref = refs[: -count - 1], refs[-count - 1 : -1], refs[-1]
    total = own_ref[...]
    for other in received:
        total = total + other[...].astype(jnp.float32)
    rows = outs[0].shape[0]
    for g in range(count):
        total_ref[g] = total[g * rows : (g + 1) * rows]
    for k in range(count):
        outs[k][...] = total_ref[lax.axis_index("gx") ^ k].astype(jnp.bfloat16)


def collect(own, received, after, gx_count):
    block, cols = own.shape
    rows = block // gx_count
    vmem = pl.BlockSpec(memory_space=pltpu.VMEM)
    return pl.pallas_call(
        functools.partial(collect_kernel, gx_count),
        out_shape=[jax.ShapeDtypeStruct((rows, cols), jnp.bfloat16)] * gx_count,
        in_specs=[vmem, pl.BlockSpec(memory_space=pl.ANY)]
        + [vmem] * len(received),
        out_specs=[vmem] * gx_count,
        scratch_shapes=[pltpu.VMEM((gx_count, rows, cols), jnp.float32)],
        compiler_params=pltpu.CompilerParams(vmem_limit_bytes=8 * 1024 * 1024),
        name="collect",
    )(own, after, *received)


def attend_kernel(dims, mask_ref, cos_ref, sin_ref, keys_ref, values_ref, *refs):
    gx_count, owned, steps, heads, width = dims
    blocks, outs = [None] * gx_count, refs[gx_count:-2]
    for k, ref in zip(farther_first(gx_count), refs):
        blocks[k] = ref
    rows_ref, result_ref = refs[-2:]
    query_cols = heads * width
    half = width // 2
    scaling = 1.0 / width**0.5
    count = gx_count * heads * steps
    cosine = jnp.concatenate([cos_ref[s] for s in range(owned)], axis=0)
    sine = jnp.concatenate([sin_ref[s] for s in range(owned)], axis=0)

    def turn(first, second, cosine, sine):
        return first * cosine - second * sine, second * cosine + first * sine

    scaled = (cosine * scaling, sine * scaling)

    key_value = [ref[:, pl.ds(query_cols, ref.shape[1] - query_cols)].astype(jnp.float32) for ref in blocks]
    key_value = jnp.concatenate(unxored(key_value, lax.axis_index("gx")), axis=1)
    new_values = key_value[:, width:]
    new_keys = turn(key_value[:, :half], key_value[:, half:width], cosine, sine)
    new_keys = jnp.concatenate(new_keys, axis=1).astype(jnp.bfloat16).astype(jnp.float32)
    for k in range(gx_count):
        for h in range(heads):
            first = blocks[k][:, pl.ds(h * width, half)].astype(jnp.float32)
            second = blocks[k][:, pl.ds(h * width + half, half)].astype(jnp.float32)
            for part, value in enumerate(turn(first, second, *scaled)):
                for s in range(owned):
                    window = pl.ds((k * heads + h) * steps, steps)
                    rows_ref[s, window, pl.ds(part * half, half)] = value[s * steps : (s + 1) * steps]
    step_of = lax.broadcasted_iota(jnp.int32, (count, 1), 0) % steps
    for s in range(owned):
        queries = rows_ref[s].astype(jnp.bfloat16)
        cached = lax.dot_general(
            queries, keys_ref[s], (((1,), (1,)), ((), ())), preferred_element_type=jnp.float32
        )
        cached = cached + mask_ref[s]
        highest = cached.max(-1, keepdims=True)
        wide = queries.astype(jnp.float32)
        fresh = []
        for u in range(steps):
            row = s * steps + u
            score = (wide * new_keys[row : row + 1]).sum(-1, keepdims=True)
            fresh.append(jnp.where(step_of >= u, score, -1e30))
            highest = jnp.maximum(highest, fresh[-1])
        exp_cached = jnp.exp(cached - highest)
        denom = exp_cached.sum(-1, keepdims=True)
        total = jnp.dot(
            exp_cached.astype(jnp.bfloat16), values_ref[s], preferred_element_type=jnp.float32
        )
        for u in range(steps):
            row = s * steps + u
            exp_fresh = jnp.exp(fresh[u] - highest)
            denom = denom + exp_fresh
            total = total + exp_fresh * new_values[row : row + 1]
        result_ref[s] = total * (1.0 / denom)
    for k in range(gx_count):
        for h in range(heads):
            window = pl.ds((k * heads + h) * steps, steps)
            value = jnp.concatenate([result_ref[s, window] for s in range(owned)], axis=0)
            outs[k][:, pl.ds(h * width, width)] = value.astype(jnp.bfloat16)


def attend(blocks, cache_keys, cache_values, lengths, query_cols):
    gx_count = len(blocks)
    owned, slots, width = cache_keys.shape
    rows = blocks[0].shape[0]
    steps = rows // owned
    heads = query_cols // width
    count = gx_count * heads * steps
    freqs = 10000.0 ** (-(jnp.arange(width // 2, dtype=jnp.float32) * 2.0 / width))
    positions = lengths[:, None, None] + jnp.arange(steps, dtype=jnp.int32)[None, :, None]
    angles = positions.astype(jnp.float32) * freqs
    mask = jnp.where(jnp.arange(slots)[None, None, :] < lengths[:, None, None], 0.0, -1e30)
    vmem = pl.BlockSpec(memory_space=pltpu.VMEM)
    return pl.pallas_call(
        functools.partial(attend_kernel, (gx_count, owned, steps, heads, width)),
        out_shape=[jax.ShapeDtypeStruct((rows, query_cols), jnp.bfloat16)] * gx_count,
        in_specs=[vmem] * (5 + gx_count),
        out_specs=[vmem] * gx_count,
        scratch_shapes=[
            pltpu.VMEM((owned, count, width), jnp.float32),
            pltpu.VMEM((owned, count, width), jnp.float32),
        ],
        compiler_params=pltpu.CompilerParams(vmem_limit_bytes=12 * 1024 * 1024),
        cost_estimate=pl.CostEstimate(
            flops=4 * owned * count * slots * width,
            bytes_accessed=4 * owned * slots * width,
            transcendentals=owned * count * slots,
        ),
        name="attend",
    )(mask, jnp.cos(angles), jnp.sin(angles), cache_keys, cache_values, *[blocks[k] for k in farther_first(gx_count)])


def order_kernel(distances, *refs):
    out_ref, sorted_ref = refs[-2:]
    for k, block in zip(distances, refs):
        sorted_ref[lax.axis_index("gx") ^ k] = block[...].astype(jnp.float32)
    parts = [sorted_ref[g] for g in range(len(distances))]
    out_ref[...] = jnp.concatenate(parts, axis=0).astype(out_ref.dtype)


def order(blocks):
    vmem = pl.BlockSpec(memory_space=pltpu.VMEM)
    rows, cols = blocks[0].shape
    count = len(blocks)
    distances = farther_first(count)
    return pl.pallas_call(
        functools.partial(order_kernel, distances),
        out_shape=jax.ShapeDtypeStruct((count * rows, cols), blocks[0].dtype),
        in_specs=[vmem] * count,
        out_specs=vmem,
        scratch_shapes=[pltpu.VMEM((count, rows, cols), jnp.float32)],
        compiler_params=pltpu.CompilerParams(vmem_limit_bytes=8 * 1024 * 1024),
        name="order",
    )(*[blocks[k] for k in distances])


def mix_kernel(dims, chunk, part, weight_ref, *refs):
    batch_count, gx_count, high_count, block = dims
    count = 2 * batch_count * high_count
    blocks, own_ref, sends, (rows_ref, sum_ref) = refs[:count][::-1], refs[count], refs[count + 1 : -2], refs[-2:]
    shards = gx_count // batch_count
    group = block // shards
    for relative in range(2):
        for db in range(batch_count):
            for dh in range(high_count):
                b, h = lax.axis_index("batch") ^ db, lax.axis_index("gh") ^ dh
                at = ((relative * batch_count + b) * high_count + h) * block
                source = blocks[(relative * batch_count + db) * high_count + dh]
                rows_ref[pl.ds(pl.multiple_of(at, block), block)] = source[...]
    lhs = rows_ref[...]
    first, out_cols = part
    for start in range(0, out_cols, chunk):
        size = min(chunk, out_cols - start)
        window = pl.ds(start, size)
        sum_ref[:, pl.ds(0, size)] = jnp.dot(
            lhs, weight_ref[:, pl.ds(first + start, size)], preferred_element_type=jnp.float32
        )
        for k in range(gx_count):
            shard = lax.axis_index("gx") ^ k
            b, hi = shard // shards, shard % shards
            parts = []
            for relative in range(2):
                for h in range(high_count):
                    at = ((relative * batch_count + b) * high_count + h) * block + hi * group
                    at = pl.multiple_of(at, group)
                    parts.append(sum_ref[pl.ds(at, group), pl.ds(0, size)])
            piece = jnp.concatenate(parts, axis=0)
            target = own_ref if k == 0 else sends[k - 1]
            target[:, window] = piece.astype(target.dtype)


def mix(blocks, w_out, dims, part):
    batch_count, gx_count, high_count, block = dims
    depth = w_out.shape[0]
    out_cols = part[1]
    rows = len(blocks) * block
    chunk = min(768, out_cols)
    vmem = pl.BlockSpec(memory_space=pltpu.VMEM)
    kept = (0, 2) if gx_count == 4 else (0,)
    shapes = [
        jax.ShapeDtypeStruct((rows // gx_count, out_cols), jnp.float32 if k in kept else jnp.bfloat16)
        for k in range(gx_count)
    ]
    return pl.pallas_call(
        functools.partial(mix_kernel, dims, chunk, part),
        out_shape=shapes,
        in_specs=[vmem] * (1 + len(blocks)),
        out_specs=[vmem] * gx_count,
        scratch_shapes=[pltpu.VMEM((rows, depth), jnp.bfloat16), pltpu.VMEM((rows, chunk), jnp.float32)],
        compiler_params=pltpu.CompilerParams(vmem_limit_bytes=20 * 1024 * 1024),
        cost_estimate=pl.CostEstimate(
            flops=2 * rows * depth * out_cols, bytes_accessed=2 * depth * out_cols, transcendentals=0
        ),
        name="mix",
    )(w_out, *blocks[::-1])


def relay_kernel(own_ref, taken_ref, near_ref, sum_ref, copy_ref):
    total = own_ref[...] + taken_ref[...].astype(jnp.float32)
    sum_ref[...] = total.astype(sum_ref.dtype)
    copy_ref[...] = near_ref[...]


def relay(own, taken, near):
    vmem = pl.BlockSpec(memory_space=pltpu.VMEM)
    return pl.pallas_call(
        relay_kernel,
        out_shape=[jax.ShapeDtypeStruct(near.shape, near.dtype)] * 2,
        in_specs=[vmem] * 3,
        out_specs=[vmem] * 2,
        compiler_params=pltpu.CompilerParams(vmem_limit_bytes=8 * 1024 * 1024),
        name="relay",
    )(own, taken, near)


def summed_terms(sends):
    count = len(sends) + 1
    if count != 4:
        return [swapped_with(sends[k - 1], "gx", (count,), (k,)) for k in farther_first(count)[1:]]
    near, far, farthest = sends
    taken = swapped_with(farthest, "gx", (count,), (1,))
    both, near = relay(far, taken, near)
    return [swapped_with(both, "gx", (count,), (2,)), swapped_with(near, "gx", (count,), (1,))]


def finish_kernel(dims, own_ref, *refs):
    received, out_ref = refs[: len(refs) - 1], refs[-1]
    batch_count, high_count, owned = dims
    steps, out_cols = out_ref.shape[1:]
    size = batch_count * owned * steps
    received = [ref for ref in received if ref.shape == own_ref.shape]
    for relative in range(2):
        low = lax.axis_index("gl") ^ relative
        for h in range(high_count):
            window = pl.ds((relative * high_count + h) * size, size)
            total = own_ref[window]
            for other in received:
                total = total + other[window].astype(jnp.float32)
            total = total.reshape(batch_count, owned, steps, out_cols).astype(jnp.bfloat16)
            for g in range(batch_count):
                first = ((g * high_count + h) * 2 + low) * owned
                out_ref[pl.ds(first, owned)] = total[g]


def finish(own, received, dims, steps, part, parts, before):
    rows, out_cols = own.shape
    whole = pl.BlockSpec((rows, out_cols), lambda step: (0, 0))
    operands = [own, *received]
    in_specs = [whole] * len(operands)
    aliases = {}
    if before is not None:
        aliases[len(operands)] = 0
        operands.append(before)
        in_specs.append(pl.BlockSpec(memory_space=pl.ANY))
    return pl.pallas_call(
        functools.partial(finish_kernel, dims),
        grid=(1,),
        out_shape=jax.ShapeDtypeStruct((rows // steps, steps, out_cols * parts), jnp.bfloat16),
        in_specs=in_specs,
        out_specs=pl.BlockSpec((rows // steps, steps, out_cols), lambda step: (0, 0, part)),
        input_output_aliases=aliases,
        compiler_params=pltpu.CompilerParams(vmem_limit_bytes=16 * 1024 * 1024),
        name="finish",
    )(*operands)


def local(tokens, w_query, w_keyval, w_out, cache_keys, cache_values, lengths):
    batch_count = lax.axis_size("batch")
    gx_count = lax.axis_size("gx")
    high_count = lax.axis_size("gh")
    sizes = (batch_count, high_count, 2)
    owned = cache_keys.shape[0]
    sequences, steps, width = tokens.shape
    query_cols = w_query.shape[1]
    rows = owned * steps
    rows_here = gx_count * rows

    kept, given = project(tokens, w_query, w_keyval, (batch_count, gx_count, high_count, owned))
    taken = swapped_with(given, PLANE, sizes, (0, 0, 1))
    far = [(db, dh) for db in range(batch_count) for dh in range(high_count)][1:]
    own, *sends = combine(staged(kept), taken, (batch_count, high_count, rows_here))
    received = [
        swapped_with(block, PLANE, sizes, (db, dh, 0)) for block, (db, dh) in zip(sends, far)
    ]
    w_out, token = near(own, w_out)
    blocks = collect(own, received, token, gx_count)
    blocks = [blocks[0]] + [
        swapped_with(blocks[k], "gx", (gx_count,), (k,)) for k in range(1, gx_count)
    ]
    blocks = attend(blocks, cache_keys, cache_values, lengths, query_cols)
    blocks = [blocks[0]] + [
        swapped_with(blocks[k], "gx", (gx_count,), (k,)) for k in range(1, gx_count)
    ]
    grouped = order(blocks)

    ours = [grouped] + [swapped_with(grouped, PLANE, sizes, (db, dh, 0)) for db, dh in far]
    theirs = [swapped_with(block, PLANE, sizes, (0, 0, 1)) for block in ours]
    out_cols = w_out.shape[1]
    parts = 2 if out_cols % 256 == 0 else 1
    size = out_cols // parts
    mixed = None
    products = [
        mix(ours + theirs, w_out, (batch_count, gx_count, high_count, rows_here), (part * size, size))
        for part in range(parts)
    ]
    for part, (own, *sends) in enumerate(products):
        received = summed_terms(sends)
        mixed = finish(own, received, (batch_count, high_count, owned), steps, part, parts, mixed)
    return mixed


def solution(mesh):
    batch_count, gx_count, gy_count = mesh.devices.shape
    split = Mesh(
        mesh.devices.reshape(batch_count, gx_count, gy_count // 2, 2), ("batch", "gx", "gh", "gl")
    )
    plane = ("batch", "gh", "gl")
    placed = (
        P(None, None, plane),
        P(plane, "gx"),
        P(plane, "gx"),
        P("gx", plane),
        P(("batch", "gx", "gh", "gl"), None, None),
        P(("batch", "gx", "gh", "gl"), None, None),
        P(("batch", "gx", "gh", "gl")),
    )
    return jax.shard_map(
        local, mesh=split, in_specs=placed, out_specs=P("gx", None, plane), check_vma=False
    )
```

```python
import functools

import jax
import jax.numpy as jnp
import numpy as np
from jax import lax
from jax.experimental import pallas as pl
from jax.experimental.pallas import tpu as pltpu
from jax.sharding import Mesh
from jax.sharding import PartitionSpec as P

PLANE = ("batch", "gh", "gl")


def swapped_with(value, axes, sizes, differs):
    pairs = []
    for place in np.ndindex(*sizes):
        target = tuple(p ^ d for p, d in zip(place, differs))
        pairs.append((int(np.ravel_multi_index(place, sizes)), int(np.ravel_multi_index(target, sizes))))
    return lax.ppermute(value, axes, pairs)


def unxored(blocks, here):
    count = len(blocks)
    bit = 1
    while bit < count:
        turn = (here & bit) != 0
        blocks = [jnp.where(turn, blocks[k ^ bit], blocks[k]) for k in range(count)]
        bit *= 2
    return blocks


def padded(rows):
    return (rows + 7) // 8 * 8


def farther_first(count):
    return [0, *range(2, count), 1]


def project_kernel(
    dims, blocks, chunks, tokens_hbm, query_hbm, pair_hbm, kept_out, given_out,
    tokens_ref, rows_ref, query_ref, pair_ref, kept_ref, given_ref, sum_ref, sems, out_sems,
):
    batch_count, gx_count, high_count, owned = dims
    query_cols = query_ref.shape[1]
    copies = [
        pltpu.make_async_copy(tokens_hbm, tokens_ref, sems.at[0]),
        pltpu.make_async_copy(pair_hbm, pair_ref, sems.at[1]),
    ]
    for place, (start, size) in enumerate(blocks):
        window = pl.ds(start, size)
        copies.append(pltpu.make_async_copy(query_hbm.at[window], query_ref.at[window], sems.at[place + 2]))
    for copy in copies:
        copy.start()
    steps, width = tokens_ref.shape[1:]
    block = gx_count * owned * steps
    half = rows_ref.shape[0] // 2
    copies[0].wait()
    for relative in range(2):
        low = lax.axis_index("gl") ^ relative
        for b in range(batch_count):
            for h in range(high_count):
                parts = []
                for g in range(gx_count):
                    first = (((b * gx_count + g) * high_count + h) * 2 + low) * owned
                    parts.append(tokens_ref[pl.ds(first, owned)])
                joined = jnp.concatenate(parts, axis=0).reshape(block, width)
                at = ((relative * batch_count + b) * high_count + h) * block
                rows_ref[pl.ds(at, block)] = joined
    writes = []

    def emit(product, start):
        product = product.astype(jnp.bfloat16)
        window = pl.ds(start, product.shape[1])
        kept_ref[:, window] = product[:half]
        given_ref[:, window] = product[half:]
        for source, target in ((given_ref, given_out), (kept_ref, kept_out)):
            copy = pltpu.make_async_copy(source.at[:, window], target.at[:, window], out_sems.at[len(writes)])
            copy.start()
            writes.append(copy)

    copies[1].wait()
    emit(jnp.dot(rows_ref[...], pair_ref[...], preferred_element_type=jnp.float32), query_cols)
    for place, (depth_at, depth) in enumerate(blocks):
        copies[2 + place].wait()
        rows = rows_ref[:, pl.ds(depth_at, depth)]
        for start, size in chunks:
            window = pl.ds(start, size)
            term = jnp.dot(
                rows, query_ref[pl.ds(depth_at, depth), window], preferred_element_type=jnp.float32
            )
            if place > 0:
                term = term + sum_ref[:, window]
            if place < len(blocks) - 1:
                sum_ref[:, window] = term
            else:
                emit(term, start)
    for copy in writes:
        copy.wait()


def cut(total, sizes):
    windows, start = [], 0
    while start < total:
        size = min(sizes[min(len(windows), len(sizes) - 1)], total - start)
        windows.append((start, size))
        start += size
    return windows


def project(tokens, w_query, w_keyval, dims):
    sequences, steps, width = tokens.shape
    query_cols, pair_cols = w_query.shape[1], w_keyval.shape[1]
    rows = sequences * steps
    blocks = cut(width, (768, 768, 512, 256))
    chunks = cut(query_cols, (768,))
    hbm = pl.BlockSpec(memory_space=pltpu.HBM)
    shape = jax.ShapeDtypeStruct((rows // 2, query_cols + pair_cols), jnp.bfloat16)
    return pl.pallas_call(
        functools.partial(project_kernel, dims, blocks, chunks),
        out_shape=(shape, shape),
        in_specs=[hbm, hbm, hbm],
        out_specs=(hbm, hbm),
        scratch_shapes=[
            pltpu.VMEM(tokens.shape, jnp.bfloat16),
            pltpu.VMEM((rows, width), jnp.bfloat16),
            pltpu.VMEM((width, query_cols), jnp.bfloat16),
            pltpu.VMEM((width, pair_cols), jnp.bfloat16),
            pltpu.VMEM((rows // 2, query_cols + pair_cols), jnp.bfloat16),
            pltpu.VMEM((rows // 2, query_cols + pair_cols), jnp.bfloat16),
            pltpu.VMEM((rows, query_cols), jnp.float32),
            pltpu.SemaphoreType.DMA((2 + len(blocks),)),
            pltpu.SemaphoreType.DMA((2 * (1 + len(chunks)),)),
        ],
        compiler_params=pltpu.CompilerParams(vmem_limit_bytes=62 * 1024 * 1024),
        cost_estimate=pl.CostEstimate(
            flops=2 * rows * width * (query_cols + pair_cols),
            bytes_accessed=2 * width * (query_cols + pair_cols),
            transcendentals=0,
        ),
        name="project",
    )(tokens, w_query, w_keyval)


def near_kernel(after_ref, source_ref, target_ref, token_ref, sem):
    copy = pltpu.make_async_copy(source_ref, target_ref, sem)
    copy.start()
    copy.wait()
    token_ref[...] = jnp.zeros_like(token_ref)


def near(after, array):
    anywhere = pl.BlockSpec(memory_space=pl.ANY)
    return pl.pallas_call(
        near_kernel,
        out_shape=(
            jax.ShapeDtypeStruct(array.shape, array.dtype),
            jax.ShapeDtypeStruct((8, 128), jnp.float32),
        ),
        in_specs=[anywhere, anywhere],
        out_specs=(anywhere, pl.BlockSpec(memory_space=pltpu.VMEM)),
        scratch_shapes=[pltpu.SemaphoreType.DMA],
        compiler_params=pltpu.CompilerParams(vmem_limit_bytes=36 * 1024 * 1024),
        cost_estimate=pl.CostEstimate(
            flops=0, bytes_accessed=2 * array.size * array.dtype.itemsize, transcendentals=0
        ),
        name="near",
    )(after, array)


def staged_kernel(source_ref, target_ref):
    target_ref[...] = source_ref[...]


def staged(array):
    vmem = pl.BlockSpec(memory_space=pltpu.VMEM)
    return pl.pallas_call(
        staged_kernel,
        out_shape=jax.ShapeDtypeStruct(array.shape, array.dtype),
        in_specs=[vmem],
        out_specs=vmem,
        compiler_params=pltpu.CompilerParams(vmem_limit_bytes=8 * 1024 * 1024),
        name="staged",
    )(array)


def combine_kernel(dims, kept_ref, taken_ref, own_ref, *sends):
    batch_count, high_count, block = dims
    for db in range(batch_count):
        for dh in range(high_count):
            at = ((lax.axis_index("batch") ^ db) * high_count + (lax.axis_index("gh") ^ dh)) * block
            window = pl.ds(pl.multiple_of(at, block), block)
            total = kept_ref[window].astype(jnp.float32) + taken_ref[window].astype(jnp.float32)
            target = sends[db * high_count + dh - 1] if db or dh else own_ref
            target[...] = total.astype(target.dtype)


def combine(kept, taken, dims):
    batch_count, high_count, block = dims
    cols = kept.shape[1]
    vmem = pl.BlockSpec(memory_space=pltpu.VMEM)
    count = batch_count * high_count
    return pl.pallas_call(
        functools.partial(combine_kernel, dims),
        out_shape=[jax.ShapeDtypeStruct((block, cols), jnp.float32)]
        + [jax.ShapeDtypeStruct((block, cols), jnp.bfloat16)] * (count - 1),
        in_specs=[vmem, vmem],
        out_specs=[vmem] * count,
        compiler_params=pltpu.CompilerParams(vmem_limit_bytes=8 * 1024 * 1024),
        name="combine",
    )(kept, taken)


def collect_kernel(count, own_ref, after_ref, *refs):
    received, outs, total_ref = refs[: -count - 1], refs[-count - 1 : -1], refs[-1]
    total = own_ref[...]
    for other in received:
        total = total + other[...].astype(jnp.float32)
    rows = outs[0].shape[0]
    for g in range(count):
        total_ref[g, pl.ds(0, rows)] = total[g * rows : (g + 1) * rows]
    for k in range(count):
        outs[k][...] = total_ref[lax.axis_index("gx") ^ k, pl.ds(0, rows)].astype(jnp.bfloat16)


def collect(own, received, after, gx_count):
    block, cols = own.shape
    rows = block // gx_count
    vmem = pl.BlockSpec(memory_space=pltpu.VMEM)
    return pl.pallas_call(
        functools.partial(collect_kernel, gx_count),
        out_shape=[jax.ShapeDtypeStruct((rows, cols), jnp.bfloat16)] * gx_count,
        in_specs=[vmem, pl.BlockSpec(memory_space=pl.ANY)]
        + [vmem] * len(received),
        out_specs=[vmem] * gx_count,
        scratch_shapes=[pltpu.VMEM((gx_count, padded(rows), cols), jnp.float32)],
        compiler_params=pltpu.CompilerParams(vmem_limit_bytes=8 * 1024 * 1024),
        name="collect",
    )(own, after, *received)


def attend_kernel(dims, mask_ref, cos_ref, sin_ref, keys_ref, values_ref, *refs):
    gx_count, owned, steps, heads, width = dims
    blocks, outs = [None] * gx_count, refs[gx_count:-2]
    for k, ref in zip(farther_first(gx_count), refs):
        blocks[k] = ref
    rows_ref, result_ref = refs[-2:]
    query_cols = heads * width
    half = width // 2
    scaling = 1.0 / width**0.5
    count = gx_count * heads * steps
    cosine = jnp.concatenate([cos_ref[s] for s in range(owned)], axis=0)
    sine = jnp.concatenate([sin_ref[s] for s in range(owned)], axis=0)

    def turn(first, second, cosine, sine):
        return first * cosine - second * sine, second * cosine + first * sine

    scaled = (cosine * scaling, sine * scaling)

    key_value = [ref[:, pl.ds(query_cols, ref.shape[1] - query_cols)].astype(jnp.float32) for ref in blocks]
    key_value = jnp.concatenate(unxored(key_value, lax.axis_index("gx")), axis=1)
    new_values = key_value[:, width:]
    new_keys = turn(key_value[:, :half], key_value[:, half:width], cosine, sine)
    new_keys = jnp.concatenate(new_keys, axis=1).astype(jnp.bfloat16).astype(jnp.float32)
    for k in range(gx_count):
        for h in range(heads):
            first = blocks[k][:, pl.ds(h * width, half)].astype(jnp.float32)
            second = blocks[k][:, pl.ds(h * width + half, half)].astype(jnp.float32)
            for part, value in enumerate(turn(first, second, *scaled)):
                for s in range(owned):
                    window = pl.ds((k * heads + h) * steps, steps)
                    rows_ref[s, window, pl.ds(part * half, half)] = value[s * steps : (s + 1) * steps]
    step_of = lax.broadcasted_iota(jnp.int32, (count, 1), 0) % steps
    for s in range(owned):
        queries = rows_ref[s, pl.ds(0, count)].astype(jnp.bfloat16)
        cached = lax.dot_general(
            queries, keys_ref[s], (((1,), (1,)), ((), ())), preferred_element_type=jnp.float32
        )
        cached = cached + mask_ref[s]
        highest = cached.max(-1, keepdims=True)
        wide = queries.astype(jnp.float32)
        fresh = []
        for u in range(steps):
            row = s * steps + u
            score = (wide * new_keys[row : row + 1]).sum(-1, keepdims=True)
            fresh.append(jnp.where(step_of >= u, score, -1e30))
            highest = jnp.maximum(highest, fresh[-1])
        exp_cached = jnp.exp(cached - highest)
        denom = exp_cached.sum(-1, keepdims=True)
        total = jnp.dot(
            exp_cached.astype(jnp.bfloat16), values_ref[s], preferred_element_type=jnp.float32
        )
        for u in range(steps):
            row = s * steps + u
            exp_fresh = jnp.exp(fresh[u] - highest)
            denom = denom + exp_fresh
            total = total + exp_fresh * new_values[row : row + 1]
        result_ref[s, pl.ds(0, count)] = total * (1.0 / denom)
    for k in range(gx_count):
        for h in range(heads):
            window = pl.ds((k * heads + h) * steps, steps)
            value = jnp.concatenate([result_ref[s, window] for s in range(owned)], axis=0)
            outs[k][:, pl.ds(h * width, width)] = value.astype(jnp.bfloat16)


def attend(blocks, cache_keys, cache_values, lengths, query_cols):
    gx_count = len(blocks)
    owned, slots, width = cache_keys.shape
    rows = blocks[0].shape[0]
    steps = rows // owned
    heads = query_cols // width
    count = gx_count * heads * steps
    freqs = 10000.0 ** (-(jnp.arange(width // 2, dtype=jnp.float32) * 2.0 / width))
    positions = lengths[:, None, None] + jnp.arange(steps, dtype=jnp.int32)[None, :, None]
    angles = positions.astype(jnp.float32) * freqs
    mask = jnp.where(jnp.arange(slots)[None, None, :] < lengths[:, None, None], 0.0, -1e30)
    vmem = pl.BlockSpec(memory_space=pltpu.VMEM)
    return pl.pallas_call(
        functools.partial(attend_kernel, (gx_count, owned, steps, heads, width)),
        out_shape=[jax.ShapeDtypeStruct((rows, query_cols), jnp.bfloat16)] * gx_count,
        in_specs=[vmem] * (5 + gx_count),
        out_specs=[vmem] * gx_count,
        scratch_shapes=[
            pltpu.VMEM((owned, padded(count) + 8, width), jnp.float32),
            pltpu.VMEM((owned, padded(count) + 8, width), jnp.float32),
        ],
        compiler_params=pltpu.CompilerParams(vmem_limit_bytes=12 * 1024 * 1024),
        cost_estimate=pl.CostEstimate(
            flops=4 * owned * count * slots * width,
            bytes_accessed=4 * owned * slots * width,
            transcendentals=owned * count * slots,
        ),
        name="attend",
    )(mask, jnp.cos(angles), jnp.sin(angles), cache_keys, cache_values, *[blocks[k] for k in farther_first(gx_count)])


def order_kernel(distances, *refs):
    out_ref, sorted_ref = refs[-2:]
    for k, block in zip(distances, refs):
        sorted_ref[lax.axis_index("gx") ^ k, pl.ds(0, block.shape[0])] = block[...].astype(jnp.float32)
    parts = [sorted_ref[g, pl.ds(0, block.shape[0])] for g in range(len(distances))]
    out_ref[...] = jnp.concatenate(parts, axis=0).astype(out_ref.dtype)


def order(blocks):
    vmem = pl.BlockSpec(memory_space=pltpu.VMEM)
    rows, cols = blocks[0].shape
    count = len(blocks)
    distances = farther_first(count)
    return pl.pallas_call(
        functools.partial(order_kernel, distances),
        out_shape=jax.ShapeDtypeStruct((count * rows, cols), blocks[0].dtype),
        in_specs=[vmem] * count,
        out_specs=vmem,
        scratch_shapes=[pltpu.VMEM((count, padded(rows), cols), jnp.float32)],
        compiler_params=pltpu.CompilerParams(vmem_limit_bytes=8 * 1024 * 1024),
        name="order",
    )(*[blocks[k] for k in distances])


def mix_kernel(dims, chunk, part, weight_ref, *refs):
    batch_count, gx_count, high_count, block = dims
    count = 2 * batch_count * high_count
    blocks, own_ref, sends, sum_ref = refs[:count][::-1], refs[count], refs[count + 1 : -1], refs[-1]
    shards = gx_count // batch_count
    group = block // shards
    lhs = jnp.concatenate([ref[...] for ref in blocks], axis=0)
    first, out_cols = part
    for start in range(0, out_cols, chunk):
        size = min(chunk, out_cols - start)
        window = pl.ds(start, size)
        sum_ref[:, pl.ds(0, size)] = jnp.dot(
            lhs, weight_ref[:, pl.ds(first + start, size)], preferred_element_type=jnp.float32
        )
        for k in range(gx_count):
            shard = lax.axis_index("gx") ^ k
            b, hi = shard // shards, shard % shards
            parts = []
            for relative in range(2):
                for h in range(high_count):
                    at = (relative * batch_count + (b ^ lax.axis_index("batch"))) * high_count + h
                    at = pl.multiple_of(at * block + hi * group, group)
                    parts.append(sum_ref[pl.ds(at, group), pl.ds(0, size)])
            piece = jnp.concatenate(parts, axis=0)
            target = own_ref if k == 0 else sends[k - 1]
            target[:, window] = piece.astype(target.dtype)


def mix(blocks, w_out, dims, part):
    batch_count, gx_count, high_count, block = dims
    depth = w_out.shape[0]
    out_cols = part[1]
    rows = len(blocks) * block
    chunk = min(768, out_cols)
    vmem = pl.BlockSpec(memory_space=pltpu.VMEM)
    kept = (0, 2) if gx_count == 4 else (0,)
    shapes = [
        jax.ShapeDtypeStruct((rows // gx_count, out_cols), jnp.float32 if k in kept else jnp.bfloat16)
        for k in range(gx_count)
    ]
    return pl.pallas_call(
        functools.partial(mix_kernel, dims, chunk, part),
        out_shape=shapes,
        in_specs=[vmem] * (1 + len(blocks)),
        out_specs=[vmem] * gx_count,
        scratch_shapes=[pltpu.VMEM((rows, chunk), jnp.float32)],
        compiler_params=pltpu.CompilerParams(vmem_limit_bytes=20 * 1024 * 1024),
        cost_estimate=pl.CostEstimate(
            flops=2 * rows * depth * out_cols, bytes_accessed=2 * depth * out_cols, transcendentals=0
        ),
        name="mix",
    )(w_out, *blocks[::-1])


def relay_kernel(own_ref, taken_ref, near_ref, sum_ref, copy_ref):
    total = own_ref[...] + taken_ref[...].astype(jnp.float32)
    sum_ref[...] = total.astype(sum_ref.dtype)
    copy_ref[...] = near_ref[...]


def relay(own, taken, near):
    vmem = pl.BlockSpec(memory_space=pltpu.VMEM)
    return pl.pallas_call(
        relay_kernel,
        out_shape=[jax.ShapeDtypeStruct(near.shape, near.dtype)] * 2,
        in_specs=[vmem] * 3,
        out_specs=[vmem] * 2,
        compiler_params=pltpu.CompilerParams(vmem_limit_bytes=8 * 1024 * 1024),
        name="relay",
    )(own, taken, near)


def summed_terms(sends):
    count = len(sends) + 1
    if count != 4:
        return [swapped_with(sends[k - 1], "gx", (count,), (k,)) for k in farther_first(count)[1:]]
    near, far, farthest = sends
    taken = swapped_with(farthest, "gx", (count,), (1,))
    both, near = relay(far, taken, near)
    return [swapped_with(both, "gx", (count,), (2,)), swapped_with(near, "gx", (count,), (1,))]


def finish_kernel(dims, own_ref, *refs):
    received, out_ref = refs[: len(refs) - 1], refs[-1]
    batch_count, high_count, owned = dims
    steps, out_cols = out_ref.shape[1:]
    size = batch_count * owned * steps
    received = [ref for ref in received if ref.shape == own_ref.shape]
    for relative in range(2):
        low = lax.axis_index("gl") ^ relative
        for h in range(high_count):
            window = pl.ds((relative * high_count + h) * size, size)
            total = own_ref[window]
            for other in received:
                total = total + other[window].astype(jnp.float32)
            total = total.reshape(batch_count, owned, steps, out_cols).astype(jnp.bfloat16)
            high = lax.axis_index("gh") ^ h
            for g in range(batch_count):
                first = ((g * high_count + high) * 2 + low) * owned
                out_ref[pl.ds(first, owned)] = total[g]


def finish(own, received, dims, steps, part, parts, before):
    rows, out_cols = own.shape
    whole = pl.BlockSpec((rows, out_cols), lambda step: (0, 0))
    operands = [own, *received]
    in_specs = [whole] * len(operands)
    aliases = {}
    if before is not None:
        aliases[len(operands)] = 0
        operands.append(before)
        in_specs.append(pl.BlockSpec(memory_space=pl.ANY))
    return pl.pallas_call(
        functools.partial(finish_kernel, dims),
        grid=(1,),
        out_shape=jax.ShapeDtypeStruct((rows // steps, steps, out_cols * parts), jnp.bfloat16),
        in_specs=in_specs,
        out_specs=pl.BlockSpec((rows // steps, steps, out_cols), lambda step: (0, 0, part)),
        input_output_aliases=aliases,
        compiler_params=pltpu.CompilerParams(vmem_limit_bytes=16 * 1024 * 1024),
        name="finish",
    )(*operands)


def local(tokens, w_query, w_keyval, w_out, cache_keys, cache_values, lengths):
    batch_count = lax.axis_size("batch")
    gx_count = lax.axis_size("gx")
    high_count = lax.axis_size("gh")
    sizes = (batch_count, high_count, 2)
    owned = cache_keys.shape[0]
    sequences, steps, width = tokens.shape
    query_cols = w_query.shape[1]
    rows = owned * steps
    rows_here = gx_count * rows

    kept, given = project(tokens, w_query, w_keyval, (batch_count, gx_count, high_count, owned))
    taken = swapped_with(given, PLANE, sizes, (0, 0, 1))
    far = [(db, dh) for db in range(batch_count) for dh in range(high_count)][1:]
    own, *sends = combine(staged(kept), taken, (batch_count, high_count, rows_here))
    received = [
        swapped_with(block, PLANE, sizes, (db, dh, 0)) for block, (db, dh) in zip(sends, far)
    ]
    w_out, token = near(own, w_out)
    blocks = collect(own, received, token, gx_count)
    blocks = [blocks[0]] + [
        swapped_with(blocks[k], "gx", (gx_count,), (k,)) for k in range(1, gx_count)
    ]
    blocks = attend(blocks, cache_keys, cache_values, lengths, query_cols)
    blocks = [blocks[0]] + [
        swapped_with(blocks[k], "gx", (gx_count,), (k,)) for k in range(1, gx_count)
    ]
    grouped = order(blocks)

    ours = [grouped] + [swapped_with(grouped, PLANE, sizes, (db, dh, 0)) for db, dh in far]
    theirs = [swapped_with(block, PLANE, sizes, (0, 0, 1)) for block in ours]
    out_cols = w_out.shape[1]
    parts = 2 if out_cols % 256 == 0 else 1
    size = out_cols // parts
    mixed = None
    products = [
        mix(ours + theirs, w_out, (batch_count, gx_count, high_count, rows_here), (part * size, size))
        for part in range(parts)
    ]
    for part, (own, *sends) in enumerate(products):
        received = summed_terms(sends)
        mixed = finish(own, received, (batch_count, high_count, owned), steps, part, parts, mixed)
    return mixed


def solution(mesh):
    batch_count, gx_count, gy_count = mesh.devices.shape
    split = Mesh(
        mesh.devices.reshape(batch_count, gx_count, gy_count // 2, 2), ("batch", "gx", "gh", "gl")
    )
    plane = ("batch", "gh", "gl")
    placed = (
        P(None, None, plane),
        P(plane, "gx"),
        P(plane, "gx"),
        P("gx", plane),
        P(("batch", "gx", "gh", "gl"), None, None),
        P(("batch", "gx", "gh", "gl"), None, None),
        P(("batch", "gx", "gh", "gl")),
    )
    return jax.shard_map(
        local, mesh=split, in_specs=placed, out_specs=P("gx", None, plane), check_vma=False
    )
```

```python
import functools

import jax
import jax.numpy as jnp
import numpy as np
from jax import lax
from jax.experimental import pallas as pl
from jax.experimental.pallas import tpu as pltpu
from jax.sharding import Mesh
from jax.sharding import PartitionSpec as P

PLANE = ("batch", "gh", "gl")


def swapped_with(value, axes, sizes, differs):
    pairs = []
    for place in np.ndindex(*sizes):
        target = tuple(p ^ d for p, d in zip(place, differs))
        pairs.append((int(np.ravel_multi_index(place, sizes)), int(np.ravel_multi_index(target, sizes))))
    return lax.ppermute(value, axes, pairs)


def unxored(blocks, here):
    count = len(blocks)
    bit = 1
    while bit < count:
        turn = (here & bit) != 0
        blocks = [jnp.where(turn, blocks[k ^ bit], blocks[k]) for k in range(count)]
        bit *= 2
    return blocks


def padded(rows):
    return (rows + 7) // 8 * 8


def farther_first(count):
    return [0, *range(2, count), 1]


def project_kernel(
    dims, blocks, chunks, tokens_hbm, query_hbm, pair_hbm, kept_out, given_out,
    tokens_ref, rows_ref, query_ref, pair_ref, kept_ref, given_ref, sum_ref, sems, out_sems,
):
    batch_count, gx_count, high_count, owned = dims
    query_cols = query_ref.shape[1]
    copies = [
        pltpu.make_async_copy(tokens_hbm, tokens_ref, sems.at[0]),
        pltpu.make_async_copy(pair_hbm, pair_ref, sems.at[1]),
    ]
    for place, (start, size) in enumerate(blocks):
        window = pl.ds(start, size)
        copies.append(pltpu.make_async_copy(query_hbm.at[window], query_ref.at[window], sems.at[place + 2]))
    for copy in copies:
        copy.start()
    steps, width = tokens_ref.shape[1:]
    block = gx_count * owned * steps
    half = rows_ref.shape[0] // 2
    copies[0].wait()
    for relative in range(2):
        low = lax.axis_index("gl") ^ relative
        for b in range(batch_count):
            for h in range(high_count):
                parts = []
                for g in range(gx_count):
                    first = (((b * gx_count + g) * high_count + h) * 2 + low) * owned
                    parts.append(tokens_ref[pl.ds(first, owned)])
                joined = jnp.concatenate(parts, axis=0).reshape(block, width)
                at = ((relative * batch_count + b) * high_count + h) * block
                rows_ref[pl.ds(at, block)] = joined
    writes = []

    def emit(product, start):
        product = product.astype(jnp.bfloat16)
        window = pl.ds(start, product.shape[1])
        kept_ref[:, window] = product[:half]
        given_ref[:, window] = product[half:]
        for source, target in ((given_ref, given_out), (kept_ref, kept_out)):
            copy = pltpu.make_async_copy(source.at[:, window], target.at[:, window], out_sems.at[len(writes)])
            copy.start()
            writes.append(copy)

    copies[1].wait()
    emit(jnp.dot(rows_ref[...], pair_ref[...], preferred_element_type=jnp.float32), query_cols)
    for place, (depth_at, depth) in enumerate(blocks):
        copies[2 + place].wait()
        rows = rows_ref[:, pl.ds(depth_at, depth)]
        for start, size in chunks:
            window = pl.ds(start, size)
            term = jnp.dot(
                rows, query_ref[pl.ds(depth_at, depth), window], preferred_element_type=jnp.float32
            )
            if place > 0:
                term = term + sum_ref[:, window]
            if place < len(blocks) - 1:
                sum_ref[:, window] = term
            else:
                emit(term, start)
    for copy in writes:
        copy.wait()


def cut(total, sizes):
    windows, start = [], 0
    while start < total:
        size = min(sizes[min(len(windows), len(sizes) - 1)], total - start)
        windows.append((start, size))
        start += size
    return windows


def project(tokens, w_query, w_keyval, dims):
    sequences, steps, width = tokens.shape
    query_cols, pair_cols = w_query.shape[1], w_keyval.shape[1]
    rows = sequences * steps
    blocks = cut(width, (768, 768, 512, 256))
    chunks = cut(query_cols, (768,))
    hbm = pl.BlockSpec(memory_space=pltpu.HBM)
    shape = jax.ShapeDtypeStruct((rows // 2, query_cols + pair_cols), jnp.bfloat16)
    return pl.pallas_call(
        functools.partial(project_kernel, dims, blocks, chunks),
        out_shape=(shape, shape),
        in_specs=[hbm, hbm, hbm],
        out_specs=(hbm, hbm),
        scratch_shapes=[
            pltpu.VMEM(tokens.shape, jnp.bfloat16),
            pltpu.VMEM((rows, width), jnp.bfloat16),
            pltpu.VMEM((width, query_cols), jnp.bfloat16),
            pltpu.VMEM((width, pair_cols), jnp.bfloat16),
            pltpu.VMEM((rows // 2, query_cols + pair_cols), jnp.bfloat16),
            pltpu.VMEM((rows // 2, query_cols + pair_cols), jnp.bfloat16),
            pltpu.VMEM((rows, query_cols), jnp.float32),
            pltpu.SemaphoreType.DMA((2 + len(blocks),)),
            pltpu.SemaphoreType.DMA((2 * (1 + len(chunks)),)),
        ],
        compiler_params=pltpu.CompilerParams(vmem_limit_bytes=62 * 1024 * 1024),
        cost_estimate=pl.CostEstimate(
            flops=2 * rows * width * (query_cols + pair_cols),
            bytes_accessed=2 * width * (query_cols + pair_cols),
            transcendentals=0,
        ),
        name="project",
    )(tokens, w_query, w_keyval)


def near_kernel(after_ref, source_ref, target_ref, token_ref, sem):
    copy = pltpu.make_async_copy(source_ref, target_ref, sem)
    copy.start()
    copy.wait()
    token_ref[...] = jnp.zeros_like(token_ref)


def near(after, array):
    anywhere = pl.BlockSpec(memory_space=pl.ANY)
    return pl.pallas_call(
        near_kernel,
        out_shape=(
            jax.ShapeDtypeStruct(array.shape, array.dtype),
            jax.ShapeDtypeStruct((8, 128), jnp.float32),
        ),
        in_specs=[anywhere, anywhere],
        out_specs=(anywhere, pl.BlockSpec(memory_space=pltpu.VMEM)),
        scratch_shapes=[pltpu.SemaphoreType.DMA],
        compiler_params=pltpu.CompilerParams(vmem_limit_bytes=36 * 1024 * 1024),
        cost_estimate=pl.CostEstimate(
            flops=0, bytes_accessed=2 * array.size * array.dtype.itemsize, transcendentals=0
        ),
        name="near",
    )(after, array)


def staged_kernel(source_ref, target_ref):
    target_ref[...] = source_ref[...]


def staged(array):
    vmem = pl.BlockSpec(memory_space=pltpu.VMEM)
    return pl.pallas_call(
        staged_kernel,
        out_shape=jax.ShapeDtypeStruct(array.shape, array.dtype),
        in_specs=[vmem],
        out_specs=vmem,
        compiler_params=pltpu.CompilerParams(vmem_limit_bytes=8 * 1024 * 1024),
        name="staged",
    )(array)


def combine_kernel(dims, kept_ref, taken_ref, own_ref, *sends):
    batch_count, high_count, block = dims
    for db in range(batch_count):
        for dh in range(high_count):
            at = ((lax.axis_index("batch") ^ db) * high_count + (lax.axis_index("gh") ^ dh)) * block
            window = pl.ds(pl.multiple_of(at, block), block)
            total = kept_ref[window].astype(jnp.float32) + taken_ref[window].astype(jnp.float32)
            target = sends[db * high_count + dh - 1] if db or dh else own_ref
            target[...] = total.astype(target.dtype)


def combine(kept, taken, dims):
    batch_count, high_count, block = dims
    cols = kept.shape[1]
    vmem = pl.BlockSpec(memory_space=pltpu.VMEM)
    count = batch_count * high_count
    return pl.pallas_call(
        functools.partial(combine_kernel, dims),
        out_shape=[jax.ShapeDtypeStruct((block, cols), jnp.float32)]
        + [jax.ShapeDtypeStruct((block, cols), jnp.bfloat16)] * (count - 1),
        in_specs=[vmem, vmem],
        out_specs=[vmem] * count,
        compiler_params=pltpu.CompilerParams(vmem_limit_bytes=8 * 1024 * 1024),
        name="combine",
    )(kept, taken)


def collect_kernel(count, own_ref, after_ref, *refs):
    received, outs, total_ref = refs[: -count - 1], refs[-count - 1 : -1], refs[-1]
    total = own_ref[...]
    for other in received:
        total = total + other[...].astype(jnp.float32)
    rows = outs[0].shape[0]
    for g in range(count):
        total_ref[g, pl.ds(0, rows)] = total[g * rows : (g + 1) * rows]
    for k in range(count):
        outs[k][...] = total_ref[lax.axis_index("gx") ^ k, pl.ds(0, rows)].astype(jnp.bfloat16)


def collect(own, received, after, gx_count):
    block, cols = own.shape
    rows = block // gx_count
    vmem = pl.BlockSpec(memory_space=pltpu.VMEM)
    return pl.pallas_call(
        functools.partial(collect_kernel, gx_count),
        out_shape=[jax.ShapeDtypeStruct((rows, cols), jnp.bfloat16)] * gx_count,
        in_specs=[vmem, pl.BlockSpec(memory_space=pl.ANY)]
        + [vmem] * len(received),
        out_specs=[vmem] * gx_count,
        scratch_shapes=[pltpu.VMEM((gx_count, padded(rows), cols), jnp.float32)],
        compiler_params=pltpu.CompilerParams(vmem_limit_bytes=8 * 1024 * 1024),
        name="collect",
    )(own, after, *received)


def attend_kernel(dims, mask_ref, cos_ref, sin_ref, keys_ref, values_ref, *refs):
    gx_count, owned, steps, heads, width = dims
    blocks, outs = [None] * gx_count, refs[gx_count:-2]
    for k, ref in zip(farther_first(gx_count), refs):
        blocks[k] = ref
    rows_ref, result_ref = refs[-2:]
    query_cols = heads * width
    half = width // 2
    scaling = 1.0 / width**0.5
    count = gx_count * heads * steps
    cosine = jnp.concatenate([cos_ref[s] for s in range(owned)], axis=0)
    sine = jnp.concatenate([sin_ref[s] for s in range(owned)], axis=0)

    def turn(first, second, cosine, sine):
        return first * cosine - second * sine, second * cosine + first * sine

    scaled = (cosine * scaling, sine * scaling)

    key_value = [ref[:, pl.ds(query_cols, ref.shape[1] - query_cols)].astype(jnp.float32) for ref in blocks]
    key_value = jnp.concatenate(unxored(key_value, lax.axis_index("gx")), axis=1)
    new_values = key_value[:, width:]
    new_keys = turn(key_value[:, :half], key_value[:, half:width], cosine, sine)
    new_keys = jnp.concatenate(new_keys, axis=1).astype(jnp.bfloat16).astype(jnp.float32)
    for k in range(gx_count):
        for h in range(heads):
            first = blocks[k][:, pl.ds(h * width, half)].astype(jnp.float32)
            second = blocks[k][:, pl.ds(h * width + half, half)].astype(jnp.float32)
            for part, value in enumerate(turn(first, second, *scaled)):
                for s in range(owned):
                    window = pl.ds((k * heads + h) * steps, steps)
                    rows_ref[s, window, pl.ds(part * half, half)] = value[s * steps : (s + 1) * steps]
    step_of = lax.broadcasted_iota(jnp.int32, (count, 1), 0) % steps
    for s in range(owned):
        queries = rows_ref[s, pl.ds(0, count)].astype(jnp.bfloat16)
        cached = lax.dot_general(
            queries, keys_ref[s], (((1,), (1,)), ((), ())), preferred_element_type=jnp.float32
        )
        cached = cached + mask_ref[s]
        highest = cached.max(-1, keepdims=True)
        wide = queries.astype(jnp.float32)
        fresh = []
        for u in range(steps):
            row = s * steps + u
            score = (wide * new_keys[row : row + 1]).sum(-1, keepdims=True)
            fresh.append(jnp.where(step_of >= u, score, -1e30))
            highest = jnp.maximum(highest, fresh[-1])
        exp_cached = jnp.exp(cached - highest)
        denom = exp_cached.sum(-1, keepdims=True)
        total = jnp.dot(
            exp_cached.astype(jnp.bfloat16), values_ref[s], preferred_element_type=jnp.float32
        )
        for u in range(steps):
            row = s * steps + u
            exp_fresh = jnp.exp(fresh[u] - highest)
            denom = denom + exp_fresh
            total = total + exp_fresh * new_values[row : row + 1]
        result_ref[s, pl.ds(0, count)] = total * (1.0 / denom)
    for k in range(gx_count):
        for h in range(heads):
            window = pl.ds((k * heads + h) * steps, steps)
            value = jnp.concatenate([result_ref[s, window] for s in range(owned)], axis=0)
            outs[k][:, pl.ds(h * width, width)] = value.astype(jnp.bfloat16)


def attend(blocks, cache_keys, cache_values, lengths, query_cols):
    gx_count = len(blocks)
    owned, slots, width = cache_keys.shape
    rows = blocks[0].shape[0]
    steps = rows // owned
    heads = query_cols // width
    count = gx_count * heads * steps
    freqs = 10000.0 ** (-(jnp.arange(width // 2, dtype=jnp.float32) * 2.0 / width))
    positions = lengths[:, None, None] + jnp.arange(steps, dtype=jnp.int32)[None, :, None]
    angles = positions.astype(jnp.float32) * freqs
    mask = jnp.where(jnp.arange(slots)[None, None, :] < lengths[:, None, None], 0.0, -1e30)
    vmem = pl.BlockSpec(memory_space=pltpu.VMEM)
    return pl.pallas_call(
        functools.partial(attend_kernel, (gx_count, owned, steps, heads, width)),
        out_shape=[jax.ShapeDtypeStruct((rows, query_cols), jnp.bfloat16)] * gx_count,
        in_specs=[vmem] * (5 + gx_count),
        out_specs=[vmem] * gx_count,
        scratch_shapes=[
            pltpu.VMEM((owned, padded(count) + 8, width), jnp.float32),
            pltpu.VMEM((owned, padded(count) + 8, width), jnp.float32),
        ],
        compiler_params=pltpu.CompilerParams(vmem_limit_bytes=12 * 1024 * 1024),
        cost_estimate=pl.CostEstimate(
            flops=4 * owned * count * slots * width,
            bytes_accessed=4 * owned * slots * width,
            transcendentals=owned * count * slots,
        ),
        name="attend",
    )(mask, jnp.cos(angles), jnp.sin(angles), cache_keys, cache_values, *[blocks[k] for k in farther_first(gx_count)])


def order_kernel(distances, *refs):
    out_ref, sorted_ref = refs[-2:]
    for k, block in zip(distances, refs):
        sorted_ref[lax.axis_index("gx") ^ k, pl.ds(0, block.shape[0])] = block[...].astype(jnp.float32)
    parts = [sorted_ref[g, pl.ds(0, block.shape[0])] for g in range(len(distances))]
    out_ref[...] = jnp.concatenate(parts, axis=0).astype(out_ref.dtype)


def order(blocks):
    vmem = pl.BlockSpec(memory_space=pltpu.VMEM)
    rows, cols = blocks[0].shape
    count = len(blocks)
    distances = farther_first(count)
    return pl.pallas_call(
        functools.partial(order_kernel, distances),
        out_shape=jax.ShapeDtypeStruct((count * rows, cols), blocks[0].dtype),
        in_specs=[vmem] * count,
        out_specs=vmem,
        scratch_shapes=[pltpu.VMEM((count, padded(rows), cols), jnp.float32)],
        compiler_params=pltpu.CompilerParams(vmem_limit_bytes=8 * 1024 * 1024),
        name="order",
    )(*[blocks[k] for k in distances])


def mix_kernel(dims, chunk, part, weight_ref, *refs):
    batch_count, gx_count, high_count, block = dims
    count = 2 * batch_count * high_count
    blocks, own_ref, sends, sum_ref = refs[:count][::-1], refs[count], refs[count + 1 : -1], refs[-1]
    shards = gx_count // batch_count
    group = block // shards
    lhs = jnp.concatenate([ref[...] for ref in blocks], axis=0)
    first, out_cols = part
    for start in range(0, out_cols, chunk):
        size = min(chunk, out_cols - start)
        window = pl.ds(start, size)
        sum_ref[:, pl.ds(0, size)] = jnp.dot(
            lhs, weight_ref[:, pl.ds(first + start, size)], preferred_element_type=jnp.float32
        )
        for k in range(gx_count):
            shard = lax.axis_index("gx") ^ k
            b, hi = shard // shards, shard % shards
            parts = []
            for relative in range(2):
                for h in range(high_count):
                    at = (relative * batch_count + (b ^ lax.axis_index("batch"))) * high_count + h
                    at = pl.multiple_of(at * block + hi * group, group)
                    parts.append(sum_ref[pl.ds(at, group), pl.ds(0, size)])
            piece = jnp.concatenate(parts, axis=0)
            target = own_ref if k == 0 else sends[k - 1]
            target[:, window] = piece.astype(target.dtype)


def mix(blocks, w_out, dims, part):
    batch_count, gx_count, high_count, block = dims
    depth = w_out.shape[0]
    out_cols = part[1]
    rows = len(blocks) * block
    chunk = min(768, out_cols)
    vmem = pl.BlockSpec(memory_space=pltpu.VMEM)
    kept = (0, 2) if gx_count == 4 else (0,)
    shapes = [
        jax.ShapeDtypeStruct((rows // gx_count, out_cols), jnp.float32 if k in kept else jnp.bfloat16)
        for k in range(gx_count)
    ]
    return pl.pallas_call(
        functools.partial(mix_kernel, dims, chunk, part),
        out_shape=shapes,
        in_specs=[vmem] * (1 + len(blocks)),
        out_specs=[vmem] * gx_count,
        scratch_shapes=[pltpu.VMEM((rows, chunk), jnp.float32)],
        compiler_params=pltpu.CompilerParams(vmem_limit_bytes=20 * 1024 * 1024),
        cost_estimate=pl.CostEstimate(
            flops=2 * rows * depth * out_cols, bytes_accessed=2 * depth * out_cols, transcendentals=0
        ),
        name="mix",
    )(w_out, *blocks[::-1])


def relay_kernel(own_ref, taken_ref, out_ref):
    total = own_ref[...] + taken_ref[...].astype(jnp.float32)
    out_ref[...] = total.astype(out_ref.dtype)


def relay(own, taken, kind):
    vmem = pl.BlockSpec(memory_space=pltpu.VMEM)
    return pl.pallas_call(
        relay_kernel,
        out_shape=jax.ShapeDtypeStruct(taken.shape, kind),
        in_specs=[vmem, vmem],
        out_specs=vmem,
        compiler_params=pltpu.CompilerParams(vmem_limit_bytes=8 * 1024 * 1024),
        name="relay",
    )(own, taken)


def held_kernel(after_ref, source_ref, out_ref):
    out_ref[...] = source_ref[...]


def held(array, after):
    vmem = pl.BlockSpec(memory_space=pltpu.VMEM)
    return pl.pallas_call(
        held_kernel,
        out_shape=jax.ShapeDtypeStruct(array.shape, array.dtype),
        in_specs=[pl.BlockSpec(memory_space=pl.ANY), vmem],
        out_specs=vmem,
        compiler_params=pltpu.CompilerParams(vmem_limit_bytes=8 * 1024 * 1024),
        name="held",
    )(after, array)


def summed_terms(products):
    count = len(products[0])
    if count != 4:
        return [
            [swapped_with(product[k], "gx", (count,), (k,)) for k in farther_first(count)[1:]]
            for product in products
        ]
    boths = [
        relay(product[2], swapped_with(product[3], "gx", (count,), (1,)), jnp.bfloat16)
        for product in products
    ]
    return [
        [
            swapped_with(both, "gx", (count,), (2,)),
            swapped_with(held(product[1], boths[-1]), "gx", (count,), (1,)),
        ]
        for both, product in zip(boths, products)
    ]


def finish_kernel(dims, counts, *refs):
    refs, out_ref = list(refs[:-1]), refs[-1]
    batch_count, high_count, owned = dims
    steps = out_ref.shape[1]
    size = batch_count * owned * steps
    begin = 0
    for count in counts:
        own_ref, *received = refs[:count]
        refs = refs[count:]
        cols = own_ref.shape[1]
        for relative in range(2):
            low = lax.axis_index("gl") ^ relative
            for h in range(high_count):
                window = pl.ds((relative * high_count + h) * size, size)
                total = own_ref[window]
                for other in received:
                    total = total + other[window].astype(jnp.float32)
                total = total.reshape(batch_count, owned, steps, cols).astype(jnp.bfloat16)
                high = lax.axis_index("gh") ^ h
                for g in range(batch_count):
                    first = ((g * high_count + high) * 2 + low) * owned
                    out_ref[pl.ds(first, owned), :, pl.ds(begin, cols)] = total[g]
        begin += cols


def finish(parts, dims, steps):
    vmem = pl.BlockSpec(memory_space=pltpu.VMEM)
    rows = parts[0][0].shape[0]
    out_cols = sum(part[0].shape[1] for part in parts)
    terms = [term for part in parts for term in part]
    return pl.pallas_call(
        functools.partial(finish_kernel, dims, [len(part) for part in parts]),
        out_shape=jax.ShapeDtypeStruct((rows // steps, steps, out_cols), jnp.bfloat16),
        in_specs=[vmem] * len(terms),
        out_specs=vmem,
        compiler_params=pltpu.CompilerParams(vmem_limit_bytes=16 * 1024 * 1024),
        name="finish",
    )(*terms)


def local(tokens, w_query, w_keyval, w_out, cache_keys, cache_values, lengths):
    batch_count = lax.axis_size("batch")
    gx_count = lax.axis_size("gx")
    high_count = lax.axis_size("gh")
    sizes = (batch_count, high_count, 2)
    owned = cache_keys.shape[0]
    sequences, steps, width = tokens.shape
    query_cols = w_query.shape[1]
    rows = owned * steps
    rows_here = gx_count * rows

    kept, given = project(tokens, w_query, w_keyval, (batch_count, gx_count, high_count, owned))
    taken = swapped_with(given, PLANE, sizes, (0, 0, 1))
    far = [(db, dh) for db in range(batch_count) for dh in range(high_count)][1:]
    own, *sends = combine(staged(kept), taken, (batch_count, high_count, rows_here))
    received = [
        swapped_with(block, PLANE, sizes, (db, dh, 0)) for block, (db, dh) in zip(sends, far)
    ]
    w_out, token = near(own, w_out)
    blocks = collect(own, received, token, gx_count)
    blocks = [blocks[0]] + [
        swapped_with(blocks[k], "gx", (gx_count,), (k,)) for k in range(1, gx_count)
    ]
    blocks = attend(blocks, cache_keys, cache_values, lengths, query_cols)
    blocks = [blocks[0]] + [
        swapped_with(blocks[k], "gx", (gx_count,), (k,)) for k in range(1, gx_count)
    ]
    grouped = order(blocks)

    ours = [grouped] + [swapped_with(grouped, PLANE, sizes, (db, dh, 0)) for db, dh in far]
    theirs = [swapped_with(block, PLANE, sizes, (0, 0, 1)) for block in ours]
    out_cols = w_out.shape[1]
    parts = 2 if out_cols % 256 == 0 else 1
    size = out_cols // parts
    products = [
        mix(ours + theirs, w_out, (batch_count, gx_count, high_count, rows_here), (part * size, size))
        for part in range(parts)
    ]
    summands = [[product[0], *terms] for product, terms in zip(products, summed_terms(products))]
    for part in range(parts - 1):
        own, both, *rest = summands[part]
        summands[part] = [relay(own, both, jnp.float32), *rest]
    return finish(summands, (batch_count, high_count, owned), steps)


def solution(mesh):
    batch_count, gx_count, gy_count = mesh.devices.shape
    split = Mesh(
        mesh.devices.reshape(batch_count, gx_count, gy_count // 2, 2), ("batch", "gx", "gh", "gl")
    )
    plane = ("batch", "gh", "gl")
    placed = (
        P(None, None, plane),
        P(plane, "gx"),
        P(plane, "gx"),
        P("gx", plane),
        P(("batch", "gx", "gh", "gl"), None, None),
        P(("batch", "gx", "gh", "gl"), None, None),
        P(("batch", "gx", "gh", "gl")),
    )
    return jax.shard_map(
        local, mesh=split, in_specs=placed, out_specs=P("gx", None, plane), check_vma=False
    )
```

```python
import functools

import jax
import jax.numpy as jnp
import numpy as np
from jax import lax
from jax.experimental import pallas as pl
from jax.experimental.pallas import tpu as pltpu
from jax.sharding import Mesh
from jax.sharding import PartitionSpec as P

PLANE = ("batch", "gh", "gl")


def swapped_with(value, axes, sizes, differs):
    pairs = []
    for place in np.ndindex(*sizes):
        target = tuple(p ^ d for p, d in zip(place, differs))
        pairs.append((int(np.ravel_multi_index(place, sizes)), int(np.ravel_multi_index(target, sizes))))
    return lax.ppermute(value, axes, pairs)


def unxored(blocks, here):
    count = len(blocks)
    bit = 1
    while bit < count:
        turn = (here & bit) != 0
        blocks = [jnp.where(turn, blocks[k ^ bit], blocks[k]) for k in range(count)]
        bit *= 2
    return blocks


def padded(rows):
    return (rows + 7) // 8 * 8


def farther_first(count):
    return [0, *range(2, count), 1]


def project_kernel(
    dims, blocks, chunks, tokens_hbm, query_hbm, pair_hbm, kept_out, given_out,
    tokens_ref, rows_ref, query_ref, pair_ref, kept_ref, given_ref, sum_ref, sems, out_sems,
):
    batch_count, gx_count, high_count, owned = dims
    query_cols = query_ref.shape[1]
    copies = [
        pltpu.make_async_copy(tokens_hbm, tokens_ref, sems.at[0]),
        pltpu.make_async_copy(pair_hbm, pair_ref, sems.at[1]),
    ]
    for place, (start, size) in enumerate(blocks):
        window = pl.ds(start, size)
        copies.append(pltpu.make_async_copy(query_hbm.at[window], query_ref.at[window], sems.at[place + 2]))
    for copy in copies:
        copy.start()
    steps, width = tokens_ref.shape[1:]
    block = gx_count * owned * steps
    half = rows_ref.shape[0] // 2
    copies[0].wait()
    for relative in range(2):
        low = lax.axis_index("gl") ^ relative
        for b in range(batch_count):
            for h in range(high_count):
                parts = []
                for g in range(gx_count):
                    first = (((b * gx_count + g) * high_count + h) * 2 + low) * owned
                    parts.append(tokens_ref[pl.ds(first, owned)])
                joined = jnp.concatenate(parts, axis=0).reshape(block, width)
                at = ((relative * batch_count + b) * high_count + h) * block
                rows_ref[pl.ds(at, block)] = joined
    writes = []

    def emit(product, start):
        product = product.astype(jnp.bfloat16)
        window = pl.ds(start, product.shape[1])
        kept_ref[:, window] = product[:half]
        given_ref[:, window] = product[half:]
        for source, target in ((given_ref, given_out), (kept_ref, kept_out)):
            copy = pltpu.make_async_copy(source.at[:, window], target.at[:, window], out_sems.at[len(writes)])
            copy.start()
            writes.append(copy)

    copies[1].wait()
    emit(jnp.dot(rows_ref[...], pair_ref[...], preferred_element_type=jnp.float32), query_cols)
    for place, (depth_at, depth) in enumerate(blocks):
        copies[2 + place].wait()
        rows = rows_ref[:, pl.ds(depth_at, depth)]
        for start, size in chunks:
            window = pl.ds(start, size)
            term = jnp.dot(
                rows, query_ref[pl.ds(depth_at, depth), window], preferred_element_type=jnp.float32
            )
            if place > 0:
                term = term + sum_ref[:, window]
            if place < len(blocks) - 1:
                sum_ref[:, window] = term
            else:
                emit(term, start)
    for copy in writes:
        copy.wait()


def cut(total, sizes):
    windows, start = [], 0
    while start < total:
        size = min(sizes[min(len(windows), len(sizes) - 1)], total - start)
        windows.append((start, size))
        start += size
    return windows


def project(tokens, w_query, w_keyval, dims):
    sequences, steps, width = tokens.shape
    query_cols, pair_cols = w_query.shape[1], w_keyval.shape[1]
    rows = sequences * steps
    blocks = cut(width, (768, 768, 512, 256))
    chunks = cut(query_cols, (768,))
    hbm = pl.BlockSpec(memory_space=pltpu.HBM)
    shape = jax.ShapeDtypeStruct((rows // 2, query_cols + pair_cols), jnp.bfloat16)
    return pl.pallas_call(
        functools.partial(project_kernel, dims, blocks, chunks),
        out_shape=(shape, shape),
        in_specs=[hbm, hbm, hbm],
        out_specs=(hbm, hbm),
        scratch_shapes=[
            pltpu.VMEM(tokens.shape, jnp.bfloat16),
            pltpu.VMEM((rows, width), jnp.bfloat16),
            pltpu.VMEM((width, query_cols), jnp.bfloat16),
            pltpu.VMEM((width, pair_cols), jnp.bfloat16),
            pltpu.VMEM((rows // 2, query_cols + pair_cols), jnp.bfloat16),
            pltpu.VMEM((rows // 2, query_cols + pair_cols), jnp.bfloat16),
            pltpu.VMEM((rows, query_cols), jnp.float32),
            pltpu.SemaphoreType.DMA((2 + len(blocks),)),
            pltpu.SemaphoreType.DMA((2 * (1 + len(chunks)),)),
        ],
        compiler_params=pltpu.CompilerParams(vmem_limit_bytes=62 * 1024 * 1024),
        cost_estimate=pl.CostEstimate(
            flops=2 * rows * width * (query_cols + pair_cols),
            bytes_accessed=2 * width * (query_cols + pair_cols),
            transcendentals=0,
        ),
        name="project",
    )(tokens, w_query, w_keyval)


def near_kernel(after_ref, source_ref, target_ref, token_ref, sem):
    copy = pltpu.make_async_copy(source_ref, target_ref, sem)
    copy.start()
    copy.wait()
    token_ref[...] = jnp.zeros_like(token_ref)


def near(after, array):
    anywhere = pl.BlockSpec(memory_space=pl.ANY)
    return pl.pallas_call(
        near_kernel,
        out_shape=(
            jax.ShapeDtypeStruct(array.shape, array.dtype),
            jax.ShapeDtypeStruct((8, 128), jnp.float32),
        ),
        in_specs=[anywhere, anywhere],
        out_specs=(anywhere, pl.BlockSpec(memory_space=pltpu.VMEM)),
        scratch_shapes=[pltpu.SemaphoreType.DMA],
        compiler_params=pltpu.CompilerParams(vmem_limit_bytes=36 * 1024 * 1024),
        cost_estimate=pl.CostEstimate(
            flops=0, bytes_accessed=2 * array.size * array.dtype.itemsize, transcendentals=0
        ),
        name="near",
    )(after, array)


def staged_kernel(source_ref, target_ref):
    target_ref[...] = source_ref[...]


def staged(array):
    vmem = pl.BlockSpec(memory_space=pltpu.VMEM)
    return pl.pallas_call(
        staged_kernel,
        out_shape=jax.ShapeDtypeStruct(array.shape, array.dtype),
        in_specs=[vmem],
        out_specs=vmem,
        compiler_params=pltpu.CompilerParams(vmem_limit_bytes=8 * 1024 * 1024),
        name="staged",
    )(array)


def combine_kernel(dims, kept_ref, taken_ref, own_ref, *sends):
    batch_count, high_count, block = dims
    for db in range(batch_count):
        for dh in range(high_count):
            at = ((lax.axis_index("batch") ^ db) * high_count + (lax.axis_index("gh") ^ dh)) * block
            window = pl.ds(pl.multiple_of(at, block), block)
            total = kept_ref[window].astype(jnp.float32) + taken_ref[window].astype(jnp.float32)
            target = sends[db * high_count + dh - 1] if db or dh else own_ref
            target[...] = total.astype(target.dtype)


def combine(kept, taken, dims):
    batch_count, high_count, block = dims
    cols = kept.shape[1]
    vmem = pl.BlockSpec(memory_space=pltpu.VMEM)
    count = batch_count * high_count
    return pl.pallas_call(
        functools.partial(combine_kernel, dims),
        out_shape=[jax.ShapeDtypeStruct((block, cols), jnp.float32)]
        + [jax.ShapeDtypeStruct((block, cols), jnp.bfloat16)] * (count - 1),
        in_specs=[vmem, vmem],
        out_specs=[vmem] * count,
        compiler_params=pltpu.CompilerParams(vmem_limit_bytes=8 * 1024 * 1024),
        name="combine",
    )(kept, taken)


def collect_kernel(count, own_ref, after_ref, *refs):
    received, outs, total_ref = refs[: -count - 1], refs[-count - 1 : -1], refs[-1]
    total = own_ref[...]
    for other in received:
        total = total + other[...].astype(jnp.float32)
    rows = outs[0].shape[0]
    for g in range(count):
        total_ref[g, pl.ds(0, rows)] = total[g * rows : (g + 1) * rows]
    for k in range(count):
        outs[k][...] = total_ref[lax.axis_index("gx") ^ k, pl.ds(0, rows)].astype(jnp.bfloat16)


def collect(own, received, after, gx_count):
    block, cols = own.shape
    rows = block // gx_count
    vmem = pl.BlockSpec(memory_space=pltpu.VMEM)
    return pl.pallas_call(
        functools.partial(collect_kernel, gx_count),
        out_shape=[jax.ShapeDtypeStruct((rows, cols), jnp.bfloat16)] * gx_count,
        in_specs=[vmem, pl.BlockSpec(memory_space=pl.ANY)]
        + [vmem] * len(received),
        out_specs=[vmem] * gx_count,
        scratch_shapes=[pltpu.VMEM((gx_count, padded(rows), cols), jnp.float32)],
        compiler_params=pltpu.CompilerParams(vmem_limit_bytes=8 * 1024 * 1024),
        name="collect",
    )(own, after, *received)


def attend_kernel(dims, mask_ref, cos_ref, sin_ref, keys_ref, values_ref, *refs):
    gx_count, owned, steps, heads, width = dims
    blocks, outs = [None] * gx_count, refs[gx_count:-2]
    for k, ref in zip(farther_first(gx_count), refs):
        blocks[k] = ref
    rows_ref, result_ref = refs[-2:]
    query_cols = heads * width
    half = width // 2
    scaling = 1.0 / width**0.5
    count = gx_count * heads * steps
    cosine = jnp.concatenate([cos_ref[s] for s in range(owned)], axis=0)
    sine = jnp.concatenate([sin_ref[s] for s in range(owned)], axis=0)

    def turn(first, second, cosine, sine):
        return first * cosine - second * sine, second * cosine + first * sine

    scaled = (cosine * scaling, sine * scaling)

    key_value = [ref[:, pl.ds(query_cols, ref.shape[1] - query_cols)].astype(jnp.float32) for ref in blocks]
    key_value = jnp.concatenate(unxored(key_value, lax.axis_index("gx")), axis=1)
    new_values = key_value[:, width:]
    new_keys = turn(key_value[:, :half], key_value[:, half:width], cosine, sine)
    new_keys = jnp.concatenate(new_keys, axis=1).astype(jnp.bfloat16).astype(jnp.float32)
    for k in range(gx_count):
        for h in range(heads):
            first = blocks[k][:, pl.ds(h * width, half)].astype(jnp.float32)
            second = blocks[k][:, pl.ds(h * width + half, half)].astype(jnp.float32)
            for part, value in enumerate(turn(first, second, *scaled)):
                for s in range(owned):
                    window = pl.ds((k * heads + h) * steps, steps)
                    rows_ref[s, window, pl.ds(part * half, half)] = value[s * steps : (s + 1) * steps]
    step_of = lax.broadcasted_iota(jnp.int32, (count, 1), 0) % steps
    all_queries = [rows_ref[s, pl.ds(0, count)].astype(jnp.bfloat16) for s in range(owned)]
    scores = [
        lax.dot_general(
            all_queries[s], keys_ref[s], (((1,), (1,)), ((), ())), preferred_element_type=jnp.float32
        )
        for s in range(owned)
    ]
    for s in range(owned):
        queries = all_queries[s]
        cached = scores[s] + mask_ref[s]
        highest = cached.max(-1, keepdims=True)
        wide = queries.astype(jnp.float32)
        fresh = []
        for u in range(steps):
            row = s * steps + u
            score = (wide * new_keys[row : row + 1]).sum(-1, keepdims=True)
            fresh.append(jnp.where(step_of >= u, score, -1e30))
            highest = jnp.maximum(highest, fresh[-1])
        exp_cached = jnp.exp(cached - highest)
        denom = exp_cached.sum(-1, keepdims=True)
        total = jnp.dot(
            exp_cached.astype(jnp.bfloat16), values_ref[s], preferred_element_type=jnp.float32
        )
        for u in range(steps):
            row = s * steps + u
            exp_fresh = jnp.exp(fresh[u] - highest)
            denom = denom + exp_fresh
            total = total + exp_fresh * new_values[row : row + 1]
        result_ref[s, pl.ds(0, count)] = total * (1.0 / denom)
    for k in range(gx_count):
        for h in range(heads):
            window = pl.ds((k * heads + h) * steps, steps)
            value = jnp.concatenate([result_ref[s, window] for s in range(owned)], axis=0)
            outs[k][:, pl.ds(h * width, width)] = value.astype(jnp.bfloat16)


def attend(blocks, cache_keys, cache_values, lengths, query_cols):
    gx_count = len(blocks)
    owned, slots, width = cache_keys.shape
    rows = blocks[0].shape[0]
    steps = rows // owned
    heads = query_cols // width
    count = gx_count * heads * steps
    freqs = 10000.0 ** (-(jnp.arange(width // 2, dtype=jnp.float32) * 2.0 / width))
    positions = lengths[:, None, None] + jnp.arange(steps, dtype=jnp.int32)[None, :, None]
    angles = positions.astype(jnp.float32) * freqs
    mask = jnp.where(jnp.arange(slots)[None, None, :] < lengths[:, None, None], 0.0, -1e30)
    vmem = pl.BlockSpec(memory_space=pltpu.VMEM)
    return pl.pallas_call(
        functools.partial(attend_kernel, (gx_count, owned, steps, heads, width)),
        out_shape=[jax.ShapeDtypeStruct((rows, query_cols), jnp.bfloat16)] * gx_count,
        in_specs=[vmem] * (5 + gx_count),
        out_specs=[vmem] * gx_count,
        scratch_shapes=[
            pltpu.VMEM((owned, padded(count) + 8, width), jnp.float32),
            pltpu.VMEM((owned, padded(count) + 8, width), jnp.float32),
        ],
        compiler_params=pltpu.CompilerParams(vmem_limit_bytes=12 * 1024 * 1024),
        cost_estimate=pl.CostEstimate(
            flops=4 * owned * count * slots * width,
            bytes_accessed=4 * owned * slots * width,
            transcendentals=owned * count * slots,
        ),
        name="attend",
    )(mask, jnp.cos(angles), jnp.sin(angles), cache_keys, cache_values, *[blocks[k] for k in farther_first(gx_count)])


def order_kernel(distances, *refs):
    out_ref, sorted_ref = refs[-2:]
    for k, block in zip(distances, refs):
        sorted_ref[lax.axis_index("gx") ^ k, pl.ds(0, block.shape[0])] = block[...].astype(jnp.float32)
    parts = [sorted_ref[g, pl.ds(0, block.shape[0])] for g in range(len(distances))]
    out_ref[...] = jnp.concatenate(parts, axis=0).astype(out_ref.dtype)


def order(blocks):
    vmem = pl.BlockSpec(memory_space=pltpu.VMEM)
    rows, cols = blocks[0].shape
    count = len(blocks)
    distances = farther_first(count)
    return pl.pallas_call(
        functools.partial(order_kernel, distances),
        out_shape=jax.ShapeDtypeStruct((count * rows, cols), blocks[0].dtype),
        in_specs=[vmem] * count,
        out_specs=vmem,
        scratch_shapes=[pltpu.VMEM((count, padded(rows), cols), jnp.float32)],
        compiler_params=pltpu.CompilerParams(vmem_limit_bytes=8 * 1024 * 1024),
        name="order",
    )(*[blocks[k] for k in distances])


def mix_kernel(dims, chunk, part, weight_ref, *refs):
    batch_count, gx_count, high_count, block = dims
    count = 2 * batch_count * high_count
    blocks, own_ref, sends, sum_ref = refs[:count][::-1], refs[count], refs[count + 1 : -1], refs[-1]
    shards = gx_count // batch_count
    group = block // shards
    lhs = jnp.concatenate([ref[...] for ref in blocks], axis=0)
    first, out_cols = part
    for start in range(0, out_cols, chunk):
        size = min(chunk, out_cols - start)
        window = pl.ds(start, size)
        sum_ref[:, pl.ds(0, size)] = jnp.dot(
            lhs, weight_ref[:, pl.ds(first + start, size)], preferred_element_type=jnp.float32
        )
        for k in range(gx_count):
            shard = lax.axis_index("gx") ^ k
            b, hi = shard // shards, shard % shards
            parts = []
            for relative in range(2):
                for h in range(high_count):
                    at = (relative * batch_count + (b ^ lax.axis_index("batch"))) * high_count + h
                    at = pl.multiple_of(at * block + hi * group, group)
                    parts.append(sum_ref[pl.ds(at, group), pl.ds(0, size)])
            piece = jnp.concatenate(parts, axis=0)
            target = own_ref if k == 0 else sends[k - 1]
            target[:, window] = piece.astype(target.dtype)


def mix(blocks, w_out, dims, part):
    batch_count, gx_count, high_count, block = dims
    depth = w_out.shape[0]
    out_cols = part[1]
    rows = len(blocks) * block
    chunk = min(768, out_cols)
    vmem = pl.BlockSpec(memory_space=pltpu.VMEM)
    kept = (0, 2) if gx_count == 4 else (0,)
    shapes = [
        jax.ShapeDtypeStruct((rows // gx_count, out_cols), jnp.float32 if k in kept else jnp.bfloat16)
        for k in range(gx_count)
    ]
    return pl.pallas_call(
        functools.partial(mix_kernel, dims, chunk, part),
        out_shape=shapes,
        in_specs=[vmem] * (1 + len(blocks)),
        out_specs=[vmem] * gx_count,
        scratch_shapes=[pltpu.VMEM((rows, chunk), jnp.float32)],
        compiler_params=pltpu.CompilerParams(vmem_limit_bytes=20 * 1024 * 1024),
        cost_estimate=pl.CostEstimate(
            flops=2 * rows * depth * out_cols, bytes_accessed=2 * depth * out_cols, transcendentals=0
        ),
        name="mix",
    )(w_out, *blocks[::-1])


def relay_kernel(own_ref, taken_ref, near_ref, sum_ref, copy_ref):
    total = own_ref[...] + taken_ref[...].astype(jnp.float32)
    sum_ref[...] = total.astype(sum_ref.dtype)
    copy_ref[...] = near_ref[...]


def relay(own, taken, near):
    vmem = pl.BlockSpec(memory_space=pltpu.VMEM)
    return pl.pallas_call(
        relay_kernel,
        out_shape=[jax.ShapeDtypeStruct(near.shape, near.dtype)] * 2,
        in_specs=[vmem] * 3,
        out_specs=[vmem] * 2,
        compiler_params=pltpu.CompilerParams(vmem_limit_bytes=8 * 1024 * 1024),
        name="relay",
    )(own, taken, near)


def summed_terms(sends):
    count = len(sends) + 1
    if count != 4:
        return [swapped_with(sends[k - 1], "gx", (count,), (k,)) for k in farther_first(count)[1:]]
    near, far, farthest = sends
    taken = swapped_with(farthest, "gx", (count,), (1,))
    both, near = relay(far, taken, near)
    return [swapped_with(both, "gx", (count,), (2,)), swapped_with(near, "gx", (count,), (1,))]


def finish_kernel(dims, own_ref, *refs):
    received, out_ref = refs[: len(refs) - 1], refs[-1]
    batch_count, high_count, owned = dims
    steps, out_cols = out_ref.shape[1:]
    size = batch_count * owned * steps
    received = [ref for ref in received if ref.shape == own_ref.shape]
    for relative in range(2):
        low = lax.axis_index("gl") ^ relative
        for h in range(high_count):
            window = pl.ds((relative * high_count + h) * size, size)
            total = own_ref[window]
            for other in received:
                total = total + other[window].astype(jnp.float32)
            total = total.reshape(batch_count, owned, steps, out_cols).astype(jnp.bfloat16)
            high = lax.axis_index("gh") ^ h
            for g in range(batch_count):
                first = ((g * high_count + high) * 2 + low) * owned
                out_ref[pl.ds(first, owned)] = total[g]


def finish(own, received, dims, steps, part, parts, before):
    rows, out_cols = own.shape
    whole = pl.BlockSpec((rows, out_cols), lambda step: (0, 0))
    operands = [own, *received]
    in_specs = [whole] * len(operands)
    aliases = {}
    if before is not None:
        aliases[len(operands)] = 0
        operands.append(before)
        in_specs.append(pl.BlockSpec(memory_space=pl.ANY))
    return pl.pallas_call(
        functools.partial(finish_kernel, dims),
        grid=(1,),
        out_shape=jax.ShapeDtypeStruct((rows // steps, steps, out_cols * parts), jnp.bfloat16),
        in_specs=in_specs,
        out_specs=pl.BlockSpec((rows // steps, steps, out_cols), lambda step: (0, 0, part)),
        input_output_aliases=aliases,
        compiler_params=pltpu.CompilerParams(vmem_limit_bytes=16 * 1024 * 1024),
        name="finish",
    )(*operands)


def local(tokens, w_query, w_keyval, w_out, cache_keys, cache_values, lengths):
    batch_count = lax.axis_size("batch")
    gx_count = lax.axis_size("gx")
    high_count = lax.axis_size("gh")
    sizes = (batch_count, high_count, 2)
    owned = cache_keys.shape[0]
    sequences, steps, width = tokens.shape
    query_cols = w_query.shape[1]
    rows = owned * steps
    rows_here = gx_count * rows

    kept, given = project(tokens, w_query, w_keyval, (batch_count, gx_count, high_count, owned))
    taken = swapped_with(given, PLANE, sizes, (0, 0, 1))
    far = [(db, dh) for db in range(batch_count) for dh in range(high_count)][1:]
    own, *sends = combine(staged(kept), taken, (batch_count, high_count, rows_here))
    received = [
        swapped_with(block, PLANE, sizes, (db, dh, 0)) for block, (db, dh) in zip(sends, far)
    ]
    w_out, token = near(own, w_out)
    blocks = collect(own, received, token, gx_count)
    blocks = [blocks[0]] + [
        swapped_with(blocks[k], "gx", (gx_count,), (k,)) for k in range(1, gx_count)
    ]
    blocks = attend(blocks, cache_keys, cache_values, lengths, query_cols)
    blocks = [blocks[0]] + [
        swapped_with(blocks[k], "gx", (gx_count,), (k,)) for k in range(1, gx_count)
    ]
    grouped = order(blocks)

    ours = [grouped] + [swapped_with(grouped, PLANE, sizes, (db, dh, 0)) for db, dh in far]
    theirs = [swapped_with(block, PLANE, sizes, (0, 0, 1)) for block in ours]
    out_cols = w_out.shape[1]
    parts = 2 if out_cols % 256 == 0 else 1
    size = out_cols // parts
    mixed = None
    products = [
        mix(ours + theirs, w_out, (batch_count, gx_count, high_count, rows_here), (part * size, size))
        for part in range(parts)
    ]
    for part, (own, *sends) in enumerate(products):
        received = summed_terms(sends)
        mixed = finish(own, received, (batch_count, high_count, owned), steps, part, parts, mixed)
    return mixed


def solution(mesh):
    batch_count, gx_count, gy_count = mesh.devices.shape
    split = Mesh(
        mesh.devices.reshape(batch_count, gx_count, gy_count // 2, 2), ("batch", "gx", "gh", "gl")
    )
    plane = ("batch", "gh", "gl")
    placed = (
        P(None, None, plane),
        P(plane, "gx"),
        P(plane, "gx"),
        P("gx", plane),
        P(("batch", "gx", "gh", "gl"), None, None),
        P(("batch", "gx", "gh", "gl"), None, None),
        P(("batch", "gx", "gh", "gl")),
    )
    return jax.shard_map(
        local, mesh=split, in_specs=placed, out_specs=P("gx", None, plane), check_vma=False
    )
```

```python
import functools

import jax
import jax.numpy as jnp
import numpy as np
from jax import lax
from jax.experimental import pallas as pl
from jax.experimental.pallas import tpu as pltpu
from jax.sharding import Mesh
from jax.sharding import PartitionSpec as P

PLANE = ("batch", "gh", "gl")


def swapped_with(value, axes, sizes, differs):
    pairs = []
    for place in np.ndindex(*sizes):
        target = tuple(p ^ d for p, d in zip(place, differs))
        pairs.append((int(np.ravel_multi_index(place, sizes)), int(np.ravel_multi_index(target, sizes))))
    return lax.ppermute(value, axes, pairs)


def unxored(blocks, here):
    count = len(blocks)
    bit = 1
    while bit < count:
        turn = (here & bit) != 0
        blocks = [jnp.where(turn, blocks[k ^ bit], blocks[k]) for k in range(count)]
        bit *= 2
    return blocks


def padded(rows):
    return (rows + 7) // 8 * 8


def farther_first(count):
    return [0, *range(2, count), 1]


def project_kernel(
    dims, blocks, chunks, tokens_hbm, query_hbm, pair_hbm, kept_out, given_out,
    tokens_ref, rows_ref, query_ref, pair_ref, kept_ref, given_ref, sum_ref, sems, out_sems,
):
    batch_count, gx_count, high_count, owned = dims
    query_cols = query_ref.shape[1]
    copies = [
        pltpu.make_async_copy(tokens_hbm, tokens_ref, sems.at[0]),
        pltpu.make_async_copy(pair_hbm, pair_ref, sems.at[1]),
    ]
    for place, (start, size) in enumerate(blocks):
        window = pl.ds(start, size)
        copies.append(pltpu.make_async_copy(query_hbm.at[window], query_ref.at[window], sems.at[place + 2]))
    for copy in copies:
        copy.start()
    steps, width = tokens_ref.shape[1:]
    block = gx_count * owned * steps
    half = rows_ref.shape[0] // 2
    copies[0].wait()
    for relative in range(2):
        low = lax.axis_index("gl") ^ relative
        for b in range(batch_count):
            for h in range(high_count):
                parts = []
                for g in range(gx_count):
                    first = (((b * gx_count + g) * high_count + h) * 2 + low) * owned
                    parts.append(tokens_ref[pl.ds(first, owned)])
                joined = jnp.concatenate(parts, axis=0).reshape(block, width)
                at = ((relative * batch_count + b) * high_count + h) * block
                rows_ref[pl.ds(at, block)] = joined
    writes = []

    def emit(product, start):
        product = product.astype(jnp.bfloat16)
        window = pl.ds(start, product.shape[1])
        kept_ref[:, window] = product[:half]
        given_ref[:, window] = product[half:]
        for source, target in ((given_ref, given_out), (kept_ref, kept_out)):
            copy = pltpu.make_async_copy(source.at[:, window], target.at[:, window], out_sems.at[len(writes)])
            copy.start()
            writes.append(copy)

    copies[1].wait()
    emit(jnp.dot(rows_ref[...], pair_ref[...], preferred_element_type=jnp.float32), query_cols)
    for place, (depth_at, depth) in enumerate(blocks):
        copies[2 + place].wait()
        rows = rows_ref[:, pl.ds(depth_at, depth)]
        for start, size in chunks:
            window = pl.ds(start, size)
            term = jnp.dot(
                rows, query_ref[pl.ds(depth_at, depth), window], preferred_element_type=jnp.float32
            )
            if place > 0:
                term = term + sum_ref[:, window]
            if place < len(blocks) - 1:
                sum_ref[:, window] = term
            else:
                emit(term, start)
    for copy in writes:
        copy.wait()


def cut(total, sizes):
    windows, start = [], 0
    while start < total:
        size = min(sizes[min(len(windows), len(sizes) - 1)], total - start)
        windows.append((start, size))
        start += size
    return windows


def project(tokens, w_query, w_keyval, dims):
    sequences, steps, width = tokens.shape
    query_cols, pair_cols = w_query.shape[1], w_keyval.shape[1]
    rows = sequences * steps
    blocks = cut(width, (768, 768, 512, 256))
    chunks = cut(query_cols, (768,))
    hbm = pl.BlockSpec(memory_space=pltpu.HBM)
    shape = jax.ShapeDtypeStruct((rows // 2, query_cols + pair_cols), jnp.bfloat16)
    return pl.pallas_call(
        functools.partial(project_kernel, dims, blocks, chunks),
        out_shape=(shape, shape),
        in_specs=[hbm, hbm, hbm],
        out_specs=(hbm, hbm),
        scratch_shapes=[
            pltpu.VMEM(tokens.shape, jnp.bfloat16),
            pltpu.VMEM((rows, width), jnp.bfloat16),
            pltpu.VMEM((width, query_cols), jnp.bfloat16),
            pltpu.VMEM((width, pair_cols), jnp.bfloat16),
            pltpu.VMEM((rows // 2, query_cols + pair_cols), jnp.bfloat16),
            pltpu.VMEM((rows // 2, query_cols + pair_cols), jnp.bfloat16),
            pltpu.VMEM((rows, query_cols), jnp.float32),
            pltpu.SemaphoreType.DMA((2 + len(blocks),)),
            pltpu.SemaphoreType.DMA((2 * (1 + len(chunks)),)),
        ],
        compiler_params=pltpu.CompilerParams(vmem_limit_bytes=62 * 1024 * 1024),
        cost_estimate=pl.CostEstimate(
            flops=2 * rows * width * (query_cols + pair_cols),
            bytes_accessed=2 * width * (query_cols + pair_cols),
            transcendentals=0,
        ),
        name="project",
    )(tokens, w_query, w_keyval)


def near_kernel(after_ref, source_ref, target_ref, token_ref, sem):
    copy = pltpu.make_async_copy(source_ref, target_ref, sem)
    copy.start()
    copy.wait()
    token_ref[...] = jnp.zeros_like(token_ref)


def near(after, array):
    anywhere = pl.BlockSpec(memory_space=pl.ANY)
    return pl.pallas_call(
        near_kernel,
        out_shape=(
            jax.ShapeDtypeStruct(array.shape, array.dtype),
            jax.ShapeDtypeStruct((8, 128), jnp.float32),
        ),
        in_specs=[anywhere, anywhere],
        out_specs=(anywhere, pl.BlockSpec(memory_space=pltpu.VMEM)),
        scratch_shapes=[pltpu.SemaphoreType.DMA],
        compiler_params=pltpu.CompilerParams(vmem_limit_bytes=36 * 1024 * 1024),
        cost_estimate=pl.CostEstimate(
            flops=0, bytes_accessed=2 * array.size * array.dtype.itemsize, transcendentals=0
        ),
        name="near",
    )(after, array)


def staged_kernel(source_ref, target_ref):
    target_ref[...] = source_ref[...]


def staged(array):
    vmem = pl.BlockSpec(memory_space=pltpu.VMEM)
    return pl.pallas_call(
        staged_kernel,
        out_shape=jax.ShapeDtypeStruct(array.shape, array.dtype),
        in_specs=[vmem],
        out_specs=vmem,
        compiler_params=pltpu.CompilerParams(vmem_limit_bytes=8 * 1024 * 1024),
        name="staged",
    )(array)


def combine_kernel(dims, kept_ref, taken_ref, own_ref, *sends):
    batch_count, high_count, block = dims
    for db in range(batch_count):
        for dh in range(high_count):
            at = ((lax.axis_index("batch") ^ db) * high_count + (lax.axis_index("gh") ^ dh)) * block
            window = pl.ds(pl.multiple_of(at, block), block)
            total = kept_ref[window].astype(jnp.float32) + taken_ref[window].astype(jnp.float32)
            target = sends[db * high_count + dh - 1] if db or dh else own_ref
            target[...] = total.astype(target.dtype)


def combine(kept, taken, dims):
    batch_count, high_count, block = dims
    cols = kept.shape[1]
    vmem = pl.BlockSpec(memory_space=pltpu.VMEM)
    count = batch_count * high_count
    return pl.pallas_call(
        functools.partial(combine_kernel, dims),
        out_shape=[jax.ShapeDtypeStruct((block, cols), jnp.float32)]
        + [jax.ShapeDtypeStruct((block, cols), jnp.bfloat16)] * (count - 1),
        in_specs=[vmem, vmem],
        out_specs=[vmem] * count,
        compiler_params=pltpu.CompilerParams(vmem_limit_bytes=8 * 1024 * 1024),
        name="combine",
    )(kept, taken)


def collect_kernel(count, own_ref, after_ref, *refs):
    received, outs, total_ref = refs[: -count - 1], refs[-count - 1 : -1], refs[-1]
    total = own_ref[...]
    for other in received:
        total = total + other[...].astype(jnp.float32)
    rows = outs[0].shape[0]
    for g in range(count):
        total_ref[g, pl.ds(0, rows)] = total[g * rows : (g + 1) * rows]
    for k in range(count):
        outs[k][...] = total_ref[lax.axis_index("gx") ^ k, pl.ds(0, rows)].astype(jnp.bfloat16)


def collect(own, received, after, gx_count):
    block, cols = own.shape
    rows = block // gx_count
    vmem = pl.BlockSpec(memory_space=pltpu.VMEM)
    return pl.pallas_call(
        functools.partial(collect_kernel, gx_count),
        out_shape=[jax.ShapeDtypeStruct((rows, cols), jnp.bfloat16)] * gx_count,
        in_specs=[vmem, pl.BlockSpec(memory_space=pl.ANY)]
        + [vmem] * len(received),
        out_specs=[vmem] * gx_count,
        scratch_shapes=[pltpu.VMEM((gx_count, padded(rows), cols), jnp.float32)],
        compiler_params=pltpu.CompilerParams(vmem_limit_bytes=8 * 1024 * 1024),
        name="collect",
    )(own, after, *received)


def attend_kernel(dims, mask_ref, cos_ref, sin_ref, keys_ref, values_ref, *refs):
    gx_count, owned, steps, heads, width = dims
    blocks, outs = [None] * gx_count, refs[gx_count:-2]
    for k, ref in zip(farther_first(gx_count), refs):
        blocks[k] = ref
    rows_ref, result_ref = refs[-2:]
    query_cols = heads * width
    half = width // 2
    scaling = 1.0 / width**0.5
    count = gx_count * heads * steps
    cosine = jnp.concatenate([cos_ref[s] for s in range(owned)], axis=0)
    sine = jnp.concatenate([sin_ref[s] for s in range(owned)], axis=0)

    def turn(first, second, cosine, sine):
        return first * cosine - second * sine, second * cosine + first * sine

    scaled = (cosine * scaling, sine * scaling)

    key_value = [ref[:, pl.ds(query_cols, ref.shape[1] - query_cols)].astype(jnp.float32) for ref in blocks]
    key_value = jnp.concatenate(unxored(key_value, lax.axis_index("gx")), axis=1)
    new_values = key_value[:, width:]
    new_keys = turn(key_value[:, :half], key_value[:, half:width], cosine, sine)
    new_keys = jnp.concatenate(new_keys, axis=1).astype(jnp.bfloat16).astype(jnp.float32)
    for k in range(gx_count):
        for h in range(heads):
            first = blocks[k][:, pl.ds(h * width, half)].astype(jnp.float32)
            second = blocks[k][:, pl.ds(h * width + half, half)].astype(jnp.float32)
            for part, value in enumerate(turn(first, second, *scaled)):
                for s in range(owned):
                    window = pl.ds((k * heads + h) * steps, steps)
                    rows_ref[s, window, pl.ds(part * half, half)] = value[s * steps : (s + 1) * steps]
    step_of = lax.broadcasted_iota(jnp.int32, (count, 1), 0) % steps
    for s in range(owned):
        queries = rows_ref[s, pl.ds(0, count)].astype(jnp.bfloat16)
        cached = lax.dot_general(
            queries, keys_ref[s], (((1,), (1,)), ((), ())), preferred_element_type=jnp.float32
        )
        cached = cached + mask_ref[s]
        highest = cached.max(-1, keepdims=True)
        wide = queries.astype(jnp.float32)
        fresh = []
        for u in range(steps):
            row = s * steps + u
            score = (wide * new_keys[row : row + 1]).sum(-1, keepdims=True)
            fresh.append(jnp.where(step_of >= u, score, -1e30))
            highest = jnp.maximum(highest, fresh[-1])
        exp_cached = jnp.exp(cached - highest)
        denom = exp_cached.sum(-1, keepdims=True)
        total = jnp.dot(
            exp_cached.astype(jnp.bfloat16), values_ref[s], preferred_element_type=jnp.float32
        )
        for u in range(steps):
            row = s * steps + u
            exp_fresh = jnp.exp(fresh[u] - highest)
            denom = denom + exp_fresh
            total = total + exp_fresh * new_values[row : row + 1]
        result_ref[s, pl.ds(0, count)] = total * (1.0 / denom)
    for k in range(gx_count):
        for h in range(heads):
            window = pl.ds((k * heads + h) * steps, steps)
            value = jnp.concatenate([result_ref[s, window] for s in range(owned)], axis=0)
            outs[k][:, pl.ds(h * width, width)] = value.astype(jnp.bfloat16)


def attend(blocks, cache_keys, cache_values, lengths, query_cols):
    gx_count = len(blocks)
    owned, slots, width = cache_keys.shape
    rows = blocks[0].shape[0]
    steps = rows // owned
    heads = query_cols // width
    count = gx_count * heads * steps
    freqs = 10000.0 ** (-(jnp.arange(width // 2, dtype=jnp.float32) * 2.0 / width))
    positions = lengths[:, None, None] + jnp.arange(steps, dtype=jnp.int32)[None, :, None]
    angles = positions.astype(jnp.float32) * freqs
    mask = jnp.where(jnp.arange(slots)[None, None, :] < lengths[:, None, None], 0.0, -1e30)
    vmem = pl.BlockSpec(memory_space=pltpu.VMEM)
    return pl.pallas_call(
        functools.partial(attend_kernel, (gx_count, owned, steps, heads, width)),
        out_shape=[jax.ShapeDtypeStruct((rows, query_cols), jnp.bfloat16)] * gx_count,
        in_specs=[vmem] * (5 + gx_count),
        out_specs=[vmem] * gx_count,
        scratch_shapes=[
            pltpu.VMEM((owned, padded(count) + 8, width), jnp.float32),
            pltpu.VMEM((owned, padded(count) + 8, width), jnp.float32),
        ],
        compiler_params=pltpu.CompilerParams(vmem_limit_bytes=12 * 1024 * 1024),
        cost_estimate=pl.CostEstimate(
            flops=4 * owned * count * slots * width,
            bytes_accessed=4 * owned * slots * width,
            transcendentals=owned * count * slots,
        ),
        name="attend",
    )(mask, jnp.cos(angles), jnp.sin(angles), cache_keys, cache_values, *[blocks[k] for k in farther_first(gx_count)])


def order_kernel(distances, *refs):
    out_ref, sorted_ref = refs[-2:]
    for k, block in zip(distances, refs):
        sorted_ref[lax.axis_index("gx") ^ k, pl.ds(0, block.shape[0])] = block[...].astype(jnp.float32)
    parts = [sorted_ref[g, pl.ds(0, block.shape[0])] for g in range(len(distances))]
    out_ref[...] = jnp.concatenate(parts, axis=0).astype(out_ref.dtype)


def order(blocks):
    vmem = pl.BlockSpec(memory_space=pltpu.VMEM)
    rows, cols = blocks[0].shape
    count = len(blocks)
    distances = farther_first(count)
    return pl.pallas_call(
        functools.partial(order_kernel, distances),
        out_shape=jax.ShapeDtypeStruct((count * rows, cols), blocks[0].dtype),
        in_specs=[vmem] * count,
        out_specs=vmem,
        scratch_shapes=[pltpu.VMEM((count, padded(rows), cols), jnp.float32)],
        compiler_params=pltpu.CompilerParams(vmem_limit_bytes=8 * 1024 * 1024),
        name="order",
    )(*[blocks[k] for k in distances])


def mix_kernel(dims, chunk, part, weight_ref, *refs):
    batch_count, gx_count, high_count, block = dims
    count = 2 * batch_count * high_count
    blocks, own_ref, sends, sum_ref = refs[:count][::-1], refs[count], refs[count + 1 : -1], refs[-1]
    shards = gx_count // batch_count
    group = block // shards
    lhs = jnp.concatenate([ref[...] for ref in blocks], axis=0)
    first, out_cols = part
    for start in range(0, out_cols, chunk):
        size = min(chunk, out_cols - start)
        window = pl.ds(start, size)
        sum_ref[:, pl.ds(0, size)] = jnp.dot(
            lhs, weight_ref[:, pl.ds(first + start, size)], preferred_element_type=jnp.float32
        )
        for k in range(gx_count):
            shard = lax.axis_index("gx") ^ k
            b, hi = shard // shards, shard % shards
            parts = []
            for relative in range(2):
                for h in range(high_count):
                    at = (relative * batch_count + (b ^ lax.axis_index("batch"))) * high_count + h
                    at = pl.multiple_of(at * block + hi * group, group)
                    parts.append(sum_ref[pl.ds(at, group), pl.ds(0, size)])
            piece = jnp.concatenate(parts, axis=0)
            target = own_ref if k == 0 else sends[k - 1]
            target[:, window] = piece.astype(target.dtype)


def mix(blocks, w_out, dims, part):
    batch_count, gx_count, high_count, block = dims
    depth = w_out.shape[0]
    out_cols = part[1]
    rows = len(blocks) * block
    chunk = min(768, out_cols)
    vmem = pl.BlockSpec(memory_space=pltpu.VMEM)
    kept = (0, 2) if gx_count == 4 else (0,)
    shapes = [
        jax.ShapeDtypeStruct((rows // gx_count, out_cols), jnp.float32 if k in kept else jnp.bfloat16)
        for k in range(gx_count)
    ]
    return pl.pallas_call(
        functools.partial(mix_kernel, dims, chunk, part),
        out_shape=shapes,
        in_specs=[vmem] * (1 + len(blocks)),
        out_specs=[vmem] * gx_count,
        scratch_shapes=[pltpu.VMEM((rows, chunk), jnp.float32)],
        compiler_params=pltpu.CompilerParams(vmem_limit_bytes=20 * 1024 * 1024),
        cost_estimate=pl.CostEstimate(
            flops=2 * rows * depth * out_cols, bytes_accessed=2 * depth * out_cols, transcendentals=0
        ),
        name="mix",
    )(w_out, *blocks[::-1])


def relay_kernel(own_ref, taken_ref, near_ref, sum_ref, copy_ref):
    total = own_ref[...] + taken_ref[...].astype(jnp.float32)
    sum_ref[...] = total.astype(sum_ref.dtype)
    copy_ref[...] = near_ref[...]


def relay(own, taken, near):
    vmem = pl.BlockSpec(memory_space=pltpu.VMEM)
    return pl.pallas_call(
        relay_kernel,
        out_shape=[jax.ShapeDtypeStruct(near.shape, near.dtype)] * 2,
        in_specs=[vmem] * 3,
        out_specs=[vmem] * 2,
        compiler_params=pltpu.CompilerParams(vmem_limit_bytes=8 * 1024 * 1024),
        name="relay",
    )(own, taken, near)


def summed_terms(sends):
    count = len(sends) + 1
    if count != 4:
        return [swapped_with(sends[k - 1], "gx", (count,), (k,)) for k in farther_first(count)[1:]]
    near, far, farthest = sends
    taken = swapped_with(farthest, "gx", (count,), (1,))
    both, near = relay(far, taken, near)
    return [swapped_with(both, "gx", (count,), (2,)), swapped_with(near, "gx", (count,), (1,))]


def finish_kernel(dims, begin, own_ref, *refs):
    received, (out_hbm, rows_ref, sems) = refs[:-3], refs[-3:]
    received = [ref for ref in received if ref.shape == own_ref.shape]
    batch_count, high_count, owned = dims
    steps, out_cols = rows_ref.shape[1:]
    size = batch_count * owned * steps
    copies = []
    for relative in range(2):
        low = lax.axis_index("gl") ^ relative
        for h in range(high_count):
            window = pl.ds((relative * high_count + h) * size, size)
            total = own_ref[window]
            for other in received:
                total = total + other[window].astype(jnp.float32)
            total = total.reshape(batch_count, owned, steps, out_cols).astype(jnp.bfloat16)
            high = lax.axis_index("gh") ^ h
            for g in range(batch_count):
                first = ((g * high_count + high) * 2 + low) * owned
                at = len(copies)
                rows_ref[pl.ds(at * owned, owned)] = total[g]
                copy = pltpu.make_async_copy(
                    rows_ref.at[pl.ds(at * owned, owned)],
                    out_hbm.at[pl.ds(first, owned), :, pl.ds(begin, out_cols)],
                    sems.at[at],
                )
                copy.start()
                copies.append(copy)
    for copy in copies:
        copy.wait()


def finish(own, received, dims, steps, part, parts, before):
    rows, out_cols = own.shape
    vmem = pl.BlockSpec(memory_space=pltpu.VMEM)
    anywhere = pl.BlockSpec(memory_space=pl.ANY)
    operands = [own, *received]
    in_specs = [vmem] * len(operands)
    aliases = {}
    if before is not None:
        aliases[len(operands)] = 0
        operands.append(before)
        in_specs.append(anywhere)
    batch_count, high_count, owned = dims
    return pl.pallas_call(
        functools.partial(finish_kernel, dims, part * out_cols),
        out_shape=jax.ShapeDtypeStruct((rows // steps, steps, out_cols * parts), jnp.bfloat16),
        in_specs=in_specs,
        out_specs=anywhere,
        input_output_aliases=aliases,
        scratch_shapes=[
            pltpu.VMEM((rows // steps, steps, out_cols), jnp.bfloat16),
            pltpu.SemaphoreType.DMA((2 * high_count * batch_count,)),
        ],
        compiler_params=pltpu.CompilerParams(vmem_limit_bytes=16 * 1024 * 1024),
        name="finish",
    )(*operands)


def local(tokens, w_query, w_keyval, w_out, cache_keys, cache_values, lengths):
    batch_count = lax.axis_size("batch")
    gx_count = lax.axis_size("gx")
    high_count = lax.axis_size("gh")
    sizes = (batch_count, high_count, 2)
    owned = cache_keys.shape[0]
    sequences, steps, width = tokens.shape
    query_cols = w_query.shape[1]
    rows = owned * steps
    rows_here = gx_count * rows

    kept, given = project(tokens, w_query, w_keyval, (batch_count, gx_count, high_count, owned))
    taken = swapped_with(given, PLANE, sizes, (0, 0, 1))
    far = [(db, dh) for db in range(batch_count) for dh in range(high_count)][1:]
    own, *sends = combine(staged(kept), taken, (batch_count, high_count, rows_here))
    received = [
        swapped_with(block, PLANE, sizes, (db, dh, 0)) for block, (db, dh) in zip(sends, far)
    ]
    w_out, token = near(own, w_out)
    blocks = collect(own, received, token, gx_count)
    blocks = [blocks[0]] + [
        swapped_with(blocks[k], "gx", (gx_count,), (k,)) for k in range(1, gx_count)
    ]
    blocks = attend(blocks, cache_keys, cache_values, lengths, query_cols)
    blocks = [blocks[0]] + [
        swapped_with(blocks[k], "gx", (gx_count,), (k,)) for k in range(1, gx_count)
    ]
    grouped = order(blocks)

    ours = [grouped] + [swapped_with(grouped, PLANE, sizes, (db, dh, 0)) for db, dh in far]
    theirs = [swapped_with(block, PLANE, sizes, (0, 0, 1)) for block in ours]
    out_cols = w_out.shape[1]
    parts = 2 if out_cols % 256 == 0 else 1
    size = out_cols // parts
    mixed = None
    products = [
        mix(ours + theirs, w_out, (batch_count, gx_count, high_count, rows_here), (part * size, size))
        for part in range(parts)
    ]
    for part, (own, *sends) in enumerate(products):
        received = summed_terms(sends)
        mixed = finish(own, received, (batch_count, high_count, owned), steps, part, parts, mixed)
    return mixed


def solution(mesh):
    batch_count, gx_count, gy_count = mesh.devices.shape
    split = Mesh(
        mesh.devices.reshape(batch_count, gx_count, gy_count // 2, 2), ("batch", "gx", "gh", "gl")
    )
    plane = ("batch", "gh", "gl")
    placed = (
        P(None, None, plane),
        P(plane, "gx"),
        P(plane, "gx"),
        P("gx", plane),
        P(("batch", "gx", "gh", "gl"), None, None),
        P(("batch", "gx", "gh", "gl"), None, None),
        P(("batch", "gx", "gh", "gl")),
    )
    return jax.shard_map(
        local, mesh=split, in_specs=placed, out_specs=P("gx", None, plane), check_vma=False
    )
```
